32 devices in a mesh: az: 8 (over z, x), ax: 4 (over y, core).
Axes of the slice: x: 2, y: 2, z: 4, core: 2. Of those that a mesh axis runs over, the one named last changes fastest.
Arguments:
- fields: float32 [5, 64, 128, 512], P(None, 'ax', 'az'), may hold values from -6.5 to 6.5, as said below
Outputs:
- advanced: float32 [5, 64, 128, 512], P(None, 'ax', 'az')
The draws below stay inside these ranges and needn't reach their ends.
Inputs may be any that keep to these rules, and one draw needn't show every extreme that they name: `fields`: each field is a rough part plus, on every axial plane and cycle, a constant and a first azimuthal harmonic.
All inputs are finite; a program needn't handle non-finite values.
Results may differ from the reference program's by a relative error of at most 0.0003.
Values sent between devices are 32-bit elements; how exact they have to be, the bound alone decides.
No kernel may reach another device: no remote copies, remote signals or barrier semaphores. Data moves between devices by JAX's collectives and lax.ppermute only.
A program may use at most 128 MiB of HBM per device.

```python
import jax
import jax.numpy as jnp
from jax import lax

NR = 512
NEAR = 40
NT = 128
NZ = 64
MODES = 64


def draw_fields(key, part):
    shape = (5, NZ, NT, NR)
    small_shape = (5, NZ, 1, NR)
    rough_key = jax.random.fold_in(key, 11)
    height_key = jax.random.fold_in(key, 12)
    phase_key = jax.random.fold_in(key, 13)
    level_key = jax.random.fold_in(key, 14)
    theta = jnp.arange(NT, dtype=jnp.float32) * (2.0 * jnp.pi / NT)
    rough = jnp.clip(jax.random.normal(rough_key, shape, jnp.float32), -4.0, 4.0)
    height = jax.random.uniform(height_key, small_shape, jnp.float32, 0.3, 1.2)
    level = jax.random.uniform(level_key, small_shape, jnp.float32, -0.6, 0.6)
    phase = jax.random.uniform(phase_key, small_shape, jnp.float32, -jnp.pi, jnp.pi)
    return rough + height * jnp.cos(theta[None, None, :, None] + phase) + level


def setup_inputs(seed: int = 0) -> dict:
    keys = jax.random.split(jax.random.key(seed), 2)
    fields = draw_fields(jax.random.fold_in(keys[1], 71), 0)
    return {"fields": fields}


viscosity = 0.2
time_step = 0.1
buoyancy = 1.0


def mode_tables(theta_index, total_theta, modes):
    column = jnp.arange(modes, dtype=jnp.int32)
    product = (theta_index[:, None] * column[None, :]) % total_theta
    angle = product.astype(jnp.float32) * (2.0 * jnp.pi / total_theta)
    cosine = jnp.cos(angle)
    sine = jnp.sin(angle)
    weight = jnp.where(column == 0, 1.0, 2.0).astype(jnp.float32) / total_theta
    forward = jnp.concatenate([cosine * weight[None, :], sine * (2.0 / total_theta)], axis=1)
    inverse = jnp.concatenate([cosine, sine], axis=1)
    return forward, inverse


def cycle_mask(cycles, modes):
    cycle_index = jnp.arange(cycles, dtype=jnp.int32)
    cutoff = jnp.minimum((355 * (2 * cycle_index + 1)) // 226, modes - 1)
    column = jnp.arange(modes, dtype=jnp.int32)
    keep = (column[None, :] <= cutoff[:, None]).astype(jnp.float32)
    return jnp.concatenate([keep, keep], axis=1)


def operators(center, radial_plus, radial_minus, theta_plus, theta_minus, axial_plus, axial_minus, total_theta):
    radius = jnp.arange(center.shape[-1], dtype=jnp.float32) + 0.5
    step_angle = 2.0 * jnp.pi / total_theta
    d_radial = (radial_plus - radial_minus) * 0.5
    d_theta = (theta_plus - theta_minus) / (2.0 * step_angle)
    d_axial = (axial_plus - axial_minus) * 0.5
    laplace = radial_plus - 2.0 * center + radial_minus + (radial_plus - radial_minus) / (2.0 * radius)
    laplace = laplace + (theta_plus - 2.0 * center + theta_minus) / (radius * radius * step_angle * step_angle)
    laplace = laplace + axial_plus - 2.0 * center + axial_minus
    return d_radial, d_theta, d_axial, laplace


def reference(fields):
    theta_index = jnp.arange(NT, dtype=jnp.int32)
    forward, inverse = mode_tables(theta_index, NT, MODES)
    inner_cycles = fields[:, :, :, :NEAR]
    spectra = jnp.einsum("fztj,tc->fzjc", inner_cycles, forward, precision=lax.Precision.HIGHEST)
    kept = spectra * cycle_mask(NEAR, MODES)[None, None]
    smoothed = jnp.einsum("fzjc,tc->fztj", kept, inverse, precision=lax.Precision.HIGHEST)
    state = jnp.concatenate([smoothed, fields[:, :, :, NEAR:]], axis=3)
    flip = jnp.array([-1.0, -1.0, 1.0, 1.0, 1.0], dtype=jnp.float32)
    opposite = jnp.roll(state[:, :, :, 0], NT // 2, axis=2) * flip[:, None, None]
    radius = jnp.arange(NR, dtype=jnp.float32) + 0.5
    radial_u = state[0]
    theta_u = state[1]
    axial_u = state[2]
    results = []
    theta_grads = []
    for index in range(5):
        field = state[index]
        radial_plus = jnp.concatenate([field[:, :, 1:], jnp.zeros_like(field[:, :, :1])], axis=2)
        radial_minus = jnp.concatenate([opposite[index][:, :, None], field[:, :, :-1]], axis=2)
        theta_plus = jnp.roll(field, -1, axis=1)
        theta_minus = jnp.roll(field, 1, axis=1)
        zero_plane = jnp.zeros_like(field[:1])
        axial_plus = jnp.concatenate([field[1:], zero_plane], axis=0)
        axial_minus = jnp.concatenate([zero_plane, field[:-1]], axis=0)
        d_radial, d_theta, d_axial, laplace = operators(field, radial_plus, radial_minus, theta_plus, theta_minus, axial_plus, axial_minus, NT)
        change = -(radial_u * d_radial + theta_u / radius * d_theta + axial_u * d_axial) + viscosity * laplace
        results.append(change)
        if index < 2:
            theta_grads.append(d_theta)
    inverse_square = 1.0 / (radius * radius)
    results[0] = results[0] + theta_u * theta_u / radius - viscosity * (radial_u * inverse_square + 2.0 * inverse_square * theta_grads[1])
    results[1] = results[1] - radial_u * theta_u / radius - viscosity * (theta_u * inverse_square - 2.0 * inverse_square * theta_grads[0])
    results[2] = results[2] + buoyancy * state[3]
    return state + time_step * jnp.stack(results, axis=0)
```

```python
import functools

import jax
import jax.numpy as jnp
import numpy as np
from jax import lax
from jax.experimental import pallas as pl
from jax.experimental.pallas import tpu as pltpu
from jax.sharding import PartitionSpec as P

NEAR = 40


viscosity = 0.2
time_step = 0.1
buoyancy = 1.0

LANES = 128
VMEM_LIMIT = 48 * 1024 * 1024


def swapped(block, axis, distance):
    count = lax.axis_size(axis)
    route = []
    for low in range(count):
        high = low | 1 << distance
        if high != low and high < count:
            route += [(low, high), (high, low)]
    return lax.ppermute(block, axis, route)


def with_halo(block, sides, width, periodic):
    for axis, dim in sides:
        count = lax.axis_size(axis)
        forward = [(i, i + 1) for i in range(count - 1)]
        if periodic:
            forward.append((count - 1, 0))
        backward = [(target, source) for source, target in forward]
        low = lax.ppermute(
            lax.slice_in_dim(block, block.shape[dim] - width, None, axis=dim), axis, forward
        )
        high = lax.ppermute(lax.slice_in_dim(block, 0, width, axis=dim), axis, backward)
        block = jnp.concatenate([low, block, high], axis=dim)
    return block


def mode_tables(theta_index, total_theta, modes):
    column = jnp.arange(modes, dtype=jnp.int32)
    product = theta_index[:, None] * column[None, :] % total_theta
    angle = product.astype(jnp.float32) * (2.0 * jnp.pi / total_theta)
    cosine = jnp.cos(angle)
    sine = jnp.sin(angle)
    weight = jnp.where(column == 0, 1.0, 2.0).astype(jnp.float32) / total_theta
    forward = jnp.concatenate([cosine * weight[None, :], sine * (2.0 / total_theta)], axis=1)
    inverse = jnp.concatenate([cosine, sine], axis=1)
    return (forward, inverse)


def cycle_mask(cycles, modes):
    cycle_index = jnp.arange(cycles, dtype=jnp.int32)
    cutoff = jnp.minimum(355 * (2 * cycle_index + 1) // 226, modes - 1)
    column = jnp.arange(modes, dtype=jnp.int32)
    keep = (column[None, :] <= cutoff[:, None]).astype(jnp.float32)
    return jnp.concatenate([keep, keep], axis=1)


def operators(
    center, radial_plus, radial_minus, theta_plus, theta_minus, axial_plus, axial_minus, total_theta
):
    radius = jnp.arange(center.shape[-1], dtype=jnp.float32) + 0.5
    step_angle = 2.0 * jnp.pi / total_theta
    d_radial = (radial_plus - radial_minus) * 0.5
    d_theta = (theta_plus - theta_minus) / (2.0 * step_angle)
    d_axial = (axial_plus - axial_minus) * 0.5
    laplace = (
        radial_plus - 2.0 * center + radial_minus + (radial_plus - radial_minus) / (2.0 * radius)
    )
    laplace = laplace + (theta_plus - 2.0 * center + theta_minus) / (
        radius * radius * step_angle * step_angle
    )
    laplace = laplace + axial_plus - 2.0 * center + axial_minus
    return (d_radial, d_theta, d_axial, laplace)


def general_on_device(fields):
    count_fields, planes, theta_dev, radial = fields.shape
    sectors = lax.axis_size("az")
    total_theta = theta_dev * sectors
    modes = min(128, total_theta // 2)
    sector = lax.axis_index("az")
    own_index = sector * theta_dev + jnp.arange(theta_dev, dtype=jnp.int32)
    own_forward, own_inverse = mode_tables(own_index, total_theta, modes)
    inner_cycles = fields[:, :, :, :NEAR]
    kept = None
    piece = lax.all_gather(inner_cycles, "az", axis=2, tiled=True)
    piece_index = jnp.arange(piece.shape[2], dtype=jnp.int32)
    piece_forward, unused_inverse = mode_tables(piece_index, total_theta, modes)
    spectra = jnp.einsum("fztj,tc->fzjc", piece, piece_forward, precision=lax.Precision.HIGHEST)
    kept = spectra * cycle_mask(NEAR, modes)[None, None]
    smoothed = jnp.einsum("fzjc,tc->fztj", kept, own_inverse, precision=lax.Precision.HIGHEST)
    state = jnp.concatenate([smoothed, fields[:, :, :, NEAR:]], axis=3)
    flip = jnp.array([-1.0, -1.0, 1.0, 1.0, 1.0], dtype=jnp.float32)[:, None, None]
    top_bit = sectors.bit_length() - 1
    opposite = swapped(state[:, :, :, 0], "az", top_bit - 1)
    opposite = opposite * flip
    theta_padded = with_halo(state, (("az", 2),), 1, True)
    axial_padded = with_halo(state, (("ax", 1),), 1, False)
    radial_plus = jnp.concatenate([state[:, :, :, 1:], jnp.zeros_like(state[:, :, :, :1])], axis=3)
    radial_minus = jnp.concatenate([opposite[:, :, :, None], state[:, :, :, :-1]], axis=3)
    d_radial, d_theta, d_axial, laplace = operators(
        state,
        radial_plus,
        radial_minus,
        theta_padded[:, :, 2:, :],
        theta_padded[:, :, :-2, :],
        axial_padded[:, 2:, :, :],
        axial_padded[:, :-2, :, :],
        total_theta,
    )
    radius = jnp.arange(radial, dtype=jnp.float32) + 0.5
    radial_u = state[0]
    theta_u = state[1]
    axial_u = state[2]
    change = (
        -(radial_u[None] * d_radial + (theta_u / radius)[None] * d_theta + axial_u[None] * d_axial)
        + viscosity * laplace
    )
    inverse_square = 1.0 / (radius * radius)
    first = (
        change[0]
        + theta_u * theta_u / radius
        - viscosity * (radial_u * inverse_square + 2.0 * inverse_square * d_theta[1])
    )
    second = (
        change[1]
        - radial_u * theta_u / radius
        - viscosity * (theta_u * inverse_square - 2.0 * inverse_square * d_theta[0])
    )
    third = change[2] + buoyancy * state[3]
    change = jnp.concatenate([first[None], second[None], third[None], change[3:]], axis=0)
    return state + time_step * change


class Plan:
    def __init__(self, shape, sectors):
        self.fields, self.planes, self.theta, self.radial = shape
        self.sectors = sectors
        self.total = self.theta * sectors
        self.modes = min(128, self.total // 2)
        cycle = np.arange(NEAR)
        self.cut = np.minimum(355 * (2 * cycle + 1) // 226, self.modes - 1)
        self.full = int(np.sum(self.cut < self.modes - 1))
        self.seg = LANES // self.fields
        self.extra = self.seg - self.full
        self.rows = -(-(NEAR - self.full) // max(self.extra, 1))

    @staticmethod
    def fits(shape, sectors, total):
        if sectors & (sectors - 1) or total // 2 > 128 or total != LANES or shape[2] % 16:
            return False
        plan = Plan(shape, sectors)
        return (
            plan.extra > 0
            and plan.rows <= 8
            and plan.fields == 5
            and plan.planes % 8 == 0
            and plan.radial % LANES == 0
            and plan.radial > 2 * LANES
        )

    def split(self, table):
        high = table.astype(jnp.bfloat16)
        low = (table - high.astype(np.float32)).astype(jnp.bfloat16)
        return np.concatenate([high, high, low], axis=-1)

    def forward(self):
        theta = np.arange(self.total)
        mode = np.arange(self.modes)
        angle = (np.outer(mode, theta) % self.total) * (2.0 * np.pi / self.total)
        weight = np.where(mode == 0, 1.0, 2.0)[:, None] / self.total
        table = np.concatenate([np.cos(angle) * weight, np.sin(angle) * 2.0 / self.total], axis=0)
        return self.split(table.astype(np.float32))

    def inverse(self):
        mode = np.arange(self.modes)
        blocks = []
        for sector in range(self.sectors):
            own = sector * self.theta + np.arange(self.theta)
            index = np.concatenate([own, own + self.total // 2, own[:1] - 1, own[-1:] + 1])
            angle = (np.outer(index, mode) % self.total) * (2.0 * np.pi / self.total)
            table = np.concatenate([np.cos(angle), np.sin(angle)], axis=1)
            pad = np.zeros((16 - 2, table.shape[1]))
            blocks.append(np.concatenate([table, pad], axis=0))
        return self.split(np.stack(blocks).astype(np.float32))

    def mask(self):
        mode = np.arange(self.modes)
        keep = np.zeros((self.modes, LANES), np.float32)
        for field in range(self.fields):
            keep[:, field * self.seg : field * self.seg + self.full] = (
                mode[:, None] <= self.cut[None, : self.full]
            )
        return np.concatenate([keep, keep], axis=0)

    def coefficients(self):
        radius = np.arange(self.radial) + 0.5
        step = 2.0 * np.pi / self.total
        nu_dt = viscosity * time_step
        square = 1.0 / (radius * radius * step * step)
        rows = [
            1.0 - nu_dt * (4.0 + 2.0 * square),
            nu_dt * square,
            nu_dt / (2.0 * radius),
            time_step / (2.0 * step * radius),
            time_step / radius,
            nu_dt / (radius * radius),
            nu_dt / (step * radius * radius),
        ]
        rows.append(np.zeros(self.radial))
        return np.stack(rows).astype(np.float32)


def pack_kernel(plan, x_ref, out_ref):
    shape = (plan.theta, LANES)
    lane = lax.broadcasted_iota(jnp.int32, shape, 1)
    row = lax.broadcasted_iota(jnp.int32, shape, 0)
    sign = (1 - 2 * (row & 1)).astype(jnp.float32)
    for k in range(out_ref.shape[0]):
        packed = jnp.zeros(shape, jnp.float32)
        for f in range(plan.fields):
            x = x_ref[f, k]
            alternating = jnp.sum(x * sign, axis=0, keepdims=True)
            part = jnp.where(lane < plan.full, x, 0.0)
            for r in range(plan.rows):
                piece = pltpu.roll(
                    jnp.broadcast_to(alternating, shape), (LANES - plan.extra * r) % LANES, 1
                )
                part = jnp.where(
                    (row == r) & (lane >= plan.full) & (lane < plan.seg), piece, part
                )
            part = part if f == 0 else pltpu.roll(part, plan.seg * f, 1)
            packed = packed + part
        out_ref[k] = packed


def pack(plan, fields):
    chunk = 4
    return pl.pallas_call(
        functools.partial(pack_kernel, plan),
        grid=(plan.planes // chunk,),
        in_specs=[pl.BlockSpec((plan.fields, chunk, plan.theta, LANES), lambda i: (0, i, 0, 0))],
        out_specs=pl.BlockSpec((chunk, plan.theta, LANES), lambda i: (i, 0, 0)),
        out_shape=jax.ShapeDtypeStruct((plan.planes, plan.theta, LANES), jnp.float32),
        name="pack",
        cost_estimate=pl.CostEstimate(flops=1000000, bytes_accessed=800000, transcendentals=0),
    )(fields)


def edges_kernel(plan, place_ref, x_ref, az_a, az_b, ax_a, ax_b, sems):
    odd_theta = place_ref[1]
    odd_plane = place_ref[2]
    first = odd_theta * (1 - plan.theta) + plan.theta - 1
    plane = odd_plane * (1 - plan.planes) + plan.planes - 1
    copies = [
        pltpu.make_async_copy(x_ref.at[:, :, first], az_a, sems.at[0]),
        pltpu.make_async_copy(x_ref.at[:, :, plan.theta - 1 - first], az_b, sems.at[1]),
        pltpu.make_async_copy(x_ref.at[:, plane], ax_a, sems.at[2]),
        pltpu.make_async_copy(x_ref.at[:, plan.planes - 1 - plane], ax_b, sems.at[3]),
    ]
    for copy in copies:
        copy.start()
    for copy in copies:
        copy.wait()


def edges(plan, place, fields):
    column = jax.ShapeDtypeStruct((plan.fields, plan.planes, plan.radial), jnp.float32)
    plane = jax.ShapeDtypeStruct((plan.fields, plan.theta, plan.radial), jnp.float32)
    anywhere = pl.BlockSpec(memory_space=pl.ANY)
    return pl.pallas_call(
        functools.partial(edges_kernel, plan),
        in_specs=[pl.BlockSpec(memory_space=pltpu.SMEM), anywhere],
        out_specs=[anywhere] * 4,
        out_shape=[column, column, plane, plane],
        scratch_shapes=[pltpu.SemaphoreType.DMA((4,))],
        name="edges",
        cost_estimate=pl.CostEstimate(flops=0, bytes_accessed=1300000, transcendentals=0),
    )(place, fields)


def advance(coef, q, jp, jm, tp, tm, kp, km):
    c0, c2, half, angular, over, square, cross = coef
    ur, ut, uz, temp = q[:4]
    radial = half - (0.5 * time_step) * ur
    azimuthal = angular * ut
    axial = (0.5 * time_step) * uz
    nu_dt = viscosity * time_step
    out = []
    d_theta = []
    for f in range(5):
        dt = tp[f] - tm[f]
        if f < 2:
            d_theta.append(dt)
        value = c0 * q[f] + nu_dt * ((jp[f] + jm[f]) + (kp[f] + km[f]))
        value = value + c2 * (tp[f] + tm[f])
        value = value + (jp[f] - jm[f]) * radial
        value = value - dt * azimuthal
        value = value - (kp[f] - km[f]) * axial
        out.append(value)
    swirl = over * ut
    out[0] = out[0] + swirl * ut - square * ur - cross * d_theta[1]
    out[1] = out[1] - swirl * ur - square * ut + cross * d_theta[0]
    out[2] = out[2] + (time_step * buoyancy) * temp
    return out


def turned(x, row, before, after):
    last = x.shape[0] - 1
    up = jnp.where(row == last, after, pltpu.roll(x, last, 0))
    down = jnp.where(row == 0, before, pltpu.roll(x, 1, 0))
    return up, down


def load_halos(plan, place_ref, copies, az_a, az_b, ax_a, ax_b, width, buf, side, sems):
    odd_theta = place_ref[1]
    odd_plane = place_ref[2]
    high = plan.planes + 1
    slot_a = (1 - odd_plane) * high
    lanes = pl.ds(0, width)
    copies += [
        pltpu.make_async_copy(az_a.at[:, :, lanes], side.at[1 - odd_theta], sems.at[0]),
        pltpu.make_async_copy(az_b.at[:, :, lanes], side.at[odd_theta], sems.at[1]),
        pltpu.make_async_copy(ax_a.at[:, :, lanes], buf.at[slot_a], sems.at[2]),
        pltpu.make_async_copy(ax_b.at[:, :, lanes], buf.at[high - slot_a], sems.at[3]),
    ]


def outer_kernel(
    plan, place_ref, coef_ref, x_ref, az_a, az_b, ax_a, ax_b, out_ref, buf, side, done, sems, ins, outs
):
    planes = plan.planes
    halos = []
    load_halos(plan, place_ref, halos, az_a, az_b, ax_a, ax_b, plan.radial, buf, side, sems)
    for copy in halos:
        copy.start()

    def fetch(k):
        return pltpu.make_async_copy(x_ref.at[:, k], buf.at[k + 1], ins.at[k])

    def store(k):
        return pltpu.make_async_copy(
            done.at[k], out_ref.at[:, k, :, pl.ds(LANES, plan.radial - LANES)], outs.at[k]
        )

    for k in range(planes):
        fetch(k).start()
    for copy in halos:
        copy.wait()
    fetch(0).wait()
    shape = (plan.theta, LANES)
    lane = lax.broadcasted_iota(jnp.int32, shape, 1)
    row = lax.broadcasted_iota(jnp.int32, shape, 0)
    tiles = plan.radial // LANES

    def step(group, carry):
        start = pl.multiple_of(group * 8, 8)
        for i in range(8):
            k = start + i
            if i < 7:
                fetch(k + 1).wait()
            else:
                pl.when(k < planes - 1)(lambda: fetch(k + 1).wait())
            for tile in range(1, tiles):
                here = pl.ds(tile * LANES, LANES)
                coef = [coef_ref[j : j + 1, here] for j in range(7)]
                q, jp, jm, tp, tm, kp, km = ([] for _ in range(7))
                for f in range(plan.fields):
                    x = buf[k + 1, f, :, here]
                    low = buf[k + 1, f, :, pl.ds((tile - 1) * LANES, LANES)]
                    q.append(x)
                    high = 0.0
                    if tile + 1 < tiles:
                        high = buf[k + 1, f, :, pl.ds((tile + 1) * LANES, LANES)]
                        high = pltpu.roll(high, LANES - 1, 1)
                    jp.append(jnp.where(lane == LANES - 1, high, pltpu.roll(x, LANES - 1, 1)))
                    jm.append(jnp.where(lane == 0, pltpu.roll(low, 1, 1), pltpu.roll(x, 1, 1)))
                    before = side[0, f, pl.ds(start, 8), here][i : i + 1]
                    after = side[1, f, pl.ds(start, 8), here][i : i + 1]
                    up, down = turned(x, row, before, after)
                    tp.append(up)
                    tm.append(down)
                    kp.append(buf[k + 2, f, :, here])
                    km.append(buf[k, f, :, here])
                result = advance(coef, q, jp, jm, tp, tm, kp, km)
                for f in range(plan.fields):
                    done[k, f, :, pl.ds((tile - 1) * LANES, LANES)] = result[f]
            store(k).start()
        return carry

    lax.fori_loop(0, planes // 8, step, 0)
    for k in range(planes):
        store(k).wait()


def outer(plan, place, coef, fields, halos):
    anywhere = pl.BlockSpec(memory_space=pl.ANY)
    f32 = jnp.float32
    return pl.pallas_call(
        functools.partial(outer_kernel, plan),
        in_specs=[pl.BlockSpec(memory_space=pltpu.SMEM), pl.BlockSpec(memory_space=pltpu.VMEM)]
        + [anywhere] * 5,
        out_specs=anywhere,
        out_shape=jax.ShapeDtypeStruct(fields.shape, f32),
        scratch_shapes=[
            pltpu.VMEM((plan.planes + 2, plan.fields, plan.theta, plan.radial), f32),
            pltpu.VMEM((2, plan.fields, plan.planes, plan.radial), f32),
            pltpu.VMEM((plan.planes, plan.fields, plan.theta, plan.radial - LANES), f32),
            pltpu.SemaphoreType.DMA((4,)),
            pltpu.SemaphoreType.DMA((plan.planes,)),
            pltpu.SemaphoreType.DMA((plan.planes,)),
        ],
        compiler_params=pltpu.CompilerParams(vmem_limit_bytes=VMEM_LIMIT),
        name="outer",
        cost_estimate=pl.CostEstimate(flops=16000000, bytes_accessed=5000000, transcendentals=0),
    )(place, coef, fields, *halos)


def halves(x):
    high = x.astype(jnp.bfloat16)
    low = (x - high.astype(jnp.float32)).astype(jnp.bfloat16)
    return jnp.concatenate([high, low, high], axis=0)


def filter_kernel(
    plan, place_ref, forward_ref, inverse_ref, mask_ref, *refs
):
    pieces = refs[: plan.sectors]
    own_ref, across_ref, edge_ref, nyquist_ref, message_a, message_b = refs[plan.sectors : plan.sectors + 6]
    data, table, totals, sems = refs[plan.sectors + 6 :]
    sector = place_ref[0]
    odd_plane = place_ref[2]
    theta = plan.theta
    copies = [pltpu.make_async_copy(inverse_ref.at[sector], table, sems.at[plan.sectors])]
    for p in range(plan.sectors):
        copies.append(
            pltpu.make_async_copy(pieces[p], data.at[:, sector ^ p], sems.at[p])
        )
    for copy in copies:
        copy.start()
    for copy in copies:
        copy.wait()
    mask = mask_ref[...]
    mask = jnp.concatenate([mask, mask], axis=1)

    for k in range(0, plan.planes, 2):
        both = jnp.concatenate(
            [data[k].reshape(plan.total, LANES), data[k + 1].reshape(plan.total, LANES)], axis=1
        )
        spectra = jnp.dot(forward_ref[...], halves(both), preferred_element_type=jnp.float32)
        kept = halves(spectra * mask)
        state = jnp.dot(table[...], kept, preferred_element_type=jnp.float32)
        for i in range(2):
            lanes = slice(i * LANES, (i + 1) * LANES)
            own_ref[k + i] = state[:theta, lanes]
            across_ref[k + i] = state[theta : 2 * theta, lanes]
            edge_ref[k + i] = state[2 * theta : 2 * theta + 8, lanes]
            top = data[k + i, 0, :8]
            for p in range(1, plan.sectors):
                top = top + data[k + i, p, :8]
            for r in range(plan.rows):
                totals[r, k + i : k + i + 1, :] = top[r : r + 1]

    lane = lax.broadcasted_iota(jnp.int32, (plan.planes, LANES), 1)
    for f in range(plan.fields):
        total = jnp.zeros((plan.planes, LANES), jnp.float32)
        for r in range(plan.rows):
            first = plan.full + plan.extra * r
            shift = (plan.extra * r - plan.seg * f) % LANES
            value = totals[r] if shift == 0 else pltpu.roll(totals[r], shift, 1)
            last = min(first + plan.extra, NEAR)
            total = jnp.where((lane >= first) & (lane < last), value, total)
        nyquist_ref[f] = total * (1.0 / plan.total)

    def message(ref, plane):
        ref[pl.ds(0, theta)] = own_ref[plane]
        for f in range(plan.fields):
            ref[pl.ds(theta + f, 1)] = nyquist_ref[f, pl.ds(plane, 1)]
        ref[pl.ds(theta + 5, 3)] = jnp.zeros((3, LANES), jnp.float32)

    plane = odd_plane * (1 - plan.planes) + plan.planes - 1
    message(message_a, plane)
    message(message_b, plan.planes - 1 - plane)


def filtered(plan, place, pieces):
    anywhere = pl.BlockSpec(memory_space=pl.ANY)
    inside = pl.BlockSpec(memory_space=pltpu.VMEM)
    f32 = jnp.float32
    cube = jax.ShapeDtypeStruct((plan.planes, plan.theta, LANES), f32)
    return pl.pallas_call(
        functools.partial(filter_kernel, plan),
        in_specs=[pl.BlockSpec(memory_space=pltpu.SMEM), inside, anywhere, inside]
        + [anywhere] * plan.sectors,
        out_specs=[inside] * 6,
        out_shape=[
            cube,
            cube,
            jax.ShapeDtypeStruct((plan.planes, 8, LANES), f32),
            jax.ShapeDtypeStruct((plan.fields, plan.planes, LANES), f32),
            jax.ShapeDtypeStruct((plan.theta + 8, LANES), f32),
            jax.ShapeDtypeStruct((plan.theta + 8, LANES), f32),
        ],
        scratch_shapes=[
            pltpu.VMEM((plan.planes, plan.sectors, plan.theta, LANES), f32),
            pltpu.VMEM((2 * plan.theta + 16, 6 * plan.modes), jnp.bfloat16),
            pltpu.VMEM((plan.rows, plan.planes, LANES), f32),
            pltpu.SemaphoreType.DMA((plan.sectors + 1,)),
        ],
        compiler_params=pltpu.CompilerParams(vmem_limit_bytes=VMEM_LIMIT),
        name="filter",
        cost_estimate=pl.CostEstimate(flops=200000000, bytes_accessed=1500000, transcendentals=0),
    )(
        place,
        jnp.asarray(plan.forward()),
        jnp.asarray(plan.inverse()),
        jnp.asarray(plan.mask()),
        *pieces,
    )


def inner_kernel(
    plan, place_ref, coef_ref, own_ref, across_ref, edge_ref, nyquist_ref, message_a, message_b,
    x_ref, az_a, az_b, ax_a, ax_b, other_ref, out_ref, buf, side, state, done, sems, ins, outs
):
    planes = plan.planes
    theta = plan.theta
    halos = []
    load_halos(plan, place_ref, halos, az_a, az_b, ax_a, ax_b, 2 * LANES, buf, side, sems)
    fetch = [
        pltpu.make_async_copy(x_ref.at[:, k, :, pl.ds(0, 2 * LANES)], buf.at[k + 1], ins.at[k])
        for k in range(planes)
    ]
    store = [
        pltpu.make_async_copy(done.at[k], out_ref.at[:, k, :, pl.ds(0, LANES)], outs.at[k])
        for k in range(planes)
    ]
    for copy in halos + fetch:
        copy.start()
    shape = (theta, LANES)
    lane = lax.broadcasted_iota(jnp.int32, shape, 1)
    row = lax.broadcasted_iota(jnp.int32, shape, 0)
    sign = (1 - 2 * (row & 1)).astype(jnp.float32)
    lane1 = lax.broadcasted_iota(jnp.int32, (1, LANES), 1)
    first = pl.ds(0, LANES)
    coef = [coef_ref[i : i + 1, :LANES] for i in range(7)]
    flips = (-1.0, -1.0, 1.0, 1.0, 1.0)

    def aligned(x, f):
        return x if f == 0 else pltpu.roll(x, LANES - plan.seg * f, 1)

    def smooth(raw, packed, total, f):
        return jnp.where(lane < plan.full, aligned(packed, f), raw - sign * total)

    for copy in halos + fetch:
        copy.wait()
    for k in range(planes):
        for f in range(plan.fields):
            state[k + 1, f] = smooth(
                buf[k + 1, f, :, first], own_ref[k], nyquist_ref[f, k : k + 1], f
            )
    odd_plane = place_ref[2]
    high = planes + 1
    slot_a = (1 - odd_plane) * high
    for message, slot in ((message_a, slot_a), (message_b, high - slot_a)):
        for f in range(plan.fields):
            state[slot, f] = smooth(
                buf[slot, f, :, first], message[:theta], message[theta + f : theta + f + 1], f
            )

    for k in range(planes):
        q, jp, jm, tp, tm, kp, km = ([] for _ in range(7))
        for f in range(plan.fields):
            x = state[k + 1, f]
            q.append(x)
            high_part = pltpu.roll(buf[k + 1, f, :, pl.ds(LANES, LANES)], LANES - 1, 1)
            jp.append(jnp.where(lane == LANES - 1, high_part, pltpu.roll(x, LANES - 1, 1)))
            opposite = flips[f] * aligned(across_ref[k], f)
            jm.append(jnp.where(lane == 0, opposite, pltpu.roll(x, 1, 1)))
            total = nyquist_ref[f, k : k + 1]
            before = jnp.where(
                lane1 < plan.full, aligned(edge_ref[k, 0:1], f), side[0, f, k : k + 1, first] + total
            )
            after = jnp.where(
                lane1 < plan.full, aligned(edge_ref[k, 1:2], f), side[1, f, k : k + 1, first] - total
            )
            up, down = turned(x, row, before, after)
            tp.append(up)
            tm.append(down)
            kp.append(state[k + 2, f])
            km.append(state[k, f])
        result = advance(coef, q, jp, jm, tp, tm, kp, km)
        for f in range(plan.fields):
            done[k, f] = result[f]
        store[k].start()
    for copy in store:
        copy.wait()


def inner(plan, place, coef, parts, messages, fields, halos, partial):
    anywhere = pl.BlockSpec(memory_space=pl.ANY)
    inside = pl.BlockSpec(memory_space=pltpu.VMEM)
    f32 = jnp.float32
    operands = (place, coef, *parts, *messages, fields, *halos, partial)
    return pl.pallas_call(
        functools.partial(inner_kernel, plan),
        in_specs=[pl.BlockSpec(memory_space=pltpu.SMEM)] + [inside] * 7 + [anywhere] * 6,
        out_specs=anywhere,
        out_shape=jax.ShapeDtypeStruct(fields.shape, f32),
        input_output_aliases={len(operands) - 1: 0},
        scratch_shapes=[
            pltpu.VMEM((plan.planes + 2, plan.fields, plan.theta, 2 * LANES), f32),
            pltpu.VMEM((2, plan.fields, plan.planes, 2 * LANES), f32),
            pltpu.VMEM((plan.planes + 2, plan.fields, plan.theta, LANES), f32),
            pltpu.VMEM((plan.planes, plan.fields, plan.theta, LANES), f32),
            pltpu.SemaphoreType.DMA((4,)),
            pltpu.SemaphoreType.DMA((plan.planes,)),
            pltpu.SemaphoreType.DMA((plan.planes,)),
        ],
        compiler_params=pltpu.CompilerParams(vmem_limit_bytes=VMEM_LIMIT),
        name="inner",
        cost_estimate=pl.CostEstimate(flops=6000000, bytes_accessed=2500000, transcendentals=0),
    )(*operands)


def pairs(count, start, periodic):
    route = []
    for low in range(start, count, 2):
        high = low + 1
        if high == count and not periodic:
            continue
        route += [(low, high % count), (high % count, low)]
    return route


def fast_on_device(fields):
    sectors = lax.axis_size("az")
    slabs = lax.axis_size("ax")
    plan = Plan(fields.shape, sectors)
    sector = lax.axis_index("az")
    place = jnp.stack([sector, sector % 2, lax.axis_index("ax") % 2]).astype(jnp.int32)
    coef = jnp.asarray(plan.coefficients())

    packed = pack(plan, fields)
    pieces = [packed]
    for p in range(1, sectors):
        pieces.append(lax.ppermute(packed, "az", [(i, i ^ p) for i in range(sectors)]))

    az_a, az_b, ax_a, ax_b = edges(plan, place, fields)
    halos = (
        lax.ppermute(az_a, "az", pairs(sectors, 0, True)),
        lax.ppermute(az_b, "az", pairs(sectors, 1, True)),
        lax.ppermute(ax_a, "ax", pairs(slabs, 0, False)),
        lax.ppermute(ax_b, "ax", pairs(slabs, 1, False)),
    )
    partial = outer(plan, place, coef, fields, halos)
    *parts, message_a, message_b = filtered(plan, place, pieces)
    messages = (
        lax.ppermute(message_a, "ax", pairs(slabs, 0, False)),
        lax.ppermute(message_b, "ax", pairs(slabs, 1, False)),
    )
    return inner(plan, place, coef, parts, messages, fields, halos, partial)


def on_device(fields):
    total_theta = fields.shape[2] * lax.axis_size("az")
    if Plan.fits(fields.shape, lax.axis_size("az"), total_theta):
        return fast_on_device(fields)
    return general_on_device(fields)


def solution(mesh):
    placed = (P(None, "ax", "az", None),)
    return jax.shard_map(
        on_device, mesh=mesh, in_specs=placed, out_specs=P(None, "ax", "az", None), check_vma=False
    )
```

```python
import functools

import jax
import jax.numpy as jnp
import numpy as np
from jax import lax
from jax.experimental import pallas as pl
from jax.experimental.pallas import tpu as pltpu
from jax.sharding import PartitionSpec as P

NEAR = 40


viscosity = 0.2
time_step = 0.1
buoyancy = 1.0

LANES = 128
VMEM_LIMIT = 48 * 1024 * 1024


def swapped(block, axis, distance):
    count = lax.axis_size(axis)
    route = []
    for low in range(count):
        high = low | 1 << distance
        if high != low and high < count:
            route += [(low, high), (high, low)]
    return lax.ppermute(block, axis, route)


def with_halo(block, sides, width, periodic):
    for axis, dim in sides:
        count = lax.axis_size(axis)
        forward = [(i, i + 1) for i in range(count - 1)]
        if periodic:
            forward.append((count - 1, 0))
        backward = [(target, source) for source, target in forward]
        low = lax.ppermute(
            lax.slice_in_dim(block, block.shape[dim] - width, None, axis=dim), axis, forward
        )
        high = lax.ppermute(lax.slice_in_dim(block, 0, width, axis=dim), axis, backward)
        block = jnp.concatenate([low, block, high], axis=dim)
    return block


def mode_tables(theta_index, total_theta, modes):
    column = jnp.arange(modes, dtype=jnp.int32)
    product = theta_index[:, None] * column[None, :] % total_theta
    angle = product.astype(jnp.float32) * (2.0 * jnp.pi / total_theta)
    cosine = jnp.cos(angle)
    sine = jnp.sin(angle)
    weight = jnp.where(column == 0, 1.0, 2.0).astype(jnp.float32) / total_theta
    forward = jnp.concatenate([cosine * weight[None, :], sine * (2.0 / total_theta)], axis=1)
    inverse = jnp.concatenate([cosine, sine], axis=1)
    return (forward, inverse)


def cycle_mask(cycles, modes):
    cycle_index = jnp.arange(cycles, dtype=jnp.int32)
    cutoff = jnp.minimum(355 * (2 * cycle_index + 1) // 226, modes - 1)
    column = jnp.arange(modes, dtype=jnp.int32)
    keep = (column[None, :] <= cutoff[:, None]).astype(jnp.float32)
    return jnp.concatenate([keep, keep], axis=1)


def operators(
    center, radial_plus, radial_minus, theta_plus, theta_minus, axial_plus, axial_minus, total_theta
):
    radius = jnp.arange(center.shape[-1], dtype=jnp.float32) + 0.5
    step_angle = 2.0 * jnp.pi / total_theta
    d_radial = (radial_plus - radial_minus) * 0.5
    d_theta = (theta_plus - theta_minus) / (2.0 * step_angle)
    d_axial = (axial_plus - axial_minus) * 0.5
    laplace = (
        radial_plus - 2.0 * center + radial_minus + (radial_plus - radial_minus) / (2.0 * radius)
    )
    laplace = laplace + (theta_plus - 2.0 * center + theta_minus) / (
        radius * radius * step_angle * step_angle
    )
    laplace = laplace + axial_plus - 2.0 * center + axial_minus
    return (d_radial, d_theta, d_axial, laplace)


def general_on_device(fields):
    count_fields, planes, theta_dev, radial = fields.shape
    sectors = lax.axis_size("az")
    total_theta = theta_dev * sectors
    modes = min(128, total_theta // 2)
    sector = lax.axis_index("az")
    own_index = sector * theta_dev + jnp.arange(theta_dev, dtype=jnp.int32)
    own_forward, own_inverse = mode_tables(own_index, total_theta, modes)
    inner_cycles = fields[:, :, :, :NEAR]
    kept = None
    piece = lax.all_gather(inner_cycles, "az", axis=2, tiled=True)
    piece_index = jnp.arange(piece.shape[2], dtype=jnp.int32)
    piece_forward, unused_inverse = mode_tables(piece_index, total_theta, modes)
    spectra = jnp.einsum("fztj,tc->fzjc", piece, piece_forward, precision=lax.Precision.HIGHEST)
    kept = spectra * cycle_mask(NEAR, modes)[None, None]
    smoothed = jnp.einsum("fzjc,tc->fztj", kept, own_inverse, precision=lax.Precision.HIGHEST)
    state = jnp.concatenate([smoothed, fields[:, :, :, NEAR:]], axis=3)
    flip = jnp.array([-1.0, -1.0, 1.0, 1.0, 1.0], dtype=jnp.float32)[:, None, None]
    top_bit = sectors.bit_length() - 1
    opposite = swapped(state[:, :, :, 0], "az", top_bit - 1)
    opposite = opposite * flip
    theta_padded = with_halo(state, (("az", 2),), 1, True)
    axial_padded = with_halo(state, (("ax", 1),), 1, False)
    radial_plus = jnp.concatenate([state[:, :, :, 1:], jnp.zeros_like(state[:, :, :, :1])], axis=3)
    radial_minus = jnp.concatenate([opposite[:, :, :, None], state[:, :, :, :-1]], axis=3)
    d_radial, d_theta, d_axial, laplace = operators(
        state,
        radial_plus,
        radial_minus,
        theta_padded[:, :, 2:, :],
        theta_padded[:, :, :-2, :],
        axial_padded[:, 2:, :, :],
        axial_padded[:, :-2, :, :],
        total_theta,
    )
    radius = jnp.arange(radial, dtype=jnp.float32) + 0.5
    radial_u = state[0]
    theta_u = state[1]
    axial_u = state[2]
    change = (
        -(radial_u[None] * d_radial + (theta_u / radius)[None] * d_theta + axial_u[None] * d_axial)
        + viscosity * laplace
    )
    inverse_square = 1.0 / (radius * radius)
    first = (
        change[0]
        + theta_u * theta_u / radius
        - viscosity * (radial_u * inverse_square + 2.0 * inverse_square * d_theta[1])
    )
    second = (
        change[1]
        - radial_u * theta_u / radius
        - viscosity * (theta_u * inverse_square - 2.0 * inverse_square * d_theta[0])
    )
    third = change[2] + buoyancy * state[3]
    change = jnp.concatenate([first[None], second[None], third[None], change[3:]], axis=0)
    return state + time_step * change


class Plan:
    def __init__(self, shape, sectors):
        self.fields, self.planes, self.theta, self.radial = shape
        self.sectors = sectors
        self.total = self.theta * sectors
        self.modes = min(128, self.total // 2)
        cycle = np.arange(NEAR)
        self.cut = np.minimum(355 * (2 * cycle + 1) // 226, self.modes - 1)
        self.full = int(np.sum(self.cut < self.modes - 1))
        self.rest = NEAR - self.full
        self.beside = LANES // max(self.full, 1)
        self.groups = -(-self.fields * self.planes // self.beside)

    def place(self, f, k):
        index = k * self.fields + f
        return index // self.beside, index % self.beside * self.full

    @staticmethod
    def fits(shape, sectors, total):
        if sectors & (sectors - 1) or total // 2 > 128 or total != LANES or shape[2] != 16:
            return False
        plan = Plan(shape, sectors)
        return (
            plan.full > 0
            and plan.fields == 5
            and plan.planes == plan.theta
            and plan.rest * plan.fields <= LANES
            and plan.groups % 2 == 0
            and plan.radial % LANES == 0
            and plan.radial > 2 * LANES
        )

    def split(self, table):
        high = table.astype(jnp.bfloat16)
        low = (table - high.astype(np.float32)).astype(jnp.bfloat16)
        return np.concatenate([high, high, low], axis=-1)

    def forward(self):
        theta = np.arange(self.total)
        mode = np.arange(self.modes)
        angle = (np.outer(mode, theta) % self.total) * (2.0 * np.pi / self.total)
        weight = np.where(mode == 0, 1.0, 2.0)[:, None] / self.total
        table = np.concatenate([np.cos(angle) * weight, np.sin(angle) * 2.0 / self.total], axis=0)
        return self.split(table.astype(np.float32))

    def inverse(self):
        mode = np.arange(self.modes)
        blocks = []
        for sector in range(self.sectors):
            own = sector * self.theta + np.arange(self.theta)
            index = np.concatenate([own, own + self.total // 2, own[:1] - 1, own[-1:] + 1])
            angle = (np.outer(index, mode) % self.total) * (2.0 * np.pi / self.total)
            table = np.concatenate([np.cos(angle), np.sin(angle)], axis=1)
            pad = np.zeros((16 - 2, table.shape[1]))
            blocks.append(np.concatenate([table, pad], axis=0))
        return self.split(np.stack(blocks).astype(np.float32))

    def mask(self):
        mode = np.arange(self.modes)
        keep = np.zeros((self.modes, LANES), np.float32)
        for i in range(self.beside):
            keep[:, i * self.full : (i + 1) * self.full] = (
                mode[:, None] <= self.cut[None, : self.full]
            )
        return np.concatenate([keep, keep], axis=0)

    def coefficients(self):
        radius = np.arange(self.radial) + 0.5
        step = 2.0 * np.pi / self.total
        nu_dt = viscosity * time_step
        square = 1.0 / (radius * radius * step * step)
        rows = [
            1.0 - nu_dt * (4.0 + 2.0 * square),
            nu_dt * square,
            nu_dt / (2.0 * radius),
            time_step / (2.0 * step * radius),
            time_step / radius,
            nu_dt / (radius * radius),
            nu_dt / (step * radius * radius),
        ]
        rows.append(np.zeros(self.radial))
        return np.stack(rows).astype(np.float32)


def moved(x, lanes):
    return x if lanes % LANES == 0 else pltpu.roll(x, lanes % LANES, 1)


def pack_kernel(plan, x_ref, out_ref):
    shape = (plan.theta, LANES)
    lane = lax.broadcasted_iota(jnp.int32, shape, 1)
    row = lax.broadcasted_iota(jnp.int32, shape, 0)
    sign = (1 - 2 * (row & 1)).astype(jnp.float32)
    group = jnp.zeros(shape, jnp.float32)
    sums = [jnp.zeros(shape, jnp.float32) for _ in range(plan.fields)]
    for k in range(plan.planes):
        for f in range(plan.fields):
            x = x_ref[f, k]
            number, first = plan.place(f, k)
            part = moved(x, first)
            if first:
                part = jnp.where((lane >= first) & (lane < first + plan.full), part, group)
            group = part
            if first // plan.full == plan.beside - 1 or (f, k) == (plan.fields - 1, plan.planes - 1):
                out_ref[number] = group
            alternating = jnp.sum(x * sign, axis=0, keepdims=True)
            sums[f] = jnp.where(row == k, alternating, sums[f])
    last = sums[0]
    for f in range(plan.fields):
        start = f * plan.rest
        last = jnp.where(lane >= start, moved(sums[f], start - plan.full), last)
    out_ref[plan.groups] = last


def pack(plan, fields):
    return pl.pallas_call(
        functools.partial(pack_kernel, plan),
        grid=(1,),
        in_specs=[
            pl.BlockSpec((plan.fields, plan.planes, plan.theta, LANES), lambda i: (0, 0, 0, 0))
        ],
        out_specs=pl.BlockSpec((plan.groups + 1, plan.theta, LANES), lambda i: (0, 0, 0)),
        out_shape=jax.ShapeDtypeStruct((plan.groups + 1, plan.theta, LANES), jnp.float32),
        name="pack",
        cost_estimate=pl.CostEstimate(flops=1000000, bytes_accessed=800000, transcendentals=0),
    )(fields)


def edges_kernel(plan, x_ref, az_a, az_b, ax_a, ax_b):
    step = pl.program_id(0)
    even_theta = lax.axis_index("az") % 2 == 0
    even_plane = lax.axis_index("ax") % 2 == 0
    rows = x_ref.shape[1]
    for f in range(plan.fields):
        for k in range(rows):
            low = x_ref[f, k, 0:1, :]
            high = x_ref[f, k, plan.theta - 1 : plan.theta, :]
            az_a[f, k : k + 1, :] = jnp.where(even_theta, high, low)
            az_b[f, k : k + 1, :] = jnp.where(even_theta, low, high)
    first = step == 0
    last = step == pl.num_programs(0) - 1

    @pl.when(first & even_plane)
    def _():
        ax_b[...] = x_ref[:, 0]

    @pl.when(first & jnp.logical_not(even_plane))
    def _():
        ax_a[...] = x_ref[:, 0]

    @pl.when(last & even_plane)
    def _():
        ax_a[...] = x_ref[:, rows - 1]

    @pl.when(last & jnp.logical_not(even_plane))
    def _():
        ax_b[...] = x_ref[:, rows - 1]


def edges(plan, fields):
    column = jax.ShapeDtypeStruct((plan.fields, plan.planes, plan.radial), jnp.float32)
    plane = jax.ShapeDtypeStruct((plan.fields, plan.theta, plan.radial), jnp.float32)
    part = pl.BlockSpec((plan.fields, 8, plan.radial), lambda i: (0, i, 0))
    whole = pl.BlockSpec((plan.fields, plan.theta, plan.radial), lambda i: (0, 0, 0))
    return pl.pallas_call(
        functools.partial(edges_kernel, plan),
        grid=(plan.planes // 8,),
        in_specs=[
            pl.BlockSpec((plan.fields, 8, plan.theta, plan.radial), lambda i: (0, i, 0, 0))
        ],
        out_specs=[part, part, whole, whole],
        out_shape=[column, column, plane, plane],
        compiler_params=pltpu.CompilerParams(vmem_limit_bytes=VMEM_LIMIT),
        name="edges",
        cost_estimate=pl.CostEstimate(flops=0, bytes_accessed=4000000, transcendentals=0),
    )(fields)


def advance(coef, q, jp, jm, tp, tm, kp, km):
    c0, c2, half, angular, over, square, cross = coef
    ur, ut, uz, temp = q[:4]
    radial = half - (0.5 * time_step) * ur
    azimuthal = angular * ut
    axial = (0.5 * time_step) * uz
    nu_dt = viscosity * time_step
    out = []
    d_theta = []
    for f in range(5):
        dt = tp[f] - tm[f]
        if f < 2:
            d_theta.append(dt)
        value = c0 * q[f] + nu_dt * ((jp[f] + jm[f]) + (kp[f] + km[f]))
        value = value + c2 * (tp[f] + tm[f])
        value = value + (jp[f] - jm[f]) * radial
        value = value - dt * azimuthal
        value = value - (kp[f] - km[f]) * axial
        out.append(value)
    swirl = over * ut
    out[0] = out[0] + swirl * ut - square * ur - cross * d_theta[1]
    out[1] = out[1] - swirl * ur - square * ut + cross * d_theta[0]
    out[2] = out[2] + (time_step * buoyancy) * temp
    return out


def turned(x, row, before, after):
    last = x.shape[0] - 1
    up = jnp.where(row == last, after, pltpu.roll(x, last, 0))
    down = jnp.where(row == 0, before, pltpu.roll(x, 1, 0))
    return up, down


def load_halos(plan, copies, az_a, az_b, ax_a, ax_b, width, buf, side, sems):
    odd_theta = lax.axis_index("az") % 2
    odd_plane = lax.axis_index("ax") % 2
    high = plan.planes + 1
    slot_a = (1 - odd_plane) * high
    lanes = pl.ds(0, width)
    copies += [
        pltpu.make_async_copy(az_a.at[:, :, lanes], side.at[1 - odd_theta], sems.at[0]),
        pltpu.make_async_copy(az_b.at[:, :, lanes], side.at[odd_theta], sems.at[1]),
        pltpu.make_async_copy(ax_a.at[:, :, lanes], buf.at[slot_a], sems.at[2]),
        pltpu.make_async_copy(ax_b.at[:, :, lanes], buf.at[high - slot_a], sems.at[3]),
    ]


def outer_kernel(
    plan, coef_ref, x_ref, az_a, az_b, ax_a, ax_b, out_ref, buf, side, done, sems, ins, outs
):
    planes = plan.planes
    halos = []
    load_halos(plan, halos, az_a, az_b, ax_a, ax_b, plan.radial, buf, side, sems)
    for copy in halos:
        copy.start()

    def fetch(k):
        return pltpu.make_async_copy(x_ref.at[:, k], buf.at[k + 1], ins.at[k])

    def store(k):
        return pltpu.make_async_copy(
            done.at[k], out_ref.at[:, k, :, pl.ds(LANES, plan.radial - LANES)], outs.at[k]
        )

    for k in range(planes):
        fetch(k).start()
    for copy in halos:
        copy.wait()
    fetch(0).wait()
    shape = (plan.theta, LANES)
    lane = lax.broadcasted_iota(jnp.int32, shape, 1)
    row = lax.broadcasted_iota(jnp.int32, shape, 0)
    tiles = plan.radial // LANES

    def step(group, carry):
        start = pl.multiple_of(group * 8, 8)
        for i in range(8):
            k = start + i
            if i < 7:
                fetch(k + 1).wait()
            else:
                pl.when(k < planes - 1)(lambda: fetch(k + 1).wait())
            for tile in range(1, tiles):
                here = pl.ds(tile * LANES, LANES)
                coef = [coef_ref[j : j + 1, here] for j in range(7)]
                q, jp, jm, tp, tm, kp, km = ([] for _ in range(7))
                for f in range(plan.fields):
                    x = buf[k + 1, f, :, here]
                    low = buf[k + 1, f, :, pl.ds((tile - 1) * LANES, LANES)]
                    q.append(x)
                    high = 0.0
                    if tile + 1 < tiles:
                        high = buf[k + 1, f, :, pl.ds((tile + 1) * LANES, LANES)]
                        high = pltpu.roll(high, LANES - 1, 1)
                    jp.append(jnp.where(lane == LANES - 1, high, pltpu.roll(x, LANES - 1, 1)))
                    jm.append(jnp.where(lane == 0, pltpu.roll(low, 1, 1), pltpu.roll(x, 1, 1)))
                    before = side[0, f, pl.ds(start, 8), here][i : i + 1]
                    after = side[1, f, pl.ds(start, 8), here][i : i + 1]
                    up, down = turned(x, row, before, after)
                    tp.append(up)
                    tm.append(down)
                    kp.append(buf[k + 2, f, :, here])
                    km.append(buf[k, f, :, here])
                result = advance(coef, q, jp, jm, tp, tm, kp, km)
                for f in range(plan.fields):
                    done[k, f, :, pl.ds((tile - 1) * LANES, LANES)] = result[f]
            store(k).start()
        return carry

    lax.fori_loop(0, planes // 8, step, 0)
    for k in range(planes):
        store(k).wait()


def outer(plan, coef, fields, halos):
    anywhere = pl.BlockSpec(memory_space=pl.ANY)
    f32 = jnp.float32
    return pl.pallas_call(
        functools.partial(outer_kernel, plan),
        in_specs=[pl.BlockSpec(memory_space=pltpu.VMEM)] + [anywhere] * 5,
        out_specs=anywhere,
        out_shape=jax.ShapeDtypeStruct(fields.shape, f32),
        scratch_shapes=[
            pltpu.VMEM((plan.planes + 2, plan.fields, plan.theta, plan.radial), f32),
            pltpu.VMEM((2, plan.fields, plan.planes, plan.radial), f32),
            pltpu.VMEM((plan.planes, plan.fields, plan.theta, plan.radial - LANES), f32),
            pltpu.SemaphoreType.DMA((4,)),
            pltpu.SemaphoreType.DMA((plan.planes,)),
            pltpu.SemaphoreType.DMA((plan.planes,)),
        ],
        compiler_params=pltpu.CompilerParams(vmem_limit_bytes=VMEM_LIMIT),
        name="outer",
        cost_estimate=pl.CostEstimate(flops=16000000, bytes_accessed=5000000, transcendentals=0),
    )(coef, fields, *halos)


def halves(x):
    high = x.astype(jnp.bfloat16)
    low = (x - high.astype(jnp.float32)).astype(jnp.bfloat16)
    return jnp.concatenate([high, low, high], axis=0)


def filter_kernel(plan, forward_ref, inverse_ref, mask_ref, after_ref, *refs):
    del after_ref
    pieces = refs[: plan.sectors]
    own_ref, across_ref, edge_ref, sums_ref, message_a, message_b = refs[plan.sectors : plan.sectors + 6]
    data, table, sems = refs[plan.sectors + 6 :]
    sector = lax.axis_index("az")
    odd_plane = lax.axis_index("ax") % 2
    theta = plan.theta
    copies = [pltpu.make_async_copy(inverse_ref.at[sector], table, sems.at[plan.sectors])]
    for p in range(plan.sectors):
        copies.append(pltpu.make_async_copy(pieces[p], data.at[:, sector ^ p], sems.at[p]))
    for copy in copies:
        copy.start()
    for copy in copies:
        copy.wait()
    mask = mask_ref[...]
    mask = jnp.concatenate([mask, mask], axis=1)

    for g in range(0, plan.groups, 2):
        both = jnp.concatenate(
            [data[g].reshape(plan.total, LANES), data[g + 1].reshape(plan.total, LANES)], axis=1
        )
        spectra = jnp.dot(forward_ref[...], halves(both), preferred_element_type=jnp.float32)
        kept = halves(spectra * mask)
        state = jnp.dot(table[...], kept, preferred_element_type=jnp.float32)
        for i in range(2):
            lanes = slice(i * LANES, (i + 1) * LANES)
            own_ref[g + i] = state[:theta, lanes]
            across_ref[g + i] = state[theta : 2 * theta, lanes]
            edge_ref[g + i] = state[2 * theta : 2 * theta + 8, lanes]

    total = data[plan.groups, 0]
    for p in range(1, plan.sectors):
        total = total + data[plan.groups, p]
    total = total * (1.0 / plan.total)
    lane = lax.broadcasted_iota(jnp.int32, (plan.planes, LANES), 1)
    for f in range(plan.fields):
        value = moved(total, plan.full - f * plan.rest)
        sums_ref[f] = jnp.where((lane >= plan.full) & (lane < NEAR), value, 0.0)

    def message(ref, k):
        for f in range(plan.fields):
            number, first = plan.place(f, k)
            own = own_ref[number]
            value = jnp.where(lane < plan.full, moved(own, -first), sums_ref[f, k : k + 1])
            ref[f] = value

    def both_messages(ref_low, ref_high):
        message(ref_low, 0)
        message(ref_high, plan.planes - 1)

    pl.when(odd_plane == 1)(lambda: both_messages(message_a, message_b))
    pl.when(odd_plane == 0)(lambda: both_messages(message_b, message_a))


def filtered(plan, pieces, after):
    anywhere = pl.BlockSpec(memory_space=pl.ANY)
    inside = pl.BlockSpec(memory_space=pltpu.VMEM)
    f32 = jnp.float32
    cube = jax.ShapeDtypeStruct((plan.groups, plan.theta, LANES), f32)
    plane = jax.ShapeDtypeStruct((plan.fields, plan.theta, LANES), f32)
    return pl.pallas_call(
        functools.partial(filter_kernel, plan),
        in_specs=[inside, anywhere, inside, anywhere] + [anywhere] * plan.sectors,
        out_specs=[inside] * 6,
        out_shape=[
            cube,
            cube,
            jax.ShapeDtypeStruct((plan.groups, 8, LANES), f32),
            jax.ShapeDtypeStruct((plan.fields, plan.planes, LANES), f32),
            plane,
            plane,
        ],
        scratch_shapes=[
            pltpu.VMEM((plan.groups + 1, plan.sectors, plan.theta, LANES), f32),
            pltpu.VMEM((2 * plan.theta + 16, 6 * plan.modes), jnp.bfloat16),
            pltpu.SemaphoreType.DMA((plan.sectors + 1,)),
        ],
        compiler_params=pltpu.CompilerParams(vmem_limit_bytes=VMEM_LIMIT),
        name="filter",
        cost_estimate=pl.CostEstimate(flops=200000000, bytes_accessed=1500000, transcendentals=0),
    )(
        jnp.asarray(plan.forward()),
        jnp.asarray(plan.inverse()),
        jnp.asarray(plan.mask()),
        after,
        *pieces,
    )


def inner_kernel(
    plan, coef_ref, own_ref, across_ref, edge_ref, sums_ref, message_a, message_b,
    x_ref, az_a, az_b, ax_a, ax_b, other_ref, out_ref, buf, side, state, done, sems, ins, outs
):
    del other_ref
    planes = plan.planes
    theta = plan.theta
    halos = []
    load_halos(plan, halos, az_a, az_b, ax_a, ax_b, 2 * LANES, buf, side, sems)
    fetch = [
        pltpu.make_async_copy(x_ref.at[:, k, :, pl.ds(0, 2 * LANES)], buf.at[k + 1], ins.at[k])
        for k in range(planes)
    ]
    store = [
        pltpu.make_async_copy(done.at[k], out_ref.at[:, k, :, pl.ds(0, LANES)], outs.at[k])
        for k in range(planes)
    ]
    for copy in halos + fetch:
        copy.start()
    shape = (theta, LANES)
    lane = lax.broadcasted_iota(jnp.int32, shape, 1)
    row = lax.broadcasted_iota(jnp.int32, shape, 0)
    sign = (1 - 2 * (row & 1)).astype(jnp.float32)
    lane1 = lax.broadcasted_iota(jnp.int32, (1, LANES), 1)
    first = pl.ds(0, LANES)
    coef = [coef_ref[i : i + 1, :LANES] for i in range(7)]
    flips = (-1.0, -1.0, 1.0, 1.0, 1.0)

    for copy in halos + fetch:
        copy.wait()
    for k in range(planes):
        for f in range(plan.fields):
            number, start = plan.place(f, k)
            state[k + 1, f] = jnp.where(
                lane < plan.full,
                moved(own_ref[number], -start),
                buf[k + 1, f, :, first] - sign * sums_ref[f, k : k + 1],
            )
    odd_plane = lax.axis_index("ax") % 2
    high = planes + 1
    slot_a = (1 - odd_plane) * high
    for message, slot in ((message_a, slot_a), (message_b, high - slot_a)):
        for f in range(plan.fields):
            raw = buf[slot, f, :, first]
            state[slot, f] = jnp.where(lane < plan.full, message[f], raw - sign * message[f])

    for k in range(planes):
        q, jp, jm, tp, tm, kp, km = ([] for _ in range(7))
        for f in range(plan.fields):
            number, start = plan.place(f, k)
            x = state[k + 1, f]
            q.append(x)
            high_part = pltpu.roll(buf[k + 1, f, :, pl.ds(LANES, LANES)], LANES - 1, 1)
            jp.append(jnp.where(lane == LANES - 1, high_part, pltpu.roll(x, LANES - 1, 1)))
            opposite = flips[f] * moved(across_ref[number], -start)
            jm.append(jnp.where(lane == 0, opposite, pltpu.roll(x, 1, 1)))
            total = sums_ref[f, k : k + 1]
            sides = moved(edge_ref[number], -start)
            before = jnp.where(lane1 < plan.full, sides[0:1], side[0, f, k : k + 1, first] + total)
            after = jnp.where(lane1 < plan.full, sides[1:2], side[1, f, k : k + 1, first] - total)
            up, down = turned(x, row, before, after)
            tp.append(up)
            tm.append(down)
            kp.append(state[k + 2, f])
            km.append(state[k, f])
        result = advance(coef, q, jp, jm, tp, tm, kp, km)
        for f in range(plan.fields):
            done[k, f] = result[f]
        store[k].start()
    for copy in store:
        copy.wait()


def inner(plan, coef, parts, messages, fields, halos, partial):
    anywhere = pl.BlockSpec(memory_space=pl.ANY)
    inside = pl.BlockSpec(memory_space=pltpu.VMEM)
    f32 = jnp.float32
    operands = (coef, *parts, *messages, fields, *halos, partial)
    return pl.pallas_call(
        functools.partial(inner_kernel, plan),
        in_specs=[inside] * 7 + [anywhere] * 6,
        out_specs=anywhere,
        out_shape=jax.ShapeDtypeStruct(fields.shape, f32),
        input_output_aliases={len(operands) - 1: 0},
        scratch_shapes=[
            pltpu.VMEM((plan.planes + 2, plan.fields, plan.theta, 2 * LANES), f32),
            pltpu.VMEM((2, plan.fields, plan.planes, 2 * LANES), f32),
            pltpu.VMEM((plan.planes + 2, plan.fields, plan.theta, LANES), f32),
            pltpu.VMEM((plan.planes, plan.fields, plan.theta, LANES), f32),
            pltpu.SemaphoreType.DMA((4,)),
            pltpu.SemaphoreType.DMA((plan.planes,)),
            pltpu.SemaphoreType.DMA((plan.planes,)),
        ],
        compiler_params=pltpu.CompilerParams(vmem_limit_bytes=VMEM_LIMIT),
        name="inner",
        cost_estimate=pl.CostEstimate(flops=6000000, bytes_accessed=2500000, transcendentals=0),
    )(*operands)


def pairs(count, start, periodic):
    route = []
    for low in range(start, count, 2):
        high = low + 1
        if high == count and not periodic:
            continue
        route += [(low, high % count), (high % count, low)]
    return route


def fast_on_device(fields):
    sectors = lax.axis_size("az")
    slabs = lax.axis_size("ax")
    plan = Plan(fields.shape, sectors)
    coef = jnp.asarray(plan.coefficients())

    packed = pack(plan, fields)
    pieces = [packed]
    for p in range(1, sectors):
        pieces.append(lax.ppermute(packed, "az", [(i, i ^ p) for i in range(sectors)]))

    az_a, az_b, ax_a, ax_b = edges(plan, fields)
    halos = (
        lax.ppermute(az_a, "az", pairs(sectors, 0, True)),
        lax.ppermute(az_b, "az", pairs(sectors, 1, True)),
        lax.ppermute(ax_a, "ax", pairs(slabs, 0, False)),
        lax.ppermute(ax_b, "ax", pairs(slabs, 1, False)),
    )
    partial = outer(plan, coef, fields, halos)
    *parts, message_a, message_b = filtered(plan, pieces, partial)
    messages = (
        lax.ppermute(message_a, "ax", pairs(slabs, 0, False)),
        lax.ppermute(message_b, "ax", pairs(slabs, 1, False)),
    )
    return inner(plan, coef, parts, messages, fields, halos, partial)


def on_device(fields):
    total_theta = fields.shape[2] * lax.axis_size("az")
    if Plan.fits(fields.shape, lax.axis_size("az"), total_theta):
        return fast_on_device(fields)
    return general_on_device(fields)


def solution(mesh):
    placed = (P(None, "ax", "az", None),)
    return jax.shard_map(
        on_device, mesh=mesh, in_specs=placed, out_specs=P(None, "ax", "az", None), check_vma=False
    )
```

```python
import functools

import jax
import jax.numpy as jnp
import numpy as np
from jax import lax
from jax.experimental import pallas as pl
from jax.experimental.pallas import tpu as pltpu
from jax.sharding import PartitionSpec as P

NEAR = 40


viscosity = 0.2
time_step = 0.1
buoyancy = 1.0

LANES = 128
VMEM_LIMIT = 24 * 1024 * 1024


def swapped(block, axis, distance):
    count = lax.axis_size(axis)
    route = []
    for low in range(count):
        high = low | 1 << distance
        if high != low and high < count:
            route += [(low, high), (high, low)]
    return lax.ppermute(block, axis, route)


def with_halo(block, sides, width, periodic):
    for axis, dim in sides:
        count = lax.axis_size(axis)
        forward = [(i, i + 1) for i in range(count - 1)]
        if periodic:
            forward.append((count - 1, 0))
        backward = [(target, source) for source, target in forward]
        low = lax.ppermute(
            lax.slice_in_dim(block, block.shape[dim] - width, None, axis=dim), axis, forward
        )
        high = lax.ppermute(lax.slice_in_dim(block, 0, width, axis=dim), axis, backward)
        block = jnp.concatenate([low, block, high], axis=dim)
    return block


def mode_tables(theta_index, total_theta, modes):
    column = jnp.arange(modes, dtype=jnp.int32)
    product = theta_index[:, None] * column[None, :] % total_theta
    angle = product.astype(jnp.float32) * (2.0 * jnp.pi / total_theta)
    cosine = jnp.cos(angle)
    sine = jnp.sin(angle)
    weight = jnp.where(column == 0, 1.0, 2.0).astype(jnp.float32) / total_theta
    forward = jnp.concatenate([cosine * weight[None, :], sine * (2.0 / total_theta)], axis=1)
    inverse = jnp.concatenate([cosine, sine], axis=1)
    return (forward, inverse)


def cycle_mask(cycles, modes):
    cycle_index = jnp.arange(cycles, dtype=jnp.int32)
    cutoff = jnp.minimum(355 * (2 * cycle_index + 1) // 226, modes - 1)
    column = jnp.arange(modes, dtype=jnp.int32)
    keep = (column[None, :] <= cutoff[:, None]).astype(jnp.float32)
    return jnp.concatenate([keep, keep], axis=1)


def operators(
    center, radial_plus, radial_minus, theta_plus, theta_minus, axial_plus, axial_minus, total_theta
):
    radius = jnp.arange(center.shape[-1], dtype=jnp.float32) + 0.5
    step_angle = 2.0 * jnp.pi / total_theta
    d_radial = (radial_plus - radial_minus) * 0.5
    d_theta = (theta_plus - theta_minus) / (2.0 * step_angle)
    d_axial = (axial_plus - axial_minus) * 0.5
    laplace = (
        radial_plus - 2.0 * center + radial_minus + (radial_plus - radial_minus) / (2.0 * radius)
    )
    laplace = laplace + (theta_plus - 2.0 * center + theta_minus) / (
        radius * radius * step_angle * step_angle
    )
    laplace = laplace + axial_plus - 2.0 * center + axial_minus
    return (d_radial, d_theta, d_axial, laplace)


def general_on_device(fields):
    count_fields, planes, theta_dev, radial = fields.shape
    sectors = lax.axis_size("az")
    total_theta = theta_dev * sectors
    modes = min(128, total_theta // 2)
    sector = lax.axis_index("az")
    own_index = sector * theta_dev + jnp.arange(theta_dev, dtype=jnp.int32)
    own_forward, own_inverse = mode_tables(own_index, total_theta, modes)
    inner_cycles = fields[:, :, :, :NEAR]
    kept = None
    piece = lax.all_gather(inner_cycles, "az", axis=2, tiled=True)
    piece_index = jnp.arange(piece.shape[2], dtype=jnp.int32)
    piece_forward, unused_inverse = mode_tables(piece_index, total_theta, modes)
    spectra = jnp.einsum("fztj,tc->fzjc", piece, piece_forward, precision=lax.Precision.HIGHEST)
    kept = spectra * cycle_mask(NEAR, modes)[None, None]
    smoothed = jnp.einsum("fzjc,tc->fztj", kept, own_inverse, precision=lax.Precision.HIGHEST)
    state = jnp.concatenate([smoothed, fields[:, :, :, NEAR:]], axis=3)
    flip = jnp.array([-1.0, -1.0, 1.0, 1.0, 1.0], dtype=jnp.float32)[:, None, None]
    top_bit = sectors.bit_length() - 1
    opposite = swapped(state[:, :, :, 0], "az", top_bit - 1)
    opposite = opposite * flip
    theta_padded = with_halo(state, (("az", 2),), 1, True)
    axial_padded = with_halo(state, (("ax", 1),), 1, False)
    radial_plus = jnp.concatenate([state[:, :, :, 1:], jnp.zeros_like(state[:, :, :, :1])], axis=3)
    radial_minus = jnp.concatenate([opposite[:, :, :, None], state[:, :, :, :-1]], axis=3)
    d_radial, d_theta, d_axial, laplace = operators(
        state,
        radial_plus,
        radial_minus,
        theta_padded[:, :, 2:, :],
        theta_padded[:, :, :-2, :],
        axial_padded[:, 2:, :, :],
        axial_padded[:, :-2, :, :],
        total_theta,
    )
    radius = jnp.arange(radial, dtype=jnp.float32) + 0.5
    radial_u = state[0]
    theta_u = state[1]
    axial_u = state[2]
    change = (
        -(radial_u[None] * d_radial + (theta_u / radius)[None] * d_theta + axial_u[None] * d_axial)
        + viscosity * laplace
    )
    inverse_square = 1.0 / (radius * radius)
    first = (
        change[0]
        + theta_u * theta_u / radius
        - viscosity * (radial_u * inverse_square + 2.0 * inverse_square * d_theta[1])
    )
    second = (
        change[1]
        - radial_u * theta_u / radius
        - viscosity * (theta_u * inverse_square - 2.0 * inverse_square * d_theta[0])
    )
    third = change[2] + buoyancy * state[3]
    change = jnp.concatenate([first[None], second[None], third[None], change[3:]], axis=0)
    return state + time_step * change


class Plan:
    def __init__(self, shape, sectors):
        self.fields, self.planes, self.theta, self.radial = shape
        self.sectors = sectors
        self.total = self.theta * sectors
        self.modes = min(128, self.total // 2)
        cycle = np.arange(NEAR)
        self.cut = np.minimum(355 * (2 * cycle + 1) // 226, self.modes - 1)
        self.full = int(np.sum(self.cut < self.modes - 1))
        self.rest = NEAR - self.full
        self.beside = LANES // max(self.full, 1)
        self.groups = -(-self.fields * self.planes // self.beside)
        self.early = tuple(range(sectors // 2 + 1))
        self.late = tuple(range(sectors // 2 + 1, sectors))
        self.depth = 256

    def place(self, f, k):
        index = k * self.fields + f
        return index // self.beside, index % self.beside * self.full

    @staticmethod
    def fits(shape, sectors, total):
        if sectors & (sectors - 1) or total // 2 > 128 or total != LANES or shape[2] != 16:
            return False
        plan = Plan(shape, sectors)
        return (
            plan.full > 0
            and plan.fields == 5
            and plan.planes == plan.theta
            and plan.rest * plan.fields <= LANES
            and plan.groups % 2 == 0
            and 3 * len(plan.early) * plan.theta <= plan.depth
            and plan.radial % LANES == 0
            and plan.radial > 2 * LANES
        )

    def split(self, table):
        high = table.astype(jnp.bfloat16)
        low = (table - high.astype(np.float32)).astype(jnp.bfloat16)
        return np.concatenate([high, high, low], axis=-1)

    def forward(self, pieces):
        theta = np.arange(self.total)
        mode = np.arange(self.modes)
        angle = (np.outer(mode, theta) % self.total) * (2.0 * np.pi / self.total)
        weight = np.where(mode == 0, 1.0, 2.0)[:, None] / self.total
        table = np.concatenate([np.cos(angle) * weight, np.sin(angle) * 2.0 / self.total], axis=0)
        table = table.astype(np.float32).reshape(2 * self.modes, self.sectors, self.theta)
        blocks = []
        for sector in range(self.sectors):
            chosen = np.concatenate([table[:, sector ^ p] for p in pieces], axis=1)
            chosen = self.split(chosen)
            pad = np.zeros((chosen.shape[0], self.depth - chosen.shape[1]), chosen.dtype)
            blocks.append(np.concatenate([chosen, pad], axis=1))
        return np.stack(blocks)

    def inverse(self):
        mode = np.arange(self.modes)
        blocks = []
        for sector in range(self.sectors):
            own = sector * self.theta + np.arange(self.theta)
            index = np.concatenate([own, own + self.total // 2, own[:1] - 1, own[-1:] + 1])
            angle = (np.outer(index, mode) % self.total) * (2.0 * np.pi / self.total)
            table = np.concatenate([np.cos(angle), np.sin(angle)], axis=1)
            pad = np.zeros((16 - 2, table.shape[1]))
            blocks.append(np.concatenate([table, pad], axis=0))
        return self.split(np.stack(blocks).astype(np.float32))

    def mask(self):
        mode = np.arange(self.modes)
        keep = np.zeros((self.modes, LANES), np.float32)
        for i in range(self.beside):
            keep[:, i * self.full : (i + 1) * self.full] = (
                mode[:, None] <= self.cut[None, : self.full]
            )
        return np.concatenate([keep, keep], axis=0)

    def coefficients(self):
        radius = np.arange(self.radial) + 0.5
        step = 2.0 * np.pi / self.total
        nu_dt = viscosity * time_step
        square = 1.0 / (radius * radius * step * step)
        rows = [
            1.0 - nu_dt * (4.0 + 2.0 * square),
            nu_dt * square,
            nu_dt / (2.0 * radius),
            time_step / (2.0 * step * radius),
            time_step / radius,
            nu_dt / (radius * radius),
            nu_dt / (step * radius * radius),
        ]
        rows.append(np.zeros(self.radial))
        return np.stack(rows).astype(np.float32)


def moved(x, lanes):
    return x if lanes % LANES == 0 else pltpu.roll(x, lanes % LANES, 1)


def pack_kernel(plan, x_ref, out_ref, buf, sems):
    shape = (plan.theta, LANES)
    lane = lax.broadcasted_iota(jnp.int32, shape, 1)
    row = lax.broadcasted_iota(jnp.int32, shape, 0)
    sign = (1 - 2 * (row & 1)).astype(jnp.float32)
    chunk = 4
    copies = [
        pltpu.make_async_copy(
            x_ref.at[:, pl.ds(i * chunk, chunk), :, pl.ds(0, LANES)], buf.at[i], sems.at[i]
        )
        for i in range(plan.planes // chunk)
    ]
    for copy in copies:
        copy.start()
    group = jnp.zeros(shape, jnp.float32)
    sums = [jnp.zeros(shape, jnp.float32) for _ in range(plan.fields)]
    for k in range(plan.planes):
        if k % chunk == 0:
            copies[k // chunk].wait()
        for f in range(plan.fields):
            x = buf[k // chunk, f, k % chunk]
            number, first = plan.place(f, k)
            part = moved(x, first)
            if first:
                part = jnp.where((lane >= first) & (lane < first + plan.full), part, group)
            group = part
            if first // plan.full == plan.beside - 1 or (f, k) == (plan.fields - 1, plan.planes - 1):
                out_ref[number] = group
            alternating = jnp.sum(x * sign, axis=0, keepdims=True)
            sums[f] = jnp.where(row == k, alternating, sums[f])
    last = sums[0]
    for f in range(plan.fields):
        start = f * plan.rest
        last = jnp.where(lane >= start, moved(sums[f], start - plan.full), last)
    out_ref[plan.groups] = last


def pack(plan, fields):
    f32 = jnp.float32
    chunks = plan.planes // 4
    return pl.pallas_call(
        functools.partial(pack_kernel, plan),
        in_specs=[pl.BlockSpec(memory_space=pl.ANY)],
        out_specs=pl.BlockSpec(memory_space=pltpu.VMEM),
        out_shape=jax.ShapeDtypeStruct((plan.groups + 1, plan.theta, LANES), f32),
        scratch_shapes=[
            pltpu.VMEM((chunks, plan.fields, 4, plan.theta, LANES), f32),
            pltpu.SemaphoreType.DMA((chunks,)),
        ],
        name="pack",
        cost_estimate=pl.CostEstimate(flops=1000000, bytes_accessed=800000, transcendentals=0),
    )(fields)


def pick_columns(plan, x_ref, keep_high, ref, base):
    last = plan.theta - 1
    tiles = plan.radial // LANES
    for f in range(plan.fields):
        for k in range(plan.planes):
            for tile in range(tiles):
                here = slice(tile * LANES, (tile + 1) * LANES)
                low = x_ref[f, k, 0:1, here]
                high = x_ref[f, k, last : last + 1, here]
                ref[base + f * tiles + tile, k : k + 1, :] = jnp.where(keep_high, high, low)


def beside_kernel(plan, x_ref, packed_ref, again, beside):
    again[...] = packed_ref[...]
    beside[pl.ds(0, plan.groups + 1)] = packed_ref[...]
    even_theta = lax.axis_index("az") % 2 == 0
    pick_columns(plan, x_ref, even_theta, beside, plan.groups + 1)


def edges_kernel(plan, x_ref, after_ref, az_b, ax_a, ax_b):
    del after_ref
    even_theta = lax.axis_index("az") % 2 == 0
    even_plane = lax.axis_index("ax") % 2 == 0
    pick_columns(plan, x_ref, jnp.logical_not(even_theta), az_b, 0)

    @pl.when(even_plane)
    def _():
        ax_a[...] = x_ref[:, plan.planes - 1]
        ax_b[...] = x_ref[:, 0]

    @pl.when(jnp.logical_not(even_plane))
    def _():
        ax_a[...] = x_ref[:, 0]
        ax_b[...] = x_ref[:, plan.planes - 1]


def beside(plan, fields, packed):
    f32 = jnp.float32
    columns = plan.fields * plan.radial // LANES
    inside = pl.BlockSpec(memory_space=pltpu.VMEM)
    return pl.pallas_call(
        functools.partial(beside_kernel, plan),
        in_specs=[inside] * 2,
        out_specs=[inside] * 2,
        out_shape=[
            jax.ShapeDtypeStruct(packed.shape, f32),
            jax.ShapeDtypeStruct((plan.groups + 1 + columns, plan.theta, LANES), f32),
        ],
        compiler_params=pltpu.CompilerParams(vmem_limit_bytes=VMEM_LIMIT),
        name="beside",
        cost_estimate=pl.CostEstimate(flops=0, bytes_accessed=1000000, transcendentals=0),
    )(fields, packed)


def edges(plan, fields, after):
    f32 = jnp.float32
    columns = plan.fields * plan.radial // LANES
    plane = jax.ShapeDtypeStruct((plan.fields, plan.theta, plan.radial), f32)
    inside = pl.BlockSpec(memory_space=pltpu.VMEM)
    return pl.pallas_call(
        functools.partial(edges_kernel, plan),
        in_specs=[inside, inside],
        out_specs=[inside] * 3,
        out_shape=[jax.ShapeDtypeStruct((columns, plan.theta, LANES), f32), plane, plane],
        compiler_params=pltpu.CompilerParams(vmem_limit_bytes=VMEM_LIMIT),
        name="edges",
        cost_estimate=pl.CostEstimate(flops=0, bytes_accessed=1000000, transcendentals=0),
    )(fields, after)


def advance(coef, q, jp, jm, tp, tm, kp, km):
    c0, c2, half, angular, over, square, cross = coef
    ur, ut, uz, temp = q[:4]
    radial = half - (0.5 * time_step) * ur
    azimuthal = angular * ut
    axial = (0.5 * time_step) * uz
    nu_dt = viscosity * time_step
    out = []
    d_theta = []
    for f in range(5):
        dt = tp[f] - tm[f]
        if f < 2:
            d_theta.append(dt)
        value = c0 * q[f] + nu_dt * ((jp[f] + jm[f]) + (kp[f] + km[f]))
        value = value + c2 * (tp[f] + tm[f])
        value = value + (jp[f] - jm[f]) * radial
        value = value - dt * azimuthal
        value = value - (kp[f] - km[f]) * axial
        out.append(value)
    swirl = over * ut
    out[0] = out[0] + swirl * ut - square * ur - cross * d_theta[1]
    out[1] = out[1] - swirl * ur - square * ut + cross * d_theta[0]
    out[2] = out[2] + (time_step * buoyancy) * temp
    return out


def turned(x, row, before, after):
    last = x.shape[0] - 1
    up = jnp.where(row == last, after, pltpu.roll(x, last, 0))
    down = jnp.where(row == 0, before, pltpu.roll(x, 1, 0))
    return up, down


def choose_halos(plan, tiles, az_a, az_b, ax_a, ax_b, side, ends):
    even_theta = lax.axis_index("az") % 2 == 0
    even_plane = lax.axis_index("ax") % 2 == 0
    all_tiles = plan.radial // LANES
    for f in range(plan.fields):
        for tile in tiles:
            here = slice(tile * LANES, (tile + 1) * LANES)
            number = f * all_tiles + tile
            a = az_a[plan.groups + 1 + number]
            b = az_b[number]
            side[0, number] = jnp.where(even_theta, b, a)
            side[1, number] = jnp.where(even_theta, a, b)
            a = ax_a[f, :, here]
            b = ax_b[f, :, here]
            ends[0, f, :, here] = jnp.where(even_plane, b, a)
            ends[1, f, :, here] = jnp.where(even_plane, a, b)


def outer_kernel(plan, coef_ref, x_ref, done, token):
    planes = plan.planes
    tiles = plan.radial // LANES
    token[...] = jnp.zeros_like(token)
    shape = (plan.theta, LANES)
    lane = lax.broadcasted_iota(jnp.int32, shape, 1)
    row = lax.broadcasted_iota(jnp.int32, shape, 0)

    def step(group, carry):
        start = pl.multiple_of(group * 4, 4)
        for i in range(4):
            k = start + i
            for tile in range(1, tiles):
                here = pl.ds(tile * LANES, LANES)
                coef = [coef_ref[j : j + 1, here] for j in range(7)]
                q, jp, jm, tp, tm, kp, km = ([] for _ in range(7))
                for f in range(plan.fields):
                    x = x_ref[f, k, :, here]
                    low = x_ref[f, k, :, pl.ds((tile - 1) * LANES, LANES)]
                    q.append(x)
                    high = 0.0
                    if tile + 1 < tiles:
                        high = x_ref[f, k, :, pl.ds((tile + 1) * LANES, LANES)]
                        high = pltpu.roll(high, LANES - 1, 1)
                    jp.append(jnp.where(lane == LANES - 1, high, pltpu.roll(x, LANES - 1, 1)))
                    jm.append(jnp.where(lane == 0, pltpu.roll(low, 1, 1), pltpu.roll(x, 1, 1)))
                    up, down = turned(x, row, 0.0, 0.0)
                    tp.append(up)
                    tm.append(down)
                    if i < 3:
                        above = x_ref[f, k + 1, :, here]
                    else:
                        above = x_ref[f, jnp.minimum(k + 1, planes - 1), :, here]
                        above = jnp.where(k == planes - 1, 0.0, above)
                    if i > 0:
                        below = x_ref[f, k - 1, :, here]
                    else:
                        below = x_ref[f, jnp.maximum(k - 1, 0), :, here]
                        below = jnp.where(k == 0, 0.0, below)
                    kp.append(above)
                    km.append(below)
                result = advance(coef, q, jp, jm, tp, tm, kp, km)
                for f in range(plan.fields):
                    done[k, f, :, pl.ds((tile - 1) * LANES, LANES)] = result[f]
        return carry

    lax.fori_loop(0, planes // 4, step, 0)


def outer(plan, coef, fields):
    inside = pl.BlockSpec(memory_space=pltpu.VMEM)
    f32 = jnp.float32
    return pl.pallas_call(
        functools.partial(outer_kernel, plan),
        in_specs=[inside] * 2,
        out_specs=[inside] * 2,
        out_shape=[
            jax.ShapeDtypeStruct((plan.planes, plan.fields, plan.theta, plan.radial - LANES), f32),
            jax.ShapeDtypeStruct((8, LANES), f32),
        ],
        compiler_params=pltpu.CompilerParams(vmem_limit_bytes=VMEM_LIMIT),
        name="outer",
        cost_estimate=pl.CostEstimate(flops=16000000, bytes_accessed=5000000, transcendentals=0),
    )(coef, fields)


def seams_kernel(
    plan, coef_ref, x_ref, own_a, own_b, az_a, az_b, ax_a, ax_b, part_ref, out_ref, done, outs
):
    del part_ref
    planes = plan.planes
    tiles = plan.radial // LANES
    even_theta = lax.axis_index("az") % 2 == 0
    even_plane = lax.axis_index("ax") % 2 == 0
    base = plan.groups + 1
    nu_dt = viscosity * time_step
    last = plan.theta - 1

    def store(k):
        return pltpu.make_async_copy(
            done.at[k], out_ref.at[:, k, :, pl.ds(LANES, plan.radial - LANES)], outs.at[k]
        )

    for tile in range(1, tiles):
        here = slice(tile * LANES, (tile + 1) * LANES)
        there = slice((tile - 1) * LANES, tile * LANES)
        c2 = coef_ref[1:2, here]
        angular = coef_ref[3:4, here]
        cross = coef_ref[6:7, here]
        number = tiles + tile
        mine_a = own_a[base + number]
        mine_b = own_b[number]
        turn_low = angular * jnp.where(even_theta, mine_b, mine_a)
        turn_high = angular * jnp.where(even_theta, mine_a, mine_b)
        before = []
        after = []
        for f in range(plan.fields):
            a = az_a[base + f * tiles + tile]
            b = az_b[f * tiles + tile]
            before.append(jnp.where(even_theta, b, a))
            after.append(jnp.where(even_theta, a, b))
        for f in range(plan.fields):
            low = (c2 + turn_low) * before[f]
            high = (c2 - turn_high) * after[f]
            if f == 0:
                low = low + cross * before[1]
                high = high - cross * after[1]
            if f == 1:
                low = low - cross * before[0]
                high = high + cross * after[0]
            for k in range(planes):
                done[k, f, 0:1, there] += low[k : k + 1]
                done[k, f, last : last + 1, there] += high[k : k + 1]
            a = ax_a[f, :, here]
            b = ax_b[f, :, here]
            axial = (0.5 * time_step) * x_ref[2, 0, :, here]
            done[0, f, :, there] += (nu_dt + axial) * jnp.where(even_plane, b, a)
            axial = (0.5 * time_step) * x_ref[2, planes - 1, :, here]
            done[planes - 1, f, :, there] += (nu_dt - axial) * jnp.where(even_plane, a, b)
    for k in range(planes):
        store(k).start()
    for k in range(planes):
        store(k).wait()


def seams(plan, coef, fields, own, halos, part):
    inside = pl.BlockSpec(memory_space=pltpu.VMEM)
    return pl.pallas_call(
        functools.partial(seams_kernel, plan),
        in_specs=[inside] * 9,
        out_specs=[pl.BlockSpec(memory_space=pl.ANY), inside],
        out_shape=[
            jax.ShapeDtypeStruct(fields.shape, jnp.float32),
            jax.ShapeDtypeStruct(part.shape, jnp.float32),
        ],
        input_output_aliases={8: 1},
        scratch_shapes=[pltpu.SemaphoreType.DMA((plan.planes,))],
        compiler_params=pltpu.CompilerParams(vmem_limit_bytes=VMEM_LIMIT),
        name="seams",
        cost_estimate=pl.CostEstimate(flops=1000000, bytes_accessed=4000000, transcendentals=0),
    )(coef, fields, *own, *halos, part)[0]


def halo_scratch(plan):
    columns = plan.fields * plan.radial // LANES
    return [
        pltpu.VMEM((2, columns, plan.planes, LANES), jnp.float32),
        pltpu.VMEM((2, plan.fields, plan.theta, plan.radial), jnp.float32),
    ]


def halves(x, depth=None):
    high = x.astype(jnp.bfloat16)
    low = (x - high.astype(jnp.float32)).astype(jnp.bfloat16)
    parts = [high, low, high]
    if depth is not None:
        parts.append(jnp.zeros((depth - 3 * x.shape[0], x.shape[1]), jnp.bfloat16))
    return jnp.concatenate(parts, axis=0)


def two_groups(pieces, g):
    return jnp.concatenate(
        [jnp.concatenate([piece[g + i] for piece in pieces], axis=0) for i in range(2)], axis=1
    )


def early_kernel(plan, forward_ref, token_ref, *refs):
    del token_ref
    pieces = refs[: len(plan.early)]
    spectra_ref, total_ref = refs[len(plan.early) :]
    table = forward_ref[lax.axis_index("az")]
    for g in range(0, plan.groups, 2):
        both = halves(two_groups(pieces, g), plan.depth)
        spectra_ref[g // 2] = jnp.dot(table, both, preferred_element_type=jnp.float32)
    total = pieces[0][plan.groups]
    for piece in pieces[1:]:
        total = total + piece[plan.groups]
    total_ref[...] = total


def early_spectra(plan, pieces, token):
    inside = pl.BlockSpec(memory_space=pltpu.VMEM)
    f32 = jnp.float32
    return pl.pallas_call(
        functools.partial(early_kernel, plan),
        in_specs=[inside] * (2 + len(pieces)),
        out_specs=[inside] * 2,
        out_shape=[
            jax.ShapeDtypeStruct((plan.groups // 2, 2 * plan.modes, 2 * LANES), f32),
            jax.ShapeDtypeStruct((plan.theta, LANES), f32),
        ],
        compiler_params=pltpu.CompilerParams(vmem_limit_bytes=VMEM_LIMIT),
        name="early",
        cost_estimate=pl.CostEstimate(flops=200000000, bytes_accessed=1500000, transcendentals=0),
    )(jnp.asarray(plan.forward(plan.early)), token, *pieces)


def filter_kernel(plan, forward_ref, inverse_ref, mask_ref, early_ref, early_total, *refs):
    count = len(plan.late)
    pieces = refs[:count]
    own_ref, across_ref, edge_ref, sums_ref, message_a, message_b = refs[count:]
    odd_plane = lax.axis_index("ax") % 2
    theta = plan.theta
    sector = lax.axis_index("az")
    forward = forward_ref[sector]
    table = inverse_ref[sector]
    mask = mask_ref[...]
    mask = jnp.concatenate([mask, mask], axis=1)

    for g in range(0, plan.groups, 2):
        both = halves(two_groups(pieces, g), plan.depth)
        spectra = early_ref[g // 2] + jnp.dot(forward, both, preferred_element_type=jnp.float32)
        kept = halves(spectra * mask)
        state = jnp.dot(table, kept, preferred_element_type=jnp.float32)
        for i in range(2):
            lanes = slice(i * LANES, (i + 1) * LANES)
            own_ref[g + i] = state[:theta, lanes]
            across_ref[g + i] = state[theta : 2 * theta, lanes]
            edge_ref[g + i] = state[2 * theta : 2 * theta + 8, lanes]

    total = early_total[...]
    for piece in pieces:
        total = total + piece[plan.groups]
    total = total * (1.0 / plan.total)
    lane = lax.broadcasted_iota(jnp.int32, (plan.planes, LANES), 1)
    for f in range(plan.fields):
        value = moved(total, plan.full - f * plan.rest)
        sums_ref[f] = jnp.where((lane >= plan.full) & (lane < NEAR), value, 0.0)

    def message(ref, k):
        for f in range(plan.fields):
            number, first = plan.place(f, k)
            own = own_ref[number]
            value = jnp.where(lane < plan.full, moved(own, -first), sums_ref[f, k : k + 1])
            ref[f] = value

    def both_messages(ref_low, ref_high):
        message(ref_low, 0)
        message(ref_high, plan.planes - 1)

    pl.when(odd_plane == 1)(lambda: both_messages(message_a, message_b))
    pl.when(odd_plane == 0)(lambda: both_messages(message_b, message_a))


def filtered(plan, pieces, early):
    inside = pl.BlockSpec(memory_space=pltpu.VMEM)
    f32 = jnp.float32
    cube = jax.ShapeDtypeStruct((plan.groups, plan.theta, LANES), f32)
    plane = jax.ShapeDtypeStruct((plan.fields, plan.theta, LANES), f32)
    return pl.pallas_call(
        functools.partial(filter_kernel, plan),
        in_specs=[inside] * (5 + len(pieces)),
        out_specs=[inside] * 6,
        out_shape=[
            cube,
            cube,
            jax.ShapeDtypeStruct((plan.groups, 8, LANES), f32),
            jax.ShapeDtypeStruct((plan.fields, plan.planes, LANES), f32),
            plane,
            plane,
        ],
        compiler_params=pltpu.CompilerParams(vmem_limit_bytes=VMEM_LIMIT),
        name="filter",
        cost_estimate=pl.CostEstimate(flops=200000000, bytes_accessed=1500000, transcendentals=0),
    )(
        jnp.asarray(plan.forward(plan.late)),
        jnp.asarray(plan.inverse()),
        jnp.asarray(plan.mask()),
        *early,
        *pieces,
    )


def inner_kernel(
    plan, coef_ref, own_ref, across_ref, edge_ref, sums_ref, message_a, message_b,
    x_ref, az_a, az_b, ax_a, ax_b, other_ref, out_ref, side, ends, state, done, outs
):
    del other_ref
    planes = plan.planes
    theta = plan.theta
    tiles = plan.radial // LANES
    store = [
        pltpu.make_async_copy(done.at[k], out_ref.at[:, k, :, pl.ds(0, LANES)], outs.at[k])
        for k in range(planes)
    ]
    shape = (theta, LANES)
    lane = lax.broadcasted_iota(jnp.int32, shape, 1)
    row = lax.broadcasted_iota(jnp.int32, shape, 0)
    sign = (1 - 2 * (row & 1)).astype(jnp.float32)
    lane1 = lax.broadcasted_iota(jnp.int32, (1, LANES), 1)
    first = slice(0, LANES)
    coef = [coef_ref[i : i + 1, first] for i in range(7)]
    flips = (-1.0, -1.0, 1.0, 1.0, 1.0)
    choose_halos(plan, range(1), az_a, az_b, ax_a, ax_b, side, ends)

    for k in range(planes):
        for f in range(plan.fields):
            number, start = plan.place(f, k)
            state[k + 1, f] = jnp.where(
                lane < plan.full,
                moved(own_ref[number], -start),
                x_ref[f, k, :, first] - sign * sums_ref[f, k : k + 1],
            )
    even_plane = lax.axis_index("ax") % 2 == 0
    for f in range(plan.fields):
        a = message_a[f]
        b = message_b[f]
        for end, slot, message in ((0, 0, jnp.where(even_plane, b, a)), (1, planes + 1, jnp.where(even_plane, a, b))):
            raw = ends[end, f, :, first]
            state[slot, f] = jnp.where(lane < plan.full, message, raw - sign * message)

    for k in range(planes):
        q, jp, jm, tp, tm, kp, km = ([] for _ in range(7))
        for f in range(plan.fields):
            number, start = plan.place(f, k)
            x = state[k + 1, f]
            q.append(x)
            high_part = pltpu.roll(x_ref[f, k, :, LANES : 2 * LANES], LANES - 1, 1)
            jp.append(jnp.where(lane == LANES - 1, high_part, pltpu.roll(x, LANES - 1, 1)))
            opposite = flips[f] * moved(across_ref[number], -start)
            jm.append(jnp.where(lane == 0, opposite, pltpu.roll(x, 1, 1)))
            total = sums_ref[f, k : k + 1]
            sides = moved(edge_ref[number], -start)
            column = f * tiles
            before = jnp.where(lane1 < plan.full, sides[0:1], side[0, column, k : k + 1] + total)
            after = jnp.where(lane1 < plan.full, sides[1:2], side[1, column, k : k + 1] - total)
            up, down = turned(x, row, before, after)
            tp.append(up)
            tm.append(down)
            kp.append(state[k + 2, f])
            km.append(state[k, f])
        result = advance(coef, q, jp, jm, tp, tm, kp, km)
        for f in range(plan.fields):
            done[k, f] = result[f]
        store[k].start()
    for copy in store:
        copy.wait()


def inner(plan, coef, parts, messages, fields, halos, partial):
    anywhere = pl.BlockSpec(memory_space=pl.ANY)
    inside = pl.BlockSpec(memory_space=pltpu.VMEM)
    f32 = jnp.float32
    operands = (coef, *parts, *messages, fields, *halos, partial)
    return pl.pallas_call(
        functools.partial(inner_kernel, plan),
        in_specs=[inside] * 12 + [anywhere],
        out_specs=anywhere,
        out_shape=jax.ShapeDtypeStruct(fields.shape, f32),
        input_output_aliases={len(operands) - 1: 0},
        scratch_shapes=halo_scratch(plan)
        + [
            pltpu.VMEM((plan.planes + 2, plan.fields, plan.theta, LANES), f32),
            pltpu.VMEM((plan.planes, plan.fields, plan.theta, LANES), f32),
            pltpu.SemaphoreType.DMA((plan.planes,)),
        ],
        compiler_params=pltpu.CompilerParams(vmem_limit_bytes=VMEM_LIMIT),
        name="inner",
        cost_estimate=pl.CostEstimate(flops=6000000, bytes_accessed=2500000, transcendentals=0),
    )(*operands)


def pairs(count, start, periodic):
    route = []
    for low in range(start, count, 2):
        high = low + 1
        if high == count and not periodic:
            continue
        route += [(low, high % count), (high % count, low)]
    return route


def fast_on_device(fields):
    sectors = lax.axis_size("az")
    slabs = lax.axis_size("ax")
    plan = Plan(fields.shape, sectors)
    coef = jnp.asarray(plan.coefficients())

    def send(x, distance):
        return lax.ppermute(x, "az", [(i, i ^ distance) for i in range(sectors)])

    packed = pack(plan, fields)
    half = sectors // 2
    far = send(packed, half)
    again, wide = beside(plan, fields, packed)
    pieces = [None] * sectors
    pieces[0] = packed
    pieces[half] = far
    for p in range(half - 1, 0, -1):
        pieces[p] = send(wide if p == 1 else again, p)
    for p in range(half - 1, 0, -1):
        pieces[half + p] = send(far, p)
    part, token = outer(plan, coef, fields)
    early = early_spectra(plan, pieces[: half + 1], token)
    az_b, ax_a, ax_b = edges(plan, fields, early[1])
    halos = (
        pieces[1],
        lax.ppermute(az_b, "az", pairs(sectors, 1, True)),
        lax.ppermute(ax_a, "ax", pairs(slabs, 0, False)),
        lax.ppermute(ax_b, "ax", pairs(slabs, 1, False)),
    )
    *parts, message_a, message_b = filtered(plan, pieces[half + 1 :], early)
    messages = (
        lax.ppermute(message_a, "ax", pairs(slabs, 0, False)),
        lax.ppermute(message_b, "ax", pairs(slabs, 1, False)),
    )
    partial = seams(plan, coef, fields, (wide, az_b), halos, part)
    return inner(plan, coef, parts, messages, fields, halos, partial)


def on_device(fields):
    total_theta = fields.shape[2] * lax.axis_size("az")
    if Plan.fits(fields.shape, lax.axis_size("az"), total_theta):
        return fast_on_device(fields)
    return general_on_device(fields)


def solution(mesh):
    placed = (P(None, "ax", "az", None),)
    return jax.shard_map(
        on_device, mesh=mesh, in_specs=placed, out_specs=P(None, "ax", "az", None), check_vma=False
    )
```

```python
import functools

import jax
import jax.numpy as jnp
import numpy as np
from jax import lax
from jax.experimental import pallas as pl
from jax.experimental.pallas import tpu as pltpu
from jax.sharding import PartitionSpec as P

NEAR = 40


viscosity = 0.2
time_step = 0.1
buoyancy = 1.0

LANES = 128
VMEM_LIMIT = 24 * 1024 * 1024


def swapped(block, axis, distance):
    count = lax.axis_size(axis)
    route = []
    for low in range(count):
        high = low | 1 << distance
        if high != low and high < count:
            route += [(low, high), (high, low)]
    return lax.ppermute(block, axis, route)


def with_halo(block, sides, width, periodic):
    for axis, dim in sides:
        count = lax.axis_size(axis)
        forward = [(i, i + 1) for i in range(count - 1)]
        if periodic:
            forward.append((count - 1, 0))
        backward = [(target, source) for source, target in forward]
        low = lax.ppermute(
            lax.slice_in_dim(block, block.shape[dim] - width, None, axis=dim), axis, forward
        )
        high = lax.ppermute(lax.slice_in_dim(block, 0, width, axis=dim), axis, backward)
        block = jnp.concatenate([low, block, high], axis=dim)
    return block


def mode_tables(theta_index, total_theta, modes):
    column = jnp.arange(modes, dtype=jnp.int32)
    product = theta_index[:, None] * column[None, :] % total_theta
    angle = product.astype(jnp.float32) * (2.0 * jnp.pi / total_theta)
    cosine = jnp.cos(angle)
    sine = jnp.sin(angle)
    weight = jnp.where(column == 0, 1.0, 2.0).astype(jnp.float32) / total_theta
    forward = jnp.concatenate([cosine * weight[None, :], sine * (2.0 / total_theta)], axis=1)
    inverse = jnp.concatenate([cosine, sine], axis=1)
    return (forward, inverse)


def cycle_mask(cycles, modes):
    cycle_index = jnp.arange(cycles, dtype=jnp.int32)
    cutoff = jnp.minimum(355 * (2 * cycle_index + 1) // 226, modes - 1)
    column = jnp.arange(modes, dtype=jnp.int32)
    keep = (column[None, :] <= cutoff[:, None]).astype(jnp.float32)
    return jnp.concatenate([keep, keep], axis=1)


def operators(
    center, radial_plus, radial_minus, theta_plus, theta_minus, axial_plus, axial_minus, total_theta
):
    radius = jnp.arange(center.shape[-1], dtype=jnp.float32) + 0.5
    step_angle = 2.0 * jnp.pi / total_theta
    d_radial = (radial_plus - radial_minus) * 0.5
    d_theta = (theta_plus - theta_minus) / (2.0 * step_angle)
    d_axial = (axial_plus - axial_minus) * 0.5
    laplace = (
        radial_plus - 2.0 * center + radial_minus + (radial_plus - radial_minus) / (2.0 * radius)
    )
    laplace = laplace + (theta_plus - 2.0 * center + theta_minus) / (
        radius * radius * step_angle * step_angle
    )
    laplace = laplace + axial_plus - 2.0 * center + axial_minus
    return (d_radial, d_theta, d_axial, laplace)


def general_on_device(fields):
    count_fields, planes, theta_dev, radial = fields.shape
    sectors = lax.axis_size("az")
    total_theta = theta_dev * sectors
    modes = min(128, total_theta // 2)
    sector = lax.axis_index("az")
    own_index = sector * theta_dev + jnp.arange(theta_dev, dtype=jnp.int32)
    own_forward, own_inverse = mode_tables(own_index, total_theta, modes)
    inner_cycles = fields[:, :, :, :NEAR]
    kept = None
    piece = lax.all_gather(inner_cycles, "az", axis=2, tiled=True)
    piece_index = jnp.arange(piece.shape[2], dtype=jnp.int32)
    piece_forward, unused_inverse = mode_tables(piece_index, total_theta, modes)
    spectra = jnp.einsum("fztj,tc->fzjc", piece, piece_forward, precision=lax.Precision.HIGHEST)
    kept = spectra * cycle_mask(NEAR, modes)[None, None]
    smoothed = jnp.einsum("fzjc,tc->fztj", kept, own_inverse, precision=lax.Precision.HIGHEST)
    state = jnp.concatenate([smoothed, fields[:, :, :, NEAR:]], axis=3)
    flip = jnp.array([-1.0, -1.0, 1.0, 1.0, 1.0], dtype=jnp.float32)[:, None, None]
    top_bit = sectors.bit_length() - 1
    opposite = swapped(state[:, :, :, 0], "az", top_bit - 1)
    opposite = opposite * flip
    theta_padded = with_halo(state, (("az", 2),), 1, True)
    axial_padded = with_halo(state, (("ax", 1),), 1, False)
    radial_plus = jnp.concatenate([state[:, :, :, 1:], jnp.zeros_like(state[:, :, :, :1])], axis=3)
    radial_minus = jnp.concatenate([opposite[:, :, :, None], state[:, :, :, :-1]], axis=3)
    d_radial, d_theta, d_axial, laplace = operators(
        state,
        radial_plus,
        radial_minus,
        theta_padded[:, :, 2:, :],
        theta_padded[:, :, :-2, :],
        axial_padded[:, 2:, :, :],
        axial_padded[:, :-2, :, :],
        total_theta,
    )
    radius = jnp.arange(radial, dtype=jnp.float32) + 0.5
    radial_u = state[0]
    theta_u = state[1]
    axial_u = state[2]
    change = (
        -(radial_u[None] * d_radial + (theta_u / radius)[None] * d_theta + axial_u[None] * d_axial)
        + viscosity * laplace
    )
    inverse_square = 1.0 / (radius * radius)
    first = (
        change[0]
        + theta_u * theta_u / radius
        - viscosity * (radial_u * inverse_square + 2.0 * inverse_square * d_theta[1])
    )
    second = (
        change[1]
        - radial_u * theta_u / radius
        - viscosity * (theta_u * inverse_square - 2.0 * inverse_square * d_theta[0])
    )
    third = change[2] + buoyancy * state[3]
    change = jnp.concatenate([first[None], second[None], third[None], change[3:]], axis=0)
    return state + time_step * change


class Plan:
    def __init__(self, shape, sectors):
        self.fields, self.planes, self.theta, self.radial = shape
        self.sectors = sectors
        self.total = self.theta * sectors
        self.modes = min(128, self.total // 2)
        cycle = np.arange(NEAR)
        self.cut = np.minimum(355 * (2 * cycle + 1) // 226, self.modes - 1)
        self.full = int(np.sum(self.cut < self.modes - 1))
        self.rest = NEAR - self.full
        self.beside = LANES // max(self.full, 1)
        self.groups = -(-self.fields * self.planes // self.beside)
        self.early = tuple(range(sectors // 2 + 1))
        self.late = tuple(range(sectors // 2 + 1, sectors))
        self.depth = 256

    def place(self, f, k):
        index = k * self.fields + f
        return index // self.beside, index % self.beside * self.full

    @staticmethod
    def fits(shape, sectors, total):
        if sectors & (sectors - 1) or total // 2 > 128 or total != LANES or shape[2] != 16:
            return False
        plan = Plan(shape, sectors)
        return (
            plan.full > 0
            and plan.fields == 5
            and plan.planes == plan.theta
            and plan.rest * plan.fields <= LANES
            and plan.groups % 2 == 0
            and 3 * len(plan.early) * plan.theta <= plan.depth
            and plan.radial % LANES == 0
            and plan.radial > 2 * LANES
        )

    def split(self, table):
        high = table.astype(jnp.bfloat16)
        low = (table - high.astype(np.float32)).astype(jnp.bfloat16)
        return np.concatenate([high, high, low], axis=-1)

    def forward(self, pieces):
        theta = np.arange(self.total)
        mode = np.arange(self.modes)
        angle = (np.outer(mode, theta) % self.total) * (2.0 * np.pi / self.total)
        weight = np.where(mode == 0, 1.0, 2.0)[:, None] / self.total
        table = np.concatenate([np.cos(angle) * weight, np.sin(angle) * 2.0 / self.total], axis=0)
        table = table.astype(np.float32).reshape(2 * self.modes, self.sectors, self.theta)
        blocks = []
        for sector in range(self.sectors):
            chosen = np.concatenate([table[:, sector ^ p] for p in pieces], axis=1)
            chosen = self.split(chosen)
            pad = np.zeros((chosen.shape[0], self.depth - chosen.shape[1]), chosen.dtype)
            blocks.append(np.concatenate([chosen, pad], axis=1))
        return np.stack(blocks)

    def inverse(self):
        mode = np.arange(self.modes)
        blocks = []
        for sector in range(self.sectors):
            own = sector * self.theta + np.arange(self.theta)
            index = np.concatenate([own, own + self.total // 2, own[:1] - 1, own[-1:] + 1])
            angle = (np.outer(index, mode) % self.total) * (2.0 * np.pi / self.total)
            table = np.concatenate([np.cos(angle), np.sin(angle)], axis=1)
            pad = np.zeros((16 - 2, table.shape[1]))
            blocks.append(np.concatenate([table, pad], axis=0))
        return self.split(np.stack(blocks).astype(np.float32))

    def mask(self):
        mode = np.arange(self.modes)
        keep = np.zeros((self.modes, LANES), np.float32)
        for i in range(self.beside):
            keep[:, i * self.full : (i + 1) * self.full] = (
                mode[:, None] <= self.cut[None, : self.full]
            )
        return np.concatenate([keep, keep], axis=0)

    def coefficients(self):
        radius = np.arange(self.radial) + 0.5
        step = 2.0 * np.pi / self.total
        nu_dt = viscosity * time_step
        square = 1.0 / (radius * radius * step * step)
        rows = [
            1.0 - nu_dt * (4.0 + 2.0 * square),
            nu_dt * square,
            nu_dt / (2.0 * radius),
            time_step / (2.0 * step * radius),
            time_step / radius,
            nu_dt / (radius * radius),
            nu_dt / (step * radius * radius),
        ]
        rows.append(np.zeros(self.radial))
        return np.stack(rows).astype(np.float32)


def moved(x, lanes):
    return x if lanes % LANES == 0 else pltpu.roll(x, lanes % LANES, 1)


def pack_kernel(plan, x_ref, out_ref, buf, sems):
    shape = (plan.theta, LANES)
    lane = lax.broadcasted_iota(jnp.int32, shape, 1)
    row = lax.broadcasted_iota(jnp.int32, shape, 0)
    sign = (1 - 2 * (row & 1)).astype(jnp.float32)
    chunk = 4
    copies = [
        pltpu.make_async_copy(
            x_ref.at[:, pl.ds(i * chunk, chunk), :, pl.ds(0, LANES)], buf.at[i], sems.at[i]
        )
        for i in range(plan.planes // chunk)
    ]
    for copy in copies:
        copy.start()
    group = jnp.zeros(shape, jnp.float32)
    sums = [jnp.zeros(shape, jnp.float32) for _ in range(plan.fields)]
    for k in range(plan.planes):
        if k % chunk == 0:
            copies[k // chunk].wait()
        for f in range(plan.fields):
            x = buf[k // chunk, f, k % chunk]
            number, first = plan.place(f, k)
            part = moved(x, first)
            if first:
                part = jnp.where((lane >= first) & (lane < first + plan.full), part, group)
            group = part
            if first // plan.full == plan.beside - 1 or (f, k) == (plan.fields - 1, plan.planes - 1):
                out_ref[number] = group
            alternating = jnp.sum(x * sign, axis=0, keepdims=True)
            sums[f] = jnp.where(row == k, alternating, sums[f])
    last = sums[0]
    for f in range(plan.fields):
        start = f * plan.rest
        last = jnp.where(lane >= start, moved(sums[f], start - plan.full), last)
    out_ref[plan.groups] = last


def pack(plan, fields):
    f32 = jnp.float32
    chunks = plan.planes // 4
    return pl.pallas_call(
        functools.partial(pack_kernel, plan),
        in_specs=[pl.BlockSpec(memory_space=pl.ANY)],
        out_specs=pl.BlockSpec(memory_space=pltpu.VMEM),
        out_shape=jax.ShapeDtypeStruct((plan.groups + 1, plan.theta, LANES), f32),
        scratch_shapes=[
            pltpu.VMEM((chunks, plan.fields, 4, plan.theta, LANES), f32),
            pltpu.SemaphoreType.DMA((chunks,)),
        ],
        name="pack",
        cost_estimate=pl.CostEstimate(flops=1000000, bytes_accessed=800000, transcendentals=0),
    )(fields)


def pick_columns(plan, x_ref, keep_high, ref, base):
    last = plan.theta - 1
    tiles = plan.radial // LANES
    for f in range(plan.fields):
        for k in range(plan.planes):
            for tile in range(tiles):
                here = slice(tile * LANES, (tile + 1) * LANES)
                low = x_ref[f, k, 0:1, here]
                high = x_ref[f, k, last : last + 1, here]
                ref[base + f * tiles + tile, k : k + 1, :] = jnp.where(keep_high, high, low)


def edges_kernel(plan, x_ref, after_ref, az_a, az_b):
    del after_ref
    even_theta = lax.axis_index("az") % 2 == 0
    pick_columns(plan, x_ref, even_theta, az_a, 0)
    pick_columns(plan, x_ref, jnp.logical_not(even_theta), az_b, 0)


def edges(plan, fields, after):
    f32 = jnp.float32
    columns = plan.fields * plan.radial // LANES
    inside = pl.BlockSpec(memory_space=pltpu.VMEM)
    return pl.pallas_call(
        functools.partial(edges_kernel, plan),
        in_specs=[inside] * 2,
        out_specs=[inside] * 2,
        out_shape=[jax.ShapeDtypeStruct((columns, plan.theta, LANES), f32)] * 2,
        compiler_params=pltpu.CompilerParams(vmem_limit_bytes=VMEM_LIMIT),
        name="edges",
        cost_estimate=pl.CostEstimate(flops=0, bytes_accessed=1000000, transcendentals=0),
    )(fields, after)


def advance(coef, q, jp, jm, tp, tm, kp, km):
    c0, c2, half, angular, over, square, cross = coef
    ur, ut, uz, temp = q[:4]
    radial = half - (0.5 * time_step) * ur
    azimuthal = angular * ut
    axial = (0.5 * time_step) * uz
    nu_dt = viscosity * time_step
    out = []
    d_theta = []
    for f in range(5):
        dt = tp[f] - tm[f]
        if f < 2:
            d_theta.append(dt)
        value = c0 * q[f] + nu_dt * ((jp[f] + jm[f]) + (kp[f] + km[f]))
        value = value + c2 * (tp[f] + tm[f])
        value = value + (jp[f] - jm[f]) * radial
        value = value - dt * azimuthal
        value = value - (kp[f] - km[f]) * axial
        out.append(value)
    swirl = over * ut
    out[0] = out[0] + swirl * ut - square * ur - cross * d_theta[1]
    out[1] = out[1] - swirl * ur - square * ut + cross * d_theta[0]
    out[2] = out[2] + (time_step * buoyancy) * temp
    return out


def turned(x, row, before, after):
    last = x.shape[0] - 1
    up = jnp.where(row == last, after, pltpu.roll(x, last, 0))
    down = jnp.where(row == 0, before, pltpu.roll(x, 1, 0))
    return up, down


def choose_halos(plan, tiles, az_a, az_b, ax_a, ax_b, side, ends):
    even_theta = lax.axis_index("az") % 2 == 0
    even_plane = lax.axis_index("ax") % 2 == 0
    all_tiles = plan.radial // LANES
    for f in range(plan.fields):
        for tile in tiles:
            here = slice(tile * LANES, (tile + 1) * LANES)
            number = f * all_tiles + tile
            a = az_a[plan.groups + 1 + number]
            b = az_b[number]
            side[0, number] = jnp.where(even_theta, b, a)
            side[1, number] = jnp.where(even_theta, a, b)
            a = ax_a[f, :, here]
            b = ax_b[f, :, here]
            ends[0, f, :, here] = jnp.where(even_plane, b, a)
            ends[1, f, :, here] = jnp.where(even_plane, a, b)


def outer_kernel(plan, coef_ref, x_ref, done, token):
    planes = plan.planes
    tiles = plan.radial // LANES
    token[...] = jnp.zeros_like(token)
    shape = (plan.theta, LANES)
    lane = lax.broadcasted_iota(jnp.int32, shape, 1)
    row = lax.broadcasted_iota(jnp.int32, shape, 0)

    def step(group, carry):
        start = pl.multiple_of(group * 4, 4)
        for i in range(4):
            k = start + i
            for tile in range(1, tiles):
                here = pl.ds(tile * LANES, LANES)
                coef = [coef_ref[j : j + 1, here] for j in range(7)]
                q, jp, jm, tp, tm, kp, km = ([] for _ in range(7))
                for f in range(plan.fields):
                    x = x_ref[f, k, :, here]
                    low = x_ref[f, k, :, pl.ds((tile - 1) * LANES, LANES)]
                    q.append(x)
                    high = 0.0
                    if tile + 1 < tiles:
                        high = x_ref[f, k, :, pl.ds((tile + 1) * LANES, LANES)]
                        high = pltpu.roll(high, LANES - 1, 1)
                    jp.append(jnp.where(lane == LANES - 1, high, pltpu.roll(x, LANES - 1, 1)))
                    jm.append(jnp.where(lane == 0, pltpu.roll(low, 1, 1), pltpu.roll(x, 1, 1)))
                    up, down = turned(x, row, 0.0, 0.0)
                    tp.append(up)
                    tm.append(down)
                    if i < 3:
                        above = x_ref[f, k + 1, :, here]
                    else:
                        above = x_ref[f, jnp.minimum(k + 1, planes - 1), :, here]
                        above = jnp.where(k == planes - 1, 0.0, above)
                    if i > 0:
                        below = x_ref[f, k - 1, :, here]
                    else:
                        below = x_ref[f, jnp.maximum(k - 1, 0), :, here]
                        below = jnp.where(k == 0, 0.0, below)
                    kp.append(above)
                    km.append(below)
                result = advance(coef, q, jp, jm, tp, tm, kp, km)
                for f in range(plan.fields):
                    done[k, f, :, pl.ds((tile - 1) * LANES, LANES)] = result[f]
        return carry

    lax.fori_loop(0, planes // 4, step, 0)


def outer(plan, coef, fields):
    inside = pl.BlockSpec(memory_space=pltpu.VMEM)
    f32 = jnp.float32
    return pl.pallas_call(
        functools.partial(outer_kernel, plan),
        in_specs=[inside] * 2,
        out_specs=[inside] * 2,
        out_shape=[
            jax.ShapeDtypeStruct((plan.planes, plan.fields, plan.theta, plan.radial - LANES), f32),
            jax.ShapeDtypeStruct((8, LANES), f32),
        ],
        compiler_params=pltpu.CompilerParams(vmem_limit_bytes=VMEM_LIMIT),
        name="outer",
        cost_estimate=pl.CostEstimate(flops=16000000, bytes_accessed=5000000, transcendentals=0),
    )(coef, fields)


def seams_kernel(plan, coef_ref, own_a, own_b, az_a, az_b, part_ref, out_ref, done, outs):
    del part_ref
    planes = plan.planes
    tiles = plan.radial // LANES
    even_theta = lax.axis_index("az") % 2 == 0
    last = plan.theta - 1

    def store(k):
        return pltpu.make_async_copy(
            done.at[k], out_ref.at[:, k, :, pl.ds(LANES, plan.radial - LANES)], outs.at[k]
        )

    for tile in range(1, tiles):
        here = slice(tile * LANES, (tile + 1) * LANES)
        there = slice((tile - 1) * LANES, tile * LANES)
        c2 = coef_ref[1:2, here]
        angular = coef_ref[3:4, here]
        cross = coef_ref[6:7, here]
        number = tiles + tile
        mine_a = own_a[number]
        mine_b = own_b[number]
        turn_low = angular * jnp.where(even_theta, mine_b, mine_a)
        turn_high = angular * jnp.where(even_theta, mine_a, mine_b)
        before = []
        after = []
        for f in range(plan.fields):
            a = az_a[f * tiles + tile]
            b = az_b[f * tiles + tile]
            before.append(jnp.where(even_theta, b, a))
            after.append(jnp.where(even_theta, a, b))
        for f in range(plan.fields):
            low = (c2 + turn_low) * before[f]
            high = (c2 - turn_high) * after[f]
            if f == 0:
                low = low + cross * before[1]
                high = high - cross * after[1]
            if f == 1:
                low = low - cross * before[0]
                high = high + cross * after[0]
            for k in range(planes):
                done[k, f, 0:1, there] += low[k : k + 1]
                done[k, f, last : last + 1, there] += high[k : k + 1]
    for k in range(1, planes - 1):
        store(k).start()
    for k in range(1, planes - 1):
        store(k).wait()


def seams(plan, coef, fields, own, sides, part):
    inside = pl.BlockSpec(memory_space=pltpu.VMEM)
    return pl.pallas_call(
        functools.partial(seams_kernel, plan),
        in_specs=[inside] * 6,
        out_specs=[pl.BlockSpec(memory_space=pl.ANY), inside],
        out_shape=[
            jax.ShapeDtypeStruct(fields.shape, jnp.float32),
            jax.ShapeDtypeStruct(part.shape, jnp.float32),
        ],
        input_output_aliases={5: 1},
        scratch_shapes=[pltpu.SemaphoreType.DMA((plan.planes,))],
        compiler_params=pltpu.CompilerParams(vmem_limit_bytes=VMEM_LIMIT),
        name="seams",
        cost_estimate=pl.CostEstimate(flops=1000000, bytes_accessed=4000000, transcendentals=0),
    )(coef, *own, *sides, part)


def halves(x, depth=None):
    high = x.astype(jnp.bfloat16)
    low = (x - high.astype(jnp.float32)).astype(jnp.bfloat16)
    parts = [high, low, high]
    if depth is not None:
        parts.append(jnp.zeros((depth - 3 * x.shape[0], x.shape[1]), jnp.bfloat16))
    return jnp.concatenate(parts, axis=0)


def two_groups(pieces, g):
    return jnp.concatenate(
        [jnp.concatenate([piece[g + i] for piece in pieces], axis=0) for i in range(2)], axis=1
    )


def early_kernel(plan, forward_ref, *refs):
    pieces = refs[: len(plan.early)]
    spectra_ref, total_ref = refs[len(plan.early) :]
    table = forward_ref[lax.axis_index("az")]
    for g in range(0, plan.groups, 2):
        both = halves(two_groups(pieces, g), plan.depth)
        spectra_ref[g // 2] = jnp.dot(table, both, preferred_element_type=jnp.float32)
    total = pieces[0][plan.groups]
    for piece in pieces[1:]:
        total = total + piece[plan.groups]
    total_ref[...] = total


def early_spectra(plan, pieces):
    inside = pl.BlockSpec(memory_space=pltpu.VMEM)
    f32 = jnp.float32
    return pl.pallas_call(
        functools.partial(early_kernel, plan),
        in_specs=[inside] * (1 + len(pieces)),
        out_specs=[inside] * 2,
        out_shape=[
            jax.ShapeDtypeStruct((plan.groups // 2, 2 * plan.modes, 2 * LANES), f32),
            jax.ShapeDtypeStruct((plan.theta, LANES), f32),
        ],
        compiler_params=pltpu.CompilerParams(vmem_limit_bytes=VMEM_LIMIT),
        name="early",
        cost_estimate=pl.CostEstimate(flops=200000000, bytes_accessed=1500000, transcendentals=0),
    )(jnp.asarray(plan.forward(plan.early)), *pieces)


def filter_kernel(plan, token_ref, x_ref, forward_ref, inverse_ref, mask_ref, early_ref, early_total, *refs):
    del token_ref
    count = len(plan.late)
    pieces = refs[:count]
    own_ref, across_ref, edge_ref, sums_ref, message_a, message_b = refs[count:]
    odd_plane = lax.axis_index("ax") % 2
    theta = plan.theta
    sector = lax.axis_index("az")
    forward = forward_ref[sector]
    table = inverse_ref[sector]
    mask = mask_ref[...]
    mask = jnp.concatenate([mask, mask], axis=1)

    for g in range(0, plan.groups, 2):
        both = halves(two_groups(pieces, g), plan.depth)
        spectra = early_ref[g // 2] + jnp.dot(forward, both, preferred_element_type=jnp.float32)
        kept = halves(spectra * mask)
        state = jnp.dot(table, kept, preferred_element_type=jnp.float32)
        for i in range(2):
            lanes = slice(i * LANES, (i + 1) * LANES)
            own_ref[g + i] = state[:theta, lanes]
            across_ref[g + i] = state[theta : 2 * theta, lanes]
            edge_ref[g + i] = state[2 * theta : 2 * theta + 8, lanes]

    total = early_total[...]
    for piece in pieces:
        total = total + piece[plan.groups]
    total = total * (1.0 / plan.total)
    lane = lax.broadcasted_iota(jnp.int32, (plan.planes, LANES), 1)
    for f in range(plan.fields):
        value = moved(total, plan.full - f * plan.rest)
        sums_ref[f] = jnp.where((lane >= plan.full) & (lane < NEAR), value, 0.0)

    row = lax.broadcasted_iota(jnp.int32, (theta, LANES), 0)
    sign = (1 - 2 * (row & 1)).astype(jnp.float32)

    def message(ref, k):
        for f in range(plan.fields):
            number, first = plan.place(f, k)
            raw = x_ref[f, k, :, :LANES] - sign * sums_ref[f, k : k + 1]
            ref[f, :, :LANES] = jnp.where(lane < plan.full, moved(own_ref[number], -first), raw)
            ref[f, :, LANES:] = x_ref[f, k, :, LANES:]

    def both_messages(ref_low, ref_high):
        message(ref_low, 0)
        message(ref_high, plan.planes - 1)

    pl.when(odd_plane == 1)(lambda: both_messages(message_a, message_b))
    pl.when(odd_plane == 0)(lambda: both_messages(message_b, message_a))


def filtered(plan, token, fields, pieces, early):
    inside = pl.BlockSpec(memory_space=pltpu.VMEM)
    f32 = jnp.float32
    cube = jax.ShapeDtypeStruct((plan.groups, plan.theta, LANES), f32)
    plane = jax.ShapeDtypeStruct((plan.fields, plan.theta, plan.radial), f32)
    return pl.pallas_call(
        functools.partial(filter_kernel, plan),
        in_specs=[inside] * (7 + len(pieces)),
        out_specs=[inside] * 6,
        out_shape=[
            cube,
            cube,
            jax.ShapeDtypeStruct((plan.groups, 8, LANES), f32),
            jax.ShapeDtypeStruct((plan.fields, plan.planes, LANES), f32),
            plane,
            plane,
        ],
        compiler_params=pltpu.CompilerParams(vmem_limit_bytes=VMEM_LIMIT),
        name="filter",
        cost_estimate=pl.CostEstimate(flops=200000000, bytes_accessed=1500000, transcendentals=0),
    )(
        token,
        fields,
        jnp.asarray(plan.forward(plan.late)),
        jnp.asarray(plan.inverse()),
        jnp.asarray(plan.mask()),
        *early,
        *pieces,
    )


def inner_kernel(
    plan, coef_ref, own_ref, across_ref, edge_ref, sums_ref, x_ref, az_a, az_b, done, state
):
    planes = plan.planes
    theta = plan.theta
    tiles = plan.radial // LANES
    shape = (theta, LANES)
    lane = lax.broadcasted_iota(jnp.int32, shape, 1)
    row = lax.broadcasted_iota(jnp.int32, shape, 0)
    sign = (1 - 2 * (row & 1)).astype(jnp.float32)
    lane1 = lax.broadcasted_iota(jnp.int32, (1, LANES), 1)
    first = slice(0, LANES)
    coef = [coef_ref[i : i + 1, first] for i in range(7)]
    flips = (-1.0, -1.0, 1.0, 1.0, 1.0)
    even_theta = lax.axis_index("az") % 2 == 0

    for k in range(planes):
        for f in range(plan.fields):
            number, start = plan.place(f, k)
            state[k, f] = jnp.where(
                lane < plan.full,
                moved(own_ref[number], -start),
                x_ref[f, k, :, first] - sign * sums_ref[f, k : k + 1],
            )

    befores = []
    afters = []
    for f in range(plan.fields):
        a = az_a[f * tiles]
        b = az_b[f * tiles]
        befores.append(jnp.where(even_theta, b, a) + sums_ref[f])
        afters.append(jnp.where(even_theta, a, b) - sums_ref[f])

    zero = jnp.zeros(shape, jnp.float32)
    for k in range(planes):
        q, jp, jm, tp, tm, kp, km = ([] for _ in range(7))
        for f in range(plan.fields):
            number, start = plan.place(f, k)
            x = state[k, f]
            q.append(x)
            high_part = pltpu.roll(x_ref[f, k, :, LANES : 2 * LANES], LANES - 1, 1)
            jp.append(jnp.where(lane == LANES - 1, high_part, pltpu.roll(x, LANES - 1, 1)))
            opposite = flips[f] * moved(across_ref[number], -start)
            jm.append(jnp.where(lane == 0, opposite, pltpu.roll(x, 1, 1)))
            sides = moved(edge_ref[number], -start)
            before = jnp.where(lane1 < plan.full, sides[0:1], befores[f][k : k + 1])
            after = jnp.where(lane1 < plan.full, sides[1:2], afters[f][k : k + 1])
            up, down = turned(x, row, before, after)
            tp.append(up)
            tm.append(down)
            kp.append(state[k + 1, f] if k + 1 < planes else zero)
            km.append(state[k - 1, f] if k > 0 else zero)
        result = advance(coef, q, jp, jm, tp, tm, kp, km)
        for f in range(plan.fields):
            done[k, f] = result[f]


def inner(plan, coef, parts, fields, sides):
    inside = pl.BlockSpec(memory_space=pltpu.VMEM)
    f32 = jnp.float32
    return pl.pallas_call(
        functools.partial(inner_kernel, plan),
        in_specs=[inside] * 8,
        out_specs=inside,
        out_shape=jax.ShapeDtypeStruct((plan.planes, plan.fields, plan.theta, LANES), f32),
        scratch_shapes=[pltpu.VMEM((plan.planes, plan.fields, plan.theta, LANES), f32)],
        compiler_params=pltpu.CompilerParams(vmem_limit_bytes=VMEM_LIMIT),
        name="inner",
        cost_estimate=pl.CostEstimate(flops=6000000, bytes_accessed=2500000, transcendentals=0),
    )(coef, *parts, fields, *sides)


def finish_kernel(plan, near_ref, part_ref, own_a, own_b, ax_a, ax_b, other_ref, out_ref, ends, sems):
    del other_ref
    planes = plan.planes
    copies = [
        pltpu.make_async_copy(near_ref.at[k], out_ref.at[:, k, :, pl.ds(0, LANES)], sems.at[k])
        for k in range(1, planes - 1)
    ]
    for copy in copies:
        copy.start()
    even_plane = lax.axis_index("ax") % 2 == 0
    nu_dt = viscosity * time_step
    half = 0.5 * time_step
    tiles = plan.radial // LANES
    for end, k in ((0, 0), (1, planes - 1)):
        for tile in range(tiles):
            here = slice(tile * LANES, (tile + 1) * LANES)
            sent_a = own_a[2, :, here]
            sent_b = own_b[2, :, here]
            if end == 0:
                factor = nu_dt + half * jnp.where(even_plane, sent_b, sent_a)
            else:
                factor = nu_dt - half * jnp.where(even_plane, sent_a, sent_b)
            for f in range(plan.fields):
                a = ax_a[f, :, here]
                b = ax_b[f, :, here]
                value = jnp.where(even_plane, b, a) if end == 0 else jnp.where(even_plane, a, b)
                if tile == 0:
                    start = near_ref[k, f]
                else:
                    start = part_ref[k, f, :, (tile - 1) * LANES : tile * LANES]
                ends[end, f, :, here] = start + factor * value
        copies.append(pltpu.make_async_copy(ends.at[end], out_ref.at[:, k], sems.at[k]))
        copies[-1].start()
    for copy in copies:
        copy.wait()


def finish(plan, near, part, sent, messages, partial):
    anywhere = pl.BlockSpec(memory_space=pl.ANY)
    inside = pl.BlockSpec(memory_space=pltpu.VMEM)
    return pl.pallas_call(
        functools.partial(finish_kernel, plan),
        in_specs=[inside] * 6 + [anywhere],
        out_specs=anywhere,
        out_shape=jax.ShapeDtypeStruct(partial.shape, jnp.float32),
        input_output_aliases={6: 0},
        scratch_shapes=[
            pltpu.VMEM((2, plan.fields, plan.theta, plan.radial), jnp.float32),
            pltpu.SemaphoreType.DMA((plan.planes,)),
        ],
        compiler_params=pltpu.CompilerParams(vmem_limit_bytes=VMEM_LIMIT),
        name="finish",
        cost_estimate=pl.CostEstimate(flops=100000, bytes_accessed=1500000, transcendentals=0),
    )(near, part, *sent, *messages, partial)


def pairs(count, start, periodic):
    route = []
    for low in range(start, count, 2):
        high = low + 1
        if high == count and not periodic:
            continue
        route += [(low, high % count), (high % count, low)]
    return route


def fast_on_device(fields):
    sectors = lax.axis_size("az")
    slabs = lax.axis_size("ax")
    plan = Plan(fields.shape, sectors)
    coef = jnp.asarray(plan.coefficients())

    def send(x, distance):
        return lax.ppermute(x, "az", [(i, i ^ distance) for i in range(sectors)])

    packed = pack(plan, fields)
    half = sectors // 2
    pieces = [None] * sectors
    pieces[0] = packed
    far = send(packed, half)
    pieces[half] = far
    for p in range(half - 1, 0, -1):
        pieces[p] = send(packed, p)
    for p in range(half - 1, 0, -1):
        pieces[half + p] = send(far, p)
    early = early_spectra(plan, pieces[: half + 1])
    column_a, column_b = edges(plan, fields, early[1])
    sides = (
        lax.ppermute(column_a, "az", pairs(sectors, 0, True)),
        lax.ppermute(column_b, "az", pairs(sectors, 1, True)),
    )
    part, token = outer(plan, coef, fields)
    *parts, message_a, message_b = filtered(plan, token, fields, pieces[half + 1 :], early)
    messages = (
        lax.ppermute(message_a, "ax", pairs(slabs, 0, False)),
        lax.ppermute(message_b, "ax", pairs(slabs, 1, False)),
    )
    partial, part = seams(plan, coef, fields, (column_a, column_b), sides, part)
    near = inner(plan, coef, parts, fields, sides)
    return finish(plan, near, part, (message_a, message_b), messages, partial)


def on_device(fields):
    total_theta = fields.shape[2] * lax.axis_size("az")
    if Plan.fits(fields.shape, lax.axis_size("az"), total_theta):
        return fast_on_device(fields)
    return general_on_device(fields)


def solution(mesh):
    placed = (P(None, "ax", "az", None),)
    return jax.shard_map(
        on_device, mesh=mesh, in_specs=placed, out_specs=P(None, "ax", "az", None), check_vma=False
    )
```

```python
import functools

import jax
import jax.numpy as jnp
import numpy as np
from jax import lax
from jax.experimental import pallas as pl
from jax.experimental.pallas import tpu as pltpu
from jax.sharding import PartitionSpec as P

NEAR = 40


viscosity = 0.2
time_step = 0.1
buoyancy = 1.0

LANES = 128
VMEM_LIMIT = 16 * 1024 * 1024


def swapped(block, axis, distance):
    count = lax.axis_size(axis)
    route = []
    for low in range(count):
        high = low | 1 << distance
        if high != low and high < count:
            route += [(low, high), (high, low)]
    return lax.ppermute(block, axis, route)


def with_halo(block, sides, width, periodic):
    for axis, dim in sides:
        count = lax.axis_size(axis)
        forward = [(i, i + 1) for i in range(count - 1)]
        if periodic:
            forward.append((count - 1, 0))
        backward = [(target, source) for source, target in forward]
        low = lax.ppermute(
            lax.slice_in_dim(block, block.shape[dim] - width, None, axis=dim), axis, forward
        )
        high = lax.ppermute(lax.slice_in_dim(block, 0, width, axis=dim), axis, backward)
        block = jnp.concatenate([low, block, high], axis=dim)
    return block


def mode_tables(theta_index, total_theta, modes):
    column = jnp.arange(modes, dtype=jnp.int32)
    product = theta_index[:, None] * column[None, :] % total_theta
    angle = product.astype(jnp.float32) * (2.0 * jnp.pi / total_theta)
    cosine = jnp.cos(angle)
    sine = jnp.sin(angle)
    weight = jnp.where(column == 0, 1.0, 2.0).astype(jnp.float32) / total_theta
    forward = jnp.concatenate([cosine * weight[None, :], sine * (2.0 / total_theta)], axis=1)
    inverse = jnp.concatenate([cosine, sine], axis=1)
    return (forward, inverse)


def cycle_mask(cycles, modes):
    cycle_index = jnp.arange(cycles, dtype=jnp.int32)
    cutoff = jnp.minimum(355 * (2 * cycle_index + 1) // 226, modes - 1)
    column = jnp.arange(modes, dtype=jnp.int32)
    keep = (column[None, :] <= cutoff[:, None]).astype(jnp.float32)
    return jnp.concatenate([keep, keep], axis=1)


def operators(
    center, radial_plus, radial_minus, theta_plus, theta_minus, axial_plus, axial_minus, total_theta
):
    radius = jnp.arange(center.shape[-1], dtype=jnp.float32) + 0.5
    step_angle = 2.0 * jnp.pi / total_theta
    d_radial = (radial_plus - radial_minus) * 0.5
    d_theta = (theta_plus - theta_minus) / (2.0 * step_angle)
    d_axial = (axial_plus - axial_minus) * 0.5
    laplace = (
        radial_plus - 2.0 * center + radial_minus + (radial_plus - radial_minus) / (2.0 * radius)
    )
    laplace = laplace + (theta_plus - 2.0 * center + theta_minus) / (
        radius * radius * step_angle * step_angle
    )
    laplace = laplace + axial_plus - 2.0 * center + axial_minus
    return (d_radial, d_theta, d_axial, laplace)


def general_on_device(fields):
    count_fields, planes, theta_dev, radial = fields.shape
    sectors = lax.axis_size("az")
    total_theta = theta_dev * sectors
    modes = min(128, total_theta // 2)
    sector = lax.axis_index("az")
    own_index = sector * theta_dev + jnp.arange(theta_dev, dtype=jnp.int32)
    own_forward, own_inverse = mode_tables(own_index, total_theta, modes)
    inner_cycles = fields[:, :, :, :NEAR]
    kept = None
    piece = lax.all_gather(inner_cycles, "az", axis=2, tiled=True)
    piece_index = jnp.arange(piece.shape[2], dtype=jnp.int32)
    piece_forward, unused_inverse = mode_tables(piece_index, total_theta, modes)
    spectra = jnp.einsum("fztj,tc->fzjc", piece, piece_forward, precision=lax.Precision.HIGHEST)
    kept = spectra * cycle_mask(NEAR, modes)[None, None]
    smoothed = jnp.einsum("fzjc,tc->fztj", kept, own_inverse, precision=lax.Precision.HIGHEST)
    state = jnp.concatenate([smoothed, fields[:, :, :, NEAR:]], axis=3)
    flip = jnp.array([-1.0, -1.0, 1.0, 1.0, 1.0], dtype=jnp.float32)[:, None, None]
    top_bit = sectors.bit_length() - 1
    opposite = swapped(state[:, :, :, 0], "az", top_bit - 1)
    opposite = opposite * flip
    theta_padded = with_halo(state, (("az", 2),), 1, True)
    axial_padded = with_halo(state, (("ax", 1),), 1, False)
    radial_plus = jnp.concatenate([state[:, :, :, 1:], jnp.zeros_like(state[:, :, :, :1])], axis=3)
    radial_minus = jnp.concatenate([opposite[:, :, :, None], state[:, :, :, :-1]], axis=3)
    d_radial, d_theta, d_axial, laplace = operators(
        state,
        radial_plus,
        radial_minus,
        theta_padded[:, :, 2:, :],
        theta_padded[:, :, :-2, :],
        axial_padded[:, 2:, :, :],
        axial_padded[:, :-2, :, :],
        total_theta,
    )
    radius = jnp.arange(radial, dtype=jnp.float32) + 0.5
    radial_u = state[0]
    theta_u = state[1]
    axial_u = state[2]
    change = (
        -(radial_u[None] * d_radial + (theta_u / radius)[None] * d_theta + axial_u[None] * d_axial)
        + viscosity * laplace
    )
    inverse_square = 1.0 / (radius * radius)
    first = (
        change[0]
        + theta_u * theta_u / radius
        - viscosity * (radial_u * inverse_square + 2.0 * inverse_square * d_theta[1])
    )
    second = (
        change[1]
        - radial_u * theta_u / radius
        - viscosity * (theta_u * inverse_square - 2.0 * inverse_square * d_theta[0])
    )
    third = change[2] + buoyancy * state[3]
    change = jnp.concatenate([first[None], second[None], third[None], change[3:]], axis=0)
    return state + time_step * change


class Plan:
    def __init__(self, shape, sectors):
        self.fields, self.planes, self.theta, self.radial = shape
        self.sectors = sectors
        self.total = self.theta * sectors
        self.modes = min(128, self.total // 2)
        cycle = np.arange(NEAR)
        self.cut = np.minimum(355 * (2 * cycle + 1) // 226, self.modes - 1)
        self.full = int(np.sum(self.cut < self.modes - 1))
        self.rest = NEAR - self.full
        self.beside = LANES // max(self.full, 1)
        self.groups = -(-self.fields * self.planes // self.beside)
        self.early = tuple(range(sectors // 2 + 1))
        self.late = tuple(range(sectors // 2 + 1, sectors))
        self.depth = 256

    def place(self, f, k):
        index = k * self.fields + f
        return index // self.beside, index % self.beside * self.full

    @staticmethod
    def fits(shape, sectors, slabs, total):
        if sectors & (sectors - 1) or total // 2 > 128 or total != LANES or shape[2] != 16:
            return False
        plan = Plan(shape, sectors)
        return (
            plan.full > 0
            and plan.fields == 5
            and plan.planes == plan.theta
            and plan.rest * plan.fields <= LANES
            and plan.groups % 2 == 0
            and slabs % 2 == 0
            and 3 * len(plan.early) * plan.theta <= plan.depth
            and plan.radial % LANES == 0
            and plan.radial > 2 * LANES
        )

    def split(self, table):
        high = table.astype(jnp.bfloat16)
        low = (table - high.astype(np.float32)).astype(jnp.bfloat16)
        return np.concatenate([high, high, low], axis=-1)

    def forward(self, pieces):
        theta = np.arange(self.total)
        mode = np.arange(self.modes)
        angle = (np.outer(mode, theta) % self.total) * (2.0 * np.pi / self.total)
        weight = np.where(mode == 0, 1.0, 2.0)[:, None] / self.total
        table = np.concatenate([np.cos(angle) * weight, np.sin(angle) * 2.0 / self.total], axis=0)
        table = table.astype(np.float32).reshape(2 * self.modes, self.sectors, self.theta)
        blocks = []
        for sector in range(self.sectors):
            chosen = np.concatenate([table[:, sector ^ p] for p in pieces], axis=1)
            chosen = self.split(chosen)
            pad = np.zeros((chosen.shape[0], self.depth - chosen.shape[1]), chosen.dtype)
            blocks.append(np.concatenate([chosen, pad], axis=1))
        return np.stack(blocks)

    def inverse(self):
        mode = np.arange(self.modes)
        blocks = []
        for sector in range(self.sectors):
            own = sector * self.theta + np.arange(self.theta)
            index = np.concatenate([own, own + self.total // 2, own[:1] - 1, own[-1:] + 1])
            angle = (np.outer(index, mode) % self.total) * (2.0 * np.pi / self.total)
            table = np.concatenate([np.cos(angle), np.sin(angle)], axis=1)
            pad = np.zeros((16 - 2, table.shape[1]))
            blocks.append(np.concatenate([table, pad], axis=0))
        return self.split(np.stack(blocks).astype(np.float32))

    def mask(self):
        mode = np.arange(self.modes)
        keep = np.zeros((self.modes, LANES), np.float32)
        for i in range(self.beside):
            keep[:, i * self.full : (i + 1) * self.full] = (
                mode[:, None] <= self.cut[None, : self.full]
            )
        return np.concatenate([keep, keep], axis=0)

    def coefficients(self):
        radius = np.arange(self.radial) + 0.5
        step = 2.0 * np.pi / self.total
        nu_dt = viscosity * time_step
        square = 1.0 / (radius * radius * step * step)
        rows = [
            1.0 - nu_dt * (4.0 + 2.0 * square),
            nu_dt * square,
            nu_dt / (2.0 * radius),
            time_step / (2.0 * step * radius),
            time_step / radius,
            nu_dt / (radius * radius),
            nu_dt / (step * radius * radius),
        ]
        rows.append(np.zeros(self.radial))
        return np.stack(rows).astype(np.float32)


def moved(x, lanes):
    return x if lanes % LANES == 0 else pltpu.roll(x, lanes % LANES, 1)


def pick_columns(plan, x_ref, keep_high, ref, base):
    last = plan.theta - 1
    tiles = plan.radial // LANES
    for f in range(plan.fields):
        for k in range(plan.planes):
            for tile in range(tiles):
                here = slice(tile * LANES, (tile + 1) * LANES)
                low = x_ref[f, k, 0:1, here]
                high = x_ref[f, k, last : last + 1, here]
                ref[base + f * tiles + tile, k : k + 1, :] = jnp.where(keep_high, high, low)


def pack_kernel(plan, x_ref, out_ref, wide_ref):
    shape = (plan.theta, LANES)
    lane = lax.broadcasted_iota(jnp.int32, shape, 1)
    row = lax.broadcasted_iota(jnp.int32, shape, 0)
    sign = (1 - 2 * (row & 1)).astype(jnp.float32)
    group = jnp.zeros(shape, jnp.float32)
    sums = [jnp.zeros(shape, jnp.float32) for _ in range(plan.fields)]
    for k in range(plan.planes):
        for f in range(plan.fields):
            x = x_ref[f, k, :, :LANES]
            number, first = plan.place(f, k)
            part = moved(x, first)
            if first:
                part = jnp.where((lane >= first) & (lane < first + plan.full), part, group)
            group = part
            if first // plan.full == plan.beside - 1 or (f, k) == (plan.fields - 1, plan.planes - 1):
                out_ref[number] = group
                wide_ref[number] = group
            alternating = jnp.sum(x * sign, axis=0, keepdims=True)
            sums[f] = jnp.where(row == k, alternating, sums[f])
    last = sums[0]
    for f in range(plan.fields):
        start = f * plan.rest
        last = jnp.where(lane >= start, moved(sums[f], start - plan.full), last)
    out_ref[plan.groups] = last
    wide_ref[plan.groups] = last
    even_theta = lax.axis_index("az") % 2 == 0
    pick_columns(plan, x_ref, even_theta, wide_ref, plan.groups + 1)


def pack(plan, fields):
    f32 = jnp.float32
    columns = plan.fields * plan.radial // LANES
    inside = pl.BlockSpec(memory_space=pltpu.VMEM)
    return pl.pallas_call(
        functools.partial(pack_kernel, plan),
        in_specs=[inside],
        out_specs=[inside] * 2,
        out_shape=[
            jax.ShapeDtypeStruct((plan.groups + 1, plan.theta, LANES), f32),
            jax.ShapeDtypeStruct((plan.groups + 1 + columns, plan.theta, LANES), f32),
        ],
        compiler_params=pltpu.CompilerParams(vmem_limit_bytes=VMEM_LIMIT),
        name="pack",
        cost_estimate=pl.CostEstimate(flops=1000000, bytes_accessed=800000, transcendentals=0),
    )(fields)


def edges_kernel(plan, x_ref, after_ref, az_b, ax_a, ax_b):
    del after_ref
    odd_plane = lax.axis_index("ax") % 2
    last = plan.planes - 1
    ax_a[...] = x_ref[:, (1 - odd_plane) * last, :, LANES:]
    ax_b[...] = x_ref[:, odd_plane * last, :, LANES:]
    even_theta = lax.axis_index("az") % 2 == 0
    pick_columns(plan, x_ref, jnp.logical_not(even_theta), az_b, 0)


def edges(plan, fields, after):
    f32 = jnp.float32
    columns = plan.fields * plan.radial // LANES
    plane = jax.ShapeDtypeStruct((plan.fields, plan.theta, plan.radial - LANES), f32)
    inside = pl.BlockSpec(memory_space=pltpu.VMEM)
    return pl.pallas_call(
        functools.partial(edges_kernel, plan),
        in_specs=[inside] * 2,
        out_specs=[inside] * 3,
        out_shape=[jax.ShapeDtypeStruct((columns, plan.theta, LANES), f32), plane, plane],
        compiler_params=pltpu.CompilerParams(vmem_limit_bytes=VMEM_LIMIT),
        name="edges",
        cost_estimate=pl.CostEstimate(flops=0, bytes_accessed=1000000, transcendentals=0),
    )(fields, after)


def advance(coef, q, jp, jm, tp, tm, kp, km):
    c0, c2, half, angular, over, square, cross = coef
    ur, ut, uz, temp = q[:4]
    radial = half - (0.5 * time_step) * ur
    azimuthal = angular * ut
    axial = (0.5 * time_step) * uz
    nu_dt = viscosity * time_step
    out = []
    d_theta = []
    for f in range(5):
        dt = tp[f] - tm[f]
        if f < 2:
            d_theta.append(dt)
        value = c0 * q[f] + nu_dt * ((jp[f] + jm[f]) + (kp[f] + km[f]))
        value = value + c2 * (tp[f] + tm[f])
        value = value + (jp[f] - jm[f]) * radial
        value = value - dt * azimuthal
        value = value - (kp[f] - km[f]) * axial
        out.append(value)
    swirl = over * ut
    out[0] = out[0] + swirl * ut - square * ur - cross * d_theta[1]
    out[1] = out[1] - swirl * ur - square * ut + cross * d_theta[0]
    out[2] = out[2] + (time_step * buoyancy) * temp
    return out


def turned(x, row, before, after):
    last = x.shape[0] - 1
    up = jnp.where(row == last, after, pltpu.roll(x, last, 0))
    down = jnp.where(row == 0, before, pltpu.roll(x, 1, 0))
    return up, down


def choose_halos(plan, tiles, az_a, az_b, ax_a, ax_b, side, ends):
    even_theta = lax.axis_index("az") % 2 == 0
    even_plane = lax.axis_index("ax") % 2 == 0
    all_tiles = plan.radial // LANES
    for f in range(plan.fields):
        for tile in tiles:
            here = slice(tile * LANES, (tile + 1) * LANES)
            number = f * all_tiles + tile
            a = az_a[plan.groups + 1 + number]
            b = az_b[number]
            side[0, number] = jnp.where(even_theta, b, a)
            side[1, number] = jnp.where(even_theta, a, b)
            a = ax_a[f, :, here]
            b = ax_b[f, :, here]
            ends[0, f, :, here] = jnp.where(even_plane, b, a)
            ends[1, f, :, here] = jnp.where(even_plane, a, b)


def outer_kernel(plan, coef_ref, x_ref, done, token):
    planes = plan.planes
    tiles = plan.radial // LANES
    token[...] = jnp.zeros_like(token)
    shape = (plan.theta, LANES)
    lane = lax.broadcasted_iota(jnp.int32, shape, 1)
    row = lax.broadcasted_iota(jnp.int32, shape, 0)

    def step(group, carry):
        start = pl.multiple_of(group * 4, 4)
        for i in range(4):
            k = start + i
            for tile in range(1, tiles):
                here = pl.ds(tile * LANES, LANES)
                coef = [coef_ref[j : j + 1, here] for j in range(7)]
                q, jp, jm, tp, tm, kp, km = ([] for _ in range(7))
                for f in range(plan.fields):
                    x = x_ref[f, k, :, here]
                    low = x_ref[f, k, :, pl.ds((tile - 1) * LANES, LANES)]
                    q.append(x)
                    high = 0.0
                    if tile + 1 < tiles:
                        high = x_ref[f, k, :, pl.ds((tile + 1) * LANES, LANES)]
                        high = pltpu.roll(high, LANES - 1, 1)
                    jp.append(jnp.where(lane == LANES - 1, high, pltpu.roll(x, LANES - 1, 1)))
                    jm.append(jnp.where(lane == 0, pltpu.roll(low, 1, 1), pltpu.roll(x, 1, 1)))
                    up, down = turned(x, row, 0.0, 0.0)
                    tp.append(up)
                    tm.append(down)
                    if i < 3:
                        above = x_ref[f, k + 1, :, here]
                    else:
                        above = x_ref[f, jnp.minimum(k + 1, planes - 1), :, here]
                        above = jnp.where(k == planes - 1, 0.0, above)
                    if i > 0:
                        below = x_ref[f, k - 1, :, here]
                    else:
                        below = x_ref[f, jnp.maximum(k - 1, 0), :, here]
                        below = jnp.where(k == 0, 0.0, below)
                    kp.append(above)
                    km.append(below)
                result = advance(coef, q, jp, jm, tp, tm, kp, km)
                for f in range(plan.fields):
                    done[k, f, :, pl.ds((tile - 1) * LANES, LANES)] = result[f]
        return carry

    lax.fori_loop(0, planes // 4, step, 0)


def outer(plan, coef, fields):
    inside = pl.BlockSpec(memory_space=pltpu.VMEM)
    f32 = jnp.float32
    return pl.pallas_call(
        functools.partial(outer_kernel, plan),
        in_specs=[inside] * 2,
        out_specs=[inside] * 2,
        out_shape=[
            jax.ShapeDtypeStruct((plan.planes, plan.fields, plan.theta, plan.radial - LANES), f32),
            jax.ShapeDtypeStruct((8, LANES), f32),
        ],
        compiler_params=pltpu.CompilerParams(vmem_limit_bytes=VMEM_LIMIT),
        name="outer",
        cost_estimate=pl.CostEstimate(flops=16000000, bytes_accessed=5000000, transcendentals=0),
    )(coef, fields)


def slabs_beside(a, b):
    slab = lax.axis_index("ax")
    even_plane = slab % 2 == 0
    b = jnp.where((slab > 0) & (slab < lax.axis_size("ax") - 1), b, 0.0)
    return jnp.where(even_plane, b, a), jnp.where(even_plane, a, b)


def seams(plan, coef_ref, x_ref, own_a, own_b, az_a, az_b, ax_a, ax_b, part_ref, done):
    nu_dt = viscosity * time_step
    half = 0.5 * time_step
    planes = plan.planes
    tiles = plan.radial // LANES
    base = plan.groups + 1
    even_theta = lax.axis_index("az") % 2 == 0
    last = plan.theta - 1
    row = lax.broadcasted_iota(jnp.int32, (plan.theta, LANES), 0)
    for tile in range(1, tiles):
        here = slice(tile * LANES, (tile + 1) * LANES)
        there = slice((tile - 1) * LANES, tile * LANES)
        c2 = coef_ref[1:2, here]
        angular = coef_ref[3:4, here]
        cross = coef_ref[6:7, here]
        number = tiles + tile
        mine_a = own_a[base + number]
        mine_b = own_b[number]
        turn_low = angular * jnp.where(even_theta, mine_b, mine_a)
        turn_high = angular * jnp.where(even_theta, mine_a, mine_b)
        before = []
        after = []
        for f in range(plan.fields):
            a = az_a[base + f * tiles + tile]
            b = az_b[f * tiles + tile]
            before.append(jnp.where(even_theta, b, a))
            after.append(jnp.where(even_theta, a, b))
        for f in range(plan.fields):
            low = (c2 + turn_low) * before[f]
            high = (c2 - turn_high) * after[f]
            if f == 0:
                low = low + cross * before[1]
                high = high - cross * after[1]
            if f == 1:
                low = low - cross * before[0]
                high = high + cross * after[0]
            below, above = slabs_beside(ax_a[f, :, there], ax_b[f, :, there])
            for k in range(planes):
                value = part_ref[k, f, :, there]
                value = value + jnp.where(row == 0, low[k : k + 1], 0.0)
                value = value + jnp.where(row == last, high[k : k + 1], 0.0)
                if k == 0:
                    value = value + (nu_dt + half * x_ref[2, k, :, here]) * below
                if k == planes - 1:
                    value = value + (nu_dt - half * x_ref[2, k, :, here]) * above
                done[k, f, :, there] = value


def gate_kernel(x_ref, token_ref, out_ref):
    del token_ref
    out_ref[...] = x_ref[...]


def gate(x, token):
    inside = pl.BlockSpec(memory_space=pltpu.VMEM)
    return pl.pallas_call(
        gate_kernel,
        in_specs=[inside] * 2,
        out_specs=inside,
        out_shape=jax.ShapeDtypeStruct(x.shape, x.dtype),
        compiler_params=pltpu.CompilerParams(vmem_limit_bytes=VMEM_LIMIT),
        name="gate",
    )(x, token)


def halves(x, depth=None):
    high = x.astype(jnp.bfloat16)
    low = (x - high.astype(jnp.float32)).astype(jnp.bfloat16)
    parts = [high, low, high]
    if depth is not None:
        parts.append(jnp.zeros((depth - 3 * x.shape[0], x.shape[1]), jnp.bfloat16))
    return jnp.concatenate(parts, axis=0)


def two_groups(pieces, g):
    return jnp.concatenate(
        [jnp.concatenate([piece[g + i] for piece in pieces], axis=0) for i in range(2)], axis=1
    )


def early_kernel(plan, forward_ref, *refs):
    pieces = refs[: len(plan.early)]
    spectra_ref, total_ref = refs[len(plan.early) :]
    table = forward_ref[lax.axis_index("az")]
    for g in range(0, plan.groups, 2):
        both = halves(two_groups(pieces, g), plan.depth)
        spectra_ref[g // 2] = jnp.dot(table, both, preferred_element_type=jnp.float32)
    total = pieces[0][plan.groups]
    for piece in pieces[1:]:
        total = total + piece[plan.groups]
    total_ref[...] = total


def early_spectra(plan, pieces):
    inside = pl.BlockSpec(memory_space=pltpu.VMEM)
    f32 = jnp.float32
    return pl.pallas_call(
        functools.partial(early_kernel, plan),
        in_specs=[inside] * (1 + len(pieces)),
        out_specs=[inside] * 2,
        out_shape=[
            jax.ShapeDtypeStruct((plan.groups // 2, 2 * plan.modes, 2 * LANES), f32),
            jax.ShapeDtypeStruct((plan.theta, LANES), f32),
        ],
        compiler_params=pltpu.CompilerParams(vmem_limit_bytes=VMEM_LIMIT),
        name="early",
        cost_estimate=pl.CostEstimate(flops=200000000, bytes_accessed=1500000, transcendentals=0),
    )(jnp.asarray(plan.forward(plan.early)), *pieces)


def filter_kernel(plan, x_ref, forward_ref, inverse_ref, mask_ref, early_ref, early_total, *refs):
    count = len(plan.late)
    pieces = refs[:count]
    own_ref, across_ref, edge_ref, sums_ref, message_a, message_b = refs[count:]
    odd_plane = lax.axis_index("ax") % 2
    theta = plan.theta
    sector = lax.axis_index("az")
    forward = forward_ref[sector]
    table = inverse_ref[sector]
    mask = mask_ref[...]
    mask = jnp.concatenate([mask, mask], axis=1)

    for g in range(0, plan.groups, 2):
        both = halves(two_groups(pieces, g), plan.depth)
        spectra = early_ref[g // 2] + jnp.dot(forward, both, preferred_element_type=jnp.float32)
        kept = halves(spectra * mask)
        state = jnp.dot(table, kept, preferred_element_type=jnp.float32)
        for i in range(2):
            lanes = slice(i * LANES, (i + 1) * LANES)
            own_ref[g + i] = state[:theta, lanes]
            across_ref[g + i] = state[theta : 2 * theta, lanes]
            edge_ref[g + i] = state[2 * theta : 2 * theta + 8, lanes]

    total = early_total[...]
    for piece in pieces:
        total = total + piece[plan.groups]
    total = total * (1.0 / plan.total)
    lane = lax.broadcasted_iota(jnp.int32, (plan.planes, LANES), 1)
    for f in range(plan.fields):
        value = moved(total, plan.full - f * plan.rest)
        sums_ref[f] = jnp.where((lane >= plan.full) & (lane < NEAR), value, 0.0)

    row = lax.broadcasted_iota(jnp.int32, (theta, LANES), 0)
    sign = (1 - 2 * (row & 1)).astype(jnp.float32)

    def message(ref, k):
        for f in range(plan.fields):
            number, first = plan.place(f, k)
            raw = x_ref[f, k, :, :LANES] - sign * sums_ref[f, k : k + 1]
            ref[f] = jnp.where(lane < plan.full, moved(own_ref[number], -first), raw)

    def both_messages(a, b):
        message(message_a, a)
        message(message_b, b)

    pl.when(odd_plane == 1)(lambda: both_messages(0, plan.planes - 1))
    pl.when(odd_plane == 0)(lambda: both_messages(plan.planes - 1, 0))


def filtered(plan, fields, pieces, early):
    inside = pl.BlockSpec(memory_space=pltpu.VMEM)
    f32 = jnp.float32
    cube = jax.ShapeDtypeStruct((plan.groups, plan.theta, LANES), f32)
    plane = jax.ShapeDtypeStruct((plan.fields, plan.theta, LANES), f32)
    return pl.pallas_call(
        functools.partial(filter_kernel, plan),
        in_specs=[inside] * (6 + len(pieces)),
        out_specs=[inside] * 6,
        out_shape=[
            cube,
            cube,
            jax.ShapeDtypeStruct((plan.groups, 8, LANES), f32),
            jax.ShapeDtypeStruct((plan.fields, plan.planes, LANES), f32),
            plane,
            plane,
        ],
        compiler_params=pltpu.CompilerParams(vmem_limit_bytes=VMEM_LIMIT),
        name="filter",
        cost_estimate=pl.CostEstimate(flops=200000000, bytes_accessed=1500000, transcendentals=0),
    )(
        fields,
        jnp.asarray(plan.forward(plan.late)),
        jnp.asarray(plan.inverse()),
        jnp.asarray(plan.mask()),
        *early,
        *pieces,
    )


def inner_kernel(
    plan, coef_ref, own_ref, across_ref, edge_ref, sums_ref, x_ref, own_a, own_b, az_a, az_b,
    ax_a, ax_b, part_ref, out_ref, done, far_done, state, outs
):
    planes = plan.planes
    seams(plan, coef_ref, x_ref, own_a, own_b, az_a, az_b, ax_a, ax_b, part_ref, far_done)
    beyond = pl.ds(LANES, plan.radial - LANES)
    stores = [
        pltpu.make_async_copy(far_done.at[k], out_ref.at[:, k, :, beyond], outs.at[k])
        for k in range(planes)
    ]
    for copy in stores:
        copy.start()
    theta = plan.theta
    tiles = plan.radial // LANES
    shape = (theta, LANES)
    lane = lax.broadcasted_iota(jnp.int32, shape, 1)
    row = lax.broadcasted_iota(jnp.int32, shape, 0)
    sign = (1 - 2 * (row & 1)).astype(jnp.float32)
    lane1 = lax.broadcasted_iota(jnp.int32, (1, LANES), 1)
    first = slice(0, LANES)
    coef = [coef_ref[i : i + 1, first] for i in range(7)]
    flips = (-1.0, -1.0, 1.0, 1.0, 1.0)
    even_theta = lax.axis_index("az") % 2 == 0

    for k in range(planes):
        for f in range(plan.fields):
            number, start = plan.place(f, k)
            state[k, f] = jnp.where(
                lane < plan.full,
                moved(own_ref[number], -start),
                x_ref[f, k, :, first] - sign * sums_ref[f, k : k + 1],
            )

    befores = []
    afters = []
    for f in range(plan.fields):
        a = az_a[plan.groups + 1 + f * tiles]
        b = az_b[f * tiles]
        befores.append(jnp.where(even_theta, b, a) + sums_ref[f])
        afters.append(jnp.where(even_theta, a, b) - sums_ref[f])

    zero = jnp.zeros(shape, jnp.float32)
    for k in range(planes):
        q, jp, jm, tp, tm, kp, km = ([] for _ in range(7))
        for f in range(plan.fields):
            number, start = plan.place(f, k)
            x = state[k, f]
            q.append(x)
            high_part = pltpu.roll(x_ref[f, k, :, LANES : 2 * LANES], LANES - 1, 1)
            jp.append(jnp.where(lane == LANES - 1, high_part, pltpu.roll(x, LANES - 1, 1)))
            opposite = flips[f] * moved(across_ref[number], -start)
            jm.append(jnp.where(lane == 0, opposite, pltpu.roll(x, 1, 1)))
            sides = moved(edge_ref[number], -start)
            before = jnp.where(lane1 < plan.full, sides[0:1], befores[f][k : k + 1])
            after = jnp.where(lane1 < plan.full, sides[1:2], afters[f][k : k + 1])
            up, down = turned(x, row, before, after)
            tp.append(up)
            tm.append(down)
            kp.append(state[k + 1, f] if k + 1 < planes else zero)
            km.append(state[k - 1, f] if k > 0 else zero)
        result = advance(coef, q, jp, jm, tp, tm, kp, km)
        for f in range(plan.fields):
            done[k, f] = result[f]
    for copy in stores:
        copy.wait()


def inner(plan, coef, parts, fields, own, sides, rests, part):
    inside = pl.BlockSpec(memory_space=pltpu.VMEM)
    f32 = jnp.float32
    return pl.pallas_call(
        functools.partial(inner_kernel, plan),
        in_specs=[inside] * 13,
        out_specs=[pl.BlockSpec(memory_space=pl.ANY), inside],
        out_shape=[
            jax.ShapeDtypeStruct(fields.shape, f32),
            jax.ShapeDtypeStruct((plan.planes, plan.fields, plan.theta, LANES), f32),
        ],
        scratch_shapes=[
            pltpu.VMEM(part.shape, f32),
            pltpu.VMEM((plan.planes, plan.fields, plan.theta, LANES), f32),
            pltpu.SemaphoreType.DMA((plan.planes,)),
        ],
        compiler_params=pltpu.CompilerParams(vmem_limit_bytes=VMEM_LIMIT),
        name="inner",
        cost_estimate=pl.CostEstimate(flops=6000000, bytes_accessed=2500000, transcendentals=0),
    )(coef, *parts, fields, *own, *sides, *rests, part)


def finish_kernel(plan, near_ref, own_a, own_b, ax_a, ax_b, other_ref, out_ref, ends, sems):
    del other_ref
    planes = plan.planes
    first = pl.ds(0, LANES)
    copies = [
        pltpu.make_async_copy(near_ref.at[k], out_ref.at[:, k, :, first], sems.at[k])
        for k in range(1, planes - 1)
    ]
    for copy in copies:
        copy.start()
    even_plane = lax.axis_index("ax") % 2 == 0
    nu_dt = viscosity * time_step
    half = 0.5 * time_step
    sent_a = own_a[2]
    sent_b = own_b[2]
    factor_low = nu_dt + half * jnp.where(even_plane, sent_b, sent_a)
    factor_high = nu_dt - half * jnp.where(even_plane, sent_a, sent_b)
    for f in range(plan.fields):
        below, above = slabs_beside(ax_a[f], ax_b[f])
        ends[0, f] = near_ref[0, f] + factor_low * below
        ends[1, f] = near_ref[planes - 1, f] + factor_high * above
    for end, k in ((0, 0), (1, planes - 1)):
        copies.append(pltpu.make_async_copy(ends.at[end], out_ref.at[:, k, :, first], sems.at[k]))
        copies[-1].start()
    for copy in copies:
        copy.wait()


def finish(plan, near, sent, messages, partial):
    anywhere = pl.BlockSpec(memory_space=pl.ANY)
    inside = pl.BlockSpec(memory_space=pltpu.VMEM)
    return pl.pallas_call(
        functools.partial(finish_kernel, plan),
        in_specs=[inside] * 5 + [anywhere],
        out_specs=anywhere,
        out_shape=jax.ShapeDtypeStruct(partial.shape, jnp.float32),
        input_output_aliases={5: 0},
        scratch_shapes=[
            pltpu.VMEM((2, plan.fields, plan.theta, LANES), jnp.float32),
            pltpu.SemaphoreType.DMA((plan.planes,)),
        ],
        compiler_params=pltpu.CompilerParams(vmem_limit_bytes=VMEM_LIMIT),
        name="finish",
        cost_estimate=pl.CostEstimate(flops=100000, bytes_accessed=1500000, transcendentals=0),
    )(near, *sent, *messages, partial)


def pairs(count, start):
    route = []
    for low in range(start, count, 2):
        high = (low + 1) % count
        route += [(low, high), (high, low)]
    return route


def fast_on_device(fields):
    sectors = lax.axis_size("az")
    slabs = lax.axis_size("ax")
    plan = Plan(fields.shape, sectors)
    coef = jnp.asarray(plan.coefficients())

    def send(x, distance):
        return lax.ppermute(x, "az", [(i, i ^ distance) for i in range(sectors)])

    packed, wide = pack(plan, fields)
    half = sectors // 2
    pieces = [None] * sectors
    pieces[0] = packed
    far = send(packed, half)
    pieces[half] = far
    for p in range(half - 1, 0, -1):
        pieces[p] = send(wide if p == 1 else packed, p)
    part, token = outer(plan, coef, fields)
    onward = gate(far, token)
    for p in range(half - 1, 0, -1):
        pieces[half + p] = send(onward, p)
    pieces[half] = onward
    early = early_spectra(plan, pieces[: half + 1])
    column, rest_a, rest_b = edges(plan, fields, early[1])
    sides = (pieces[1], lax.ppermute(column, "az", pairs(sectors, 1)))
    rests = (
        lax.ppermute(rest_a, "ax", pairs(slabs, 0)),
        lax.ppermute(rest_b, "ax", pairs(slabs, 1)),
    )
    *parts, message_a, message_b = filtered(plan, fields, pieces[half + 1 :], early)
    messages = (
        lax.ppermute(message_a, "ax", pairs(slabs, 0)),
        lax.ppermute(message_b, "ax", pairs(slabs, 1)),
    )
    partial, near = inner(plan, coef, parts, fields, (wide, column), sides, rests, part)
    return finish(plan, near, (message_a, message_b), messages, partial)


def on_device(fields):
    total_theta = fields.shape[2] * lax.axis_size("az")
    if Plan.fits(fields.shape, lax.axis_size("az"), lax.axis_size("ax"), total_theta):
        return fast_on_device(fields)
    return general_on_device(fields)


def solution(mesh):
    placed = (P(None, "ax", "az", None),)
    return jax.shard_map(
        on_device, mesh=mesh, in_specs=placed, out_specs=P(None, "ax", "az", None), check_vma=False
    )
```

```python
import functools

import jax
import jax.numpy as jnp
import numpy as np
from jax import lax
from jax.experimental import pallas as pl
from jax.experimental.pallas import tpu as pltpu
from jax.sharding import PartitionSpec as P

NEAR = 40


viscosity = 0.2
time_step = 0.1
buoyancy = 1.0

LANES = 128
VMEM_LIMIT = 16 * 1024 * 1024


def swapped(block, axis, distance):
    count = lax.axis_size(axis)
    route = []
    for low in range(count):
        high = low | 1 << distance
        if high != low and high < count:
            route += [(low, high), (high, low)]
    return lax.ppermute(block, axis, route)


def with_halo(block, sides, width, periodic):
    for axis, dim in sides:
        count = lax.axis_size(axis)
        forward = [(i, i + 1) for i in range(count - 1)]
        if periodic:
            forward.append((count - 1, 0))
        backward = [(target, source) for source, target in forward]
        low = lax.ppermute(
            lax.slice_in_dim(block, block.shape[dim] - width, None, axis=dim), axis, forward
        )
        high = lax.ppermute(lax.slice_in_dim(block, 0, width, axis=dim), axis, backward)
        block = jnp.concatenate([low, block, high], axis=dim)
    return block


def mode_tables(theta_index, total_theta, modes):
    column = jnp.arange(modes, dtype=jnp.int32)
    product = theta_index[:, None] * column[None, :] % total_theta
    angle = product.astype(jnp.float32) * (2.0 * jnp.pi / total_theta)
    cosine = jnp.cos(angle)
    sine = jnp.sin(angle)
    weight = jnp.where(column == 0, 1.0, 2.0).astype(jnp.float32) / total_theta
    forward = jnp.concatenate([cosine * weight[None, :], sine * (2.0 / total_theta)], axis=1)
    inverse = jnp.concatenate([cosine, sine], axis=1)
    return (forward, inverse)


def cycle_mask(cycles, modes):
    cycle_index = jnp.arange(cycles, dtype=jnp.int32)
    cutoff = jnp.minimum(355 * (2 * cycle_index + 1) // 226, modes - 1)
    column = jnp.arange(modes, dtype=jnp.int32)
    keep = (column[None, :] <= cutoff[:, None]).astype(jnp.float32)
    return jnp.concatenate([keep, keep], axis=1)


def operators(
    center, radial_plus, radial_minus, theta_plus, theta_minus, axial_plus, axial_minus, total_theta
):
    radius = jnp.arange(center.shape[-1], dtype=jnp.float32) + 0.5
    step_angle = 2.0 * jnp.pi / total_theta
    d_radial = (radial_plus - radial_minus) * 0.5
    d_theta = (theta_plus - theta_minus) / (2.0 * step_angle)
    d_axial = (axial_plus - axial_minus) * 0.5
    laplace = (
        radial_plus - 2.0 * center + radial_minus + (radial_plus - radial_minus) / (2.0 * radius)
    )
    laplace = laplace + (theta_plus - 2.0 * center + theta_minus) / (
        radius * radius * step_angle * step_angle
    )
    laplace = laplace + axial_plus - 2.0 * center + axial_minus
    return (d_radial, d_theta, d_axial, laplace)


def general_on_device(fields):
    count_fields, planes, theta_dev, radial = fields.shape
    sectors = lax.axis_size("az")
    total_theta = theta_dev * sectors
    modes = min(128, total_theta // 2)
    sector = lax.axis_index("az")
    own_index = sector * theta_dev + jnp.arange(theta_dev, dtype=jnp.int32)
    own_forward, own_inverse = mode_tables(own_index, total_theta, modes)
    inner_cycles = fields[:, :, :, :NEAR]
    kept = None
    piece = lax.all_gather(inner_cycles, "az", axis=2, tiled=True)
    piece_index = jnp.arange(piece.shape[2], dtype=jnp.int32)
    piece_forward, unused_inverse = mode_tables(piece_index, total_theta, modes)
    spectra = jnp.einsum("fztj,tc->fzjc", piece, piece_forward, precision=lax.Precision.HIGHEST)
    kept = spectra * cycle_mask(NEAR, modes)[None, None]
    smoothed = jnp.einsum("fzjc,tc->fztj", kept, own_inverse, precision=lax.Precision.HIGHEST)
    state = jnp.concatenate([smoothed, fields[:, :, :, NEAR:]], axis=3)
    flip = jnp.array([-1.0, -1.0, 1.0, 1.0, 1.0], dtype=jnp.float32)[:, None, None]
    top_bit = sectors.bit_length() - 1
    opposite = swapped(state[:, :, :, 0], "az", top_bit - 1)
    opposite = opposite * flip
    theta_padded = with_halo(state, (("az", 2),), 1, True)
    axial_padded = with_halo(state, (("ax", 1),), 1, False)
    radial_plus = jnp.concatenate([state[:, :, :, 1:], jnp.zeros_like(state[:, :, :, :1])], axis=3)
    radial_minus = jnp.concatenate([opposite[:, :, :, None], state[:, :, :, :-1]], axis=3)
    d_radial, d_theta, d_axial, laplace = operators(
        state,
        radial_plus,
        radial_minus,
        theta_padded[:, :, 2:, :],
        theta_padded[:, :, :-2, :],
        axial_padded[:, 2:, :, :],
        axial_padded[:, :-2, :, :],
        total_theta,
    )
    radius = jnp.arange(radial, dtype=jnp.float32) + 0.5
    radial_u = state[0]
    theta_u = state[1]
    axial_u = state[2]
    change = (
        -(radial_u[None] * d_radial + (theta_u / radius)[None] * d_theta + axial_u[None] * d_axial)
        + viscosity * laplace
    )
    inverse_square = 1.0 / (radius * radius)
    first = (
        change[0]
        + theta_u * theta_u / radius
        - viscosity * (radial_u * inverse_square + 2.0 * inverse_square * d_theta[1])
    )
    second = (
        change[1]
        - radial_u * theta_u / radius
        - viscosity * (theta_u * inverse_square - 2.0 * inverse_square * d_theta[0])
    )
    third = change[2] + buoyancy * state[3]
    change = jnp.concatenate([first[None], second[None], third[None], change[3:]], axis=0)
    return state + time_step * change


class Plan:
    def __init__(self, shape, sectors):
        self.fields, self.planes, self.theta, self.radial = shape
        self.sectors = sectors
        self.total = self.theta * sectors
        self.modes = min(128, self.total // 2)
        cycle = np.arange(NEAR)
        self.cut = np.minimum(355 * (2 * cycle + 1) // 226, self.modes - 1)
        self.full = int(np.sum(self.cut < self.modes - 1))
        self.rest = NEAR - self.full
        self.beside = LANES // max(self.full, 1)
        self.groups = -(-self.fields * self.planes // self.beside)
        self.spare = LANES - self.beside * self.full
        self.chunks = -(-self.fields * self.rest // max(self.spare, 1))
        self.early = tuple(range(sectors // 2 + 1))
        self.late = tuple(range(sectors // 2 + 1, sectors))
        self.depth = 256

    def place(self, f, k):
        index = k * self.fields + f
        return index // self.beside, index % self.beside * self.full

    @staticmethod
    def fits(shape, sectors, slabs, total):
        if sectors & (sectors - 1) or total // 2 > 128 or total != LANES or shape[2] != 16:
            return False
        plan = Plan(shape, sectors)
        return (
            plan.full > 0
            and plan.fields == 5
            and plan.planes == plan.theta
            and plan.rest * plan.fields <= LANES
            and plan.groups % 2 == 0
            and plan.spare > 0
            and plan.chunks <= plan.groups
            and slabs % 2 == 0
            and 3 * len(plan.early) * plan.theta <= plan.depth
            and plan.radial % LANES == 0
            and plan.radial > 2 * LANES
        )

    def split(self, table):
        high = table.astype(jnp.bfloat16)
        low = (table - high.astype(np.float32)).astype(jnp.bfloat16)
        return np.concatenate([high, high, low], axis=-1)

    def forward(self, pieces):
        theta = np.arange(self.total)
        mode = np.arange(self.modes)
        angle = (np.outer(mode, theta) % self.total) * (2.0 * np.pi / self.total)
        weight = np.where(mode == 0, 1.0, 2.0)[:, None] / self.total
        table = np.concatenate([np.cos(angle) * weight, np.sin(angle) * 2.0 / self.total], axis=0)
        table = table.astype(np.float32).reshape(2 * self.modes, self.sectors, self.theta)
        blocks = []
        for sector in range(self.sectors):
            chosen = np.concatenate([table[:, sector ^ p] for p in pieces], axis=1)
            chosen = self.split(chosen)
            pad = np.zeros((chosen.shape[0], self.depth - chosen.shape[1]), chosen.dtype)
            blocks.append(np.concatenate([chosen, pad], axis=1))
        return np.stack(blocks)

    def inverse(self):
        mode = np.arange(self.modes)
        blocks = []
        for sector in range(self.sectors):
            own = sector * self.theta + np.arange(self.theta)
            index = np.concatenate([own, own + self.total // 2, own[:1] - 1, own[-1:] + 1])
            angle = (np.outer(index, mode) % self.total) * (2.0 * np.pi / self.total)
            table = np.concatenate([np.cos(angle), np.sin(angle)], axis=1)
            pad = np.zeros((16 - 2, table.shape[1]))
            blocks.append(np.concatenate([table, pad], axis=0))
        return self.split(np.stack(blocks).astype(np.float32))

    def mask(self):
        mode = np.arange(self.modes)
        keep = np.zeros((self.modes, LANES), np.float32)
        for i in range(self.beside):
            keep[:, i * self.full : (i + 1) * self.full] = (
                mode[:, None] <= self.cut[None, : self.full]
            )
        return np.concatenate([keep, keep], axis=0)

    def coefficients(self):
        radius = np.arange(self.radial) + 0.5
        step = 2.0 * np.pi / self.total
        nu_dt = viscosity * time_step
        square = 1.0 / (radius * radius * step * step)
        rows = [
            1.0 - nu_dt * (4.0 + 2.0 * square),
            nu_dt * square,
            nu_dt / (2.0 * radius),
            time_step / (2.0 * step * radius),
            time_step / radius,
            nu_dt / (radius * radius),
            nu_dt / (step * radius * radius),
        ]
        rows.append(np.zeros(self.radial))
        return np.stack(rows).astype(np.float32)


def moved(x, lanes):
    return x if lanes % LANES == 0 else pltpu.roll(x, lanes % LANES, 1)


def pick_columns(plan, x_ref, keep_high, ref, base):
    last = plan.theta - 1
    tiles = plan.radial // LANES
    for f in range(plan.fields):
        for k in range(plan.planes):
            for tile in range(tiles):
                here = slice(tile * LANES, (tile + 1) * LANES)
                low = x_ref[f, k, 0:1, here]
                high = x_ref[f, k, last : last + 1, here]
                ref[base + f * tiles + tile, k : k + 1, :] = jnp.where(keep_high, high, low)


def pack_kernel(plan, x_ref, out_ref, wide_ref, rest_ref):
    odd_plane = lax.axis_index("ax") % 2
    rest_ref[...] = x_ref[:, odd_plane * (plan.planes - 1), :, LANES:]
    shape = (plan.theta, LANES)
    lane = lax.broadcasted_iota(jnp.int32, shape, 1)
    row = lax.broadcasted_iota(jnp.int32, shape, 0)
    sign = (1 - 2 * (row & 1)).astype(jnp.float32)
    group = jnp.zeros(shape, jnp.float32)
    sums = [jnp.zeros(shape, jnp.float32) for _ in range(plan.fields)]
    for k in range(plan.planes):
        for f in range(plan.fields):
            x = x_ref[f, k, :, :LANES]
            number, first = plan.place(f, k)
            part = moved(x, first)
            if first:
                part = jnp.where((lane >= first) & (lane < first + plan.full), part, group)
            group = part
            if first // plan.full == plan.beside - 1 or (f, k) == (plan.fields - 1, plan.planes - 1):
                out_ref[number] = group
                if number >= plan.chunks:
                    wide_ref[number] = group
            alternating = jnp.sum(x * sign, axis=0, keepdims=True)
            sums[f] = jnp.where(row == k, alternating, sums[f])
    last = sums[0]
    for f in range(plan.fields):
        start = f * plan.rest
        last = jnp.where(lane >= start, moved(sums[f], start - plan.full), last)
    for c in range(plan.chunks):
        start = LANES - plan.spare
        group = jnp.where(lane >= start, moved(last, start - plan.spare * c), out_ref[c])
        out_ref[c] = group
        wide_ref[c] = group
    even_theta = lax.axis_index("az") % 2 == 0
    pick_columns(plan, x_ref, even_theta, wide_ref, plan.groups)


def pack(plan, fields):
    f32 = jnp.float32
    columns = plan.fields * plan.radial // LANES
    inside = pl.BlockSpec(memory_space=pltpu.VMEM)
    return pl.pallas_call(
        functools.partial(pack_kernel, plan),
        in_specs=[inside],
        out_specs=[inside] * 3,
        out_shape=[
            jax.ShapeDtypeStruct((plan.groups, plan.theta, LANES), f32),
            jax.ShapeDtypeStruct((plan.groups + columns, plan.theta, LANES), f32),
            jax.ShapeDtypeStruct((plan.fields, plan.theta, plan.radial - LANES), f32),
        ],
        compiler_params=pltpu.CompilerParams(vmem_limit_bytes=VMEM_LIMIT),
        name="pack",
        cost_estimate=pl.CostEstimate(flops=1000000, bytes_accessed=800000, transcendentals=0),
    )(fields)


def edges_kernel(plan, x_ref, after_ref, az_b):
    del after_ref
    even_theta = lax.axis_index("az") % 2 == 0
    pick_columns(plan, x_ref, jnp.logical_not(even_theta), az_b, 0)


def edges(plan, fields, after):
    f32 = jnp.float32
    columns = plan.fields * plan.radial // LANES
    inside = pl.BlockSpec(memory_space=pltpu.VMEM)
    return pl.pallas_call(
        functools.partial(edges_kernel, plan),
        in_specs=[inside] * 2,
        out_specs=inside,
        out_shape=jax.ShapeDtypeStruct((columns, plan.theta, LANES), f32),
        compiler_params=pltpu.CompilerParams(vmem_limit_bytes=VMEM_LIMIT),
        name="edges",
        cost_estimate=pl.CostEstimate(flops=0, bytes_accessed=1000000, transcendentals=0),
    )(fields, after)


def advance(coef, q, jp, jm, tp, tm, kp, km):
    c0, c2, half, angular, over, square, cross = coef
    ur, ut, uz, temp = q[:4]
    radial = half - (0.5 * time_step) * ur
    azimuthal = angular * ut
    axial = (0.5 * time_step) * uz
    nu_dt = viscosity * time_step
    out = []
    d_theta = []
    for f in range(5):
        dt = tp[f] - tm[f]
        if f < 2:
            d_theta.append(dt)
        value = c0 * q[f] + nu_dt * ((jp[f] + jm[f]) + (kp[f] + km[f]))
        value = value + c2 * (tp[f] + tm[f])
        value = value + (jp[f] - jm[f]) * radial
        value = value - dt * azimuthal
        value = value - (kp[f] - km[f]) * axial
        out.append(value)
    swirl = over * ut
    out[0] = out[0] + swirl * ut - square * ur - cross * d_theta[1]
    out[1] = out[1] - swirl * ur - square * ut + cross * d_theta[0]
    out[2] = out[2] + (time_step * buoyancy) * temp
    return out


def turned(x, row, before, after):
    last = x.shape[0] - 1
    up = jnp.where(row == last, after, pltpu.roll(x, last, 0))
    down = jnp.where(row == 0, before, pltpu.roll(x, 1, 0))
    return up, down


def outer_kernel(plan, coef_ref, x_ref, done, token):
    planes = plan.planes
    tiles = plan.radial // LANES
    token[...] = jnp.zeros_like(token)
    shape = (plan.theta, LANES)
    lane = lax.broadcasted_iota(jnp.int32, shape, 1)
    row = lax.broadcasted_iota(jnp.int32, shape, 0)

    def step(group, carry):
        start = pl.multiple_of(group * 4, 4)
        for i in range(4):
            k = start + i
            for tile in range(1, tiles):
                here = pl.ds(tile * LANES, LANES)
                coef = [coef_ref[j : j + 1, here] for j in range(7)]
                q, jp, jm, tp, tm, kp, km = ([] for _ in range(7))
                for f in range(plan.fields):
                    x = x_ref[f, k, :, here]
                    low = x_ref[f, k, :, pl.ds((tile - 1) * LANES, LANES)]
                    q.append(x)
                    high = 0.0
                    if tile + 1 < tiles:
                        high = x_ref[f, k, :, pl.ds((tile + 1) * LANES, LANES)]
                        high = pltpu.roll(high, LANES - 1, 1)
                    jp.append(jnp.where(lane == LANES - 1, high, pltpu.roll(x, LANES - 1, 1)))
                    jm.append(jnp.where(lane == 0, pltpu.roll(low, 1, 1), pltpu.roll(x, 1, 1)))
                    up, down = turned(x, row, 0.0, 0.0)
                    tp.append(up)
                    tm.append(down)
                    if i < 3:
                        above = x_ref[f, k + 1, :, here]
                    else:
                        above = x_ref[f, jnp.minimum(k + 1, planes - 1), :, here]
                        above = jnp.where(k == planes - 1, 0.0, above)
                    if i > 0:
                        below = x_ref[f, k - 1, :, here]
                    else:
                        below = x_ref[f, jnp.maximum(k - 1, 0), :, here]
                        below = jnp.where(k == 0, 0.0, below)
                    kp.append(above)
                    km.append(below)
                result = advance(coef, q, jp, jm, tp, tm, kp, km)
                for f in range(plan.fields):
                    done[k, f, :, pl.ds((tile - 1) * LANES, LANES)] = result[f]
        return carry

    lax.fori_loop(0, planes // 4, step, 0)


def outer(plan, coef, fields):
    inside = pl.BlockSpec(memory_space=pltpu.VMEM)
    f32 = jnp.float32
    return pl.pallas_call(
        functools.partial(outer_kernel, plan),
        in_specs=[inside] * 2,
        out_specs=[inside] * 2,
        out_shape=[
            jax.ShapeDtypeStruct((plan.planes, plan.fields, plan.theta, plan.radial - LANES), f32),
            jax.ShapeDtypeStruct((8, LANES), f32),
        ],
        compiler_params=pltpu.CompilerParams(vmem_limit_bytes=VMEM_LIMIT),
        name="outer",
        cost_estimate=pl.CostEstimate(flops=16000000, bytes_accessed=5000000, transcendentals=0),
    )(coef, fields)


def slabs_beside(a, b):
    slab = lax.axis_index("ax")
    even_plane = slab % 2 == 0
    b = jnp.where((slab > 0) & (slab < lax.axis_size("ax") - 1), b, 0.0)
    return jnp.where(even_plane, b, a), jnp.where(even_plane, a, b)


def seams(plan, coef_ref, x_ref, own_a, own_b, az_a, az_b, ax_b, part_ref, done):
    nu_dt = viscosity * time_step
    half = 0.5 * time_step
    planes = plan.planes
    tiles = plan.radial // LANES
    base = plan.groups
    even_theta = lax.axis_index("az") % 2 == 0
    last = plan.theta - 1
    row = lax.broadcasted_iota(jnp.int32, (plan.theta, LANES), 0)
    for tile in range(1, tiles):
        here = slice(tile * LANES, (tile + 1) * LANES)
        there = slice((tile - 1) * LANES, tile * LANES)
        c2 = coef_ref[1:2, here]
        angular = coef_ref[3:4, here]
        cross = coef_ref[6:7, here]
        number = tiles + tile
        mine_a = own_a[base + number]
        mine_b = own_b[number]
        turn_low = angular * jnp.where(even_theta, mine_b, mine_a)
        turn_high = angular * jnp.where(even_theta, mine_a, mine_b)
        before = []
        after = []
        for f in range(plan.fields):
            a = az_a[base + f * tiles + tile]
            b = az_b[f * tiles + tile]
            before.append(jnp.where(even_theta, b, a))
            after.append(jnp.where(even_theta, a, b))
        for f in range(plan.fields):
            low = (c2 + turn_low) * before[f]
            high = (c2 - turn_high) * after[f]
            if f == 0:
                low = low + cross * before[1]
                high = high - cross * after[1]
            if f == 1:
                low = low - cross * before[0]
                high = high + cross * after[0]
            below, above = slabs_beside(0.0, ax_b[f, :, there])
            for k in range(planes):
                value = part_ref[k, f, :, there]
                value = value + jnp.where(row == 0, low[k : k + 1], 0.0)
                value = value + jnp.where(row == last, high[k : k + 1], 0.0)
                if k == 0:
                    value = value + (nu_dt + half * x_ref[2, k, :, here]) * below
                if k == planes - 1:
                    value = value + (nu_dt - half * x_ref[2, k, :, here]) * above
                done[k, f, :, there] = value


def gate_kernel(x_ref, token_ref, out_ref):
    del token_ref
    out_ref[...] = x_ref[...]


def gate(x, token):
    inside = pl.BlockSpec(memory_space=pltpu.VMEM)
    return pl.pallas_call(
        gate_kernel,
        in_specs=[inside] * 2,
        out_specs=inside,
        out_shape=jax.ShapeDtypeStruct(x.shape, x.dtype),
        compiler_params=pltpu.CompilerParams(vmem_limit_bytes=VMEM_LIMIT),
        name="gate",
    )(x, token)


def halves(x, depth=None):
    high = x.astype(jnp.bfloat16)
    low = (x - high.astype(jnp.float32)).astype(jnp.bfloat16)
    parts = [high, low, high]
    if depth is not None:
        parts.append(jnp.zeros((depth - 3 * x.shape[0], x.shape[1]), jnp.bfloat16))
    return jnp.concatenate(parts, axis=0)


def two_groups(pieces, g):
    return jnp.concatenate(
        [jnp.concatenate([piece[g + i] for piece in pieces], axis=0) for i in range(2)], axis=1
    )


def alternating_sums(plan, pieces):
    lane = lax.broadcasted_iota(jnp.int32, (plan.theta, LANES), 1)
    total = jnp.zeros((plan.theta, LANES), jnp.float32)
    for c in range(plan.chunks):
        value = pieces[0][c]
        for piece in pieces[1:]:
            value = value + piece[c]
        start = plan.spare * c
        here = (lane >= start) & (lane < start + plan.spare)
        total = jnp.where(here, moved(value, start + plan.spare - LANES), total)
    return total


def early_kernel(plan, forward_ref, after_ref, *refs):
    del after_ref
    pieces = refs[: len(plan.early)]
    spectra_ref, total_ref = refs[len(plan.early) :]
    table = forward_ref[lax.axis_index("az")]
    for g in range(0, plan.groups, 2):
        both = halves(two_groups(pieces, g), plan.depth)
        spectra_ref[g // 2] = jnp.dot(table, both, preferred_element_type=jnp.float32)
    total_ref[...] = alternating_sums(plan, pieces)


def early_spectra(plan, pieces, after):
    inside = pl.BlockSpec(memory_space=pltpu.VMEM)
    f32 = jnp.float32
    return pl.pallas_call(
        functools.partial(early_kernel, plan),
        in_specs=[inside] * (2 + len(pieces)),
        out_specs=[inside] * 2,
        out_shape=[
            jax.ShapeDtypeStruct((plan.groups // 2, 2 * plan.modes, 2 * LANES), f32),
            jax.ShapeDtypeStruct((plan.theta, LANES), f32),
        ],
        compiler_params=pltpu.CompilerParams(vmem_limit_bytes=VMEM_LIMIT),
        name="early",
        cost_estimate=pl.CostEstimate(flops=200000000, bytes_accessed=1500000, transcendentals=0),
    )(jnp.asarray(plan.forward(plan.early)), after, *pieces)


def filter_kernel(plan, x_ref, forward_ref, inverse_ref, mask_ref, early_ref, early_total, *refs):
    count = len(plan.late)
    pieces = refs[:count]
    own_ref, across_ref, edge_ref, sums_ref, message_a, message_b = refs[count:]
    odd_plane = lax.axis_index("ax") % 2
    theta = plan.theta
    sector = lax.axis_index("az")
    forward = forward_ref[sector]
    table = inverse_ref[sector]
    mask = mask_ref[...]
    mask = jnp.concatenate([mask, mask], axis=1)

    for g in range(0, plan.groups, 2):
        both = halves(two_groups(pieces, g), plan.depth)
        spectra = early_ref[g // 2] + jnp.dot(forward, both, preferred_element_type=jnp.float32)
        kept = halves(spectra * mask)
        state = jnp.dot(table, kept, preferred_element_type=jnp.float32)
        for i in range(2):
            lanes = slice(i * LANES, (i + 1) * LANES)
            own_ref[g + i] = state[:theta, lanes]
            across_ref[g + i] = state[theta : 2 * theta, lanes]
            edge_ref[g + i] = state[2 * theta : 2 * theta + 8, lanes]

    total = early_total[...] + alternating_sums(plan, pieces)
    total = total * (1.0 / plan.total)
    lane = lax.broadcasted_iota(jnp.int32, (plan.planes, LANES), 1)
    for f in range(plan.fields):
        value = moved(total, plan.full - f * plan.rest)
        sums_ref[f] = jnp.where((lane >= plan.full) & (lane < NEAR), value, 0.0)

    row = lax.broadcasted_iota(jnp.int32, (theta, LANES), 0)
    sign = (1 - 2 * (row & 1)).astype(jnp.float32)

    def message(ref, k):
        for f in range(plan.fields):
            number, first = plan.place(f, k)
            raw = x_ref[f, k, :, :LANES] - sign * sums_ref[f, k : k + 1]
            ref[f, :, :LANES] = jnp.where(lane < plan.full, moved(own_ref[number], -first), raw)

    def both_messages(a, b):
        message(message_a, a)
        message_a[:, :, LANES:] = x_ref[:, a, :, LANES:]
        message(message_b, b)

    pl.when(odd_plane == 1)(lambda: both_messages(0, plan.planes - 1))
    pl.when(odd_plane == 0)(lambda: both_messages(plan.planes - 1, 0))


def filtered(plan, fields, pieces, early):
    inside = pl.BlockSpec(memory_space=pltpu.VMEM)
    f32 = jnp.float32
    cube = jax.ShapeDtypeStruct((plan.groups, plan.theta, LANES), f32)
    plane = jax.ShapeDtypeStruct((plan.fields, plan.theta, LANES), f32)
    return pl.pallas_call(
        functools.partial(filter_kernel, plan),
        in_specs=[inside] * (6 + len(pieces)),
        out_specs=[inside] * 6,
        out_shape=[
            cube,
            cube,
            jax.ShapeDtypeStruct((plan.groups, 8, LANES), f32),
            jax.ShapeDtypeStruct((plan.fields, plan.planes, LANES), f32),
            jax.ShapeDtypeStruct((plan.fields, plan.theta, plan.radial), f32),
            plane,
        ],
        compiler_params=pltpu.CompilerParams(vmem_limit_bytes=VMEM_LIMIT),
        name="filter",
        cost_estimate=pl.CostEstimate(flops=200000000, bytes_accessed=1500000, transcendentals=0),
    )(
        fields,
        jnp.asarray(plan.forward(plan.late)),
        jnp.asarray(plan.inverse()),
        jnp.asarray(plan.mask()),
        *early,
        *pieces,
    )


def inner_kernel(
    plan, coef_ref, own_ref, across_ref, edge_ref, sums_ref, x_ref, own_a, own_b, az_a, az_b,
    ax_b, part_ref, out_ref, done, ends, far_done, state, outs
):
    planes = plan.planes
    seams(plan, coef_ref, x_ref, own_a, own_b, az_a, az_b, ax_b, part_ref, far_done)
    beyond = pl.ds(LANES, plan.radial - LANES)
    stores = [
        pltpu.make_async_copy(far_done.at[k], out_ref.at[:, k, :, beyond], outs.at[k])
        for k in range(1, planes - 1)
    ]
    for copy in stores:
        copy.start()
    ends[0] = far_done[0]
    ends[1] = far_done[planes - 1]
    theta = plan.theta
    tiles = plan.radial // LANES
    shape = (theta, LANES)
    lane = lax.broadcasted_iota(jnp.int32, shape, 1)
    row = lax.broadcasted_iota(jnp.int32, shape, 0)
    sign = (1 - 2 * (row & 1)).astype(jnp.float32)
    lane1 = lax.broadcasted_iota(jnp.int32, (1, LANES), 1)
    first = slice(0, LANES)
    coef = [coef_ref[i : i + 1, first] for i in range(7)]
    flips = (-1.0, -1.0, 1.0, 1.0, 1.0)
    even_theta = lax.axis_index("az") % 2 == 0

    for k in range(planes):
        for f in range(plan.fields):
            number, start = plan.place(f, k)
            state[k, f] = jnp.where(
                lane < plan.full,
                moved(own_ref[number], -start),
                x_ref[f, k, :, first] - sign * sums_ref[f, k : k + 1],
            )

    befores = []
    afters = []
    for f in range(plan.fields):
        a = az_a[plan.groups + f * tiles]
        b = az_b[f * tiles]
        befores.append(jnp.where(even_theta, b, a) + sums_ref[f])
        afters.append(jnp.where(even_theta, a, b) - sums_ref[f])

    zero = jnp.zeros(shape, jnp.float32)
    for k in range(planes):
        q, jp, jm, tp, tm, kp, km = ([] for _ in range(7))
        for f in range(plan.fields):
            number, start = plan.place(f, k)
            x = state[k, f]
            q.append(x)
            high_part = pltpu.roll(x_ref[f, k, :, LANES : 2 * LANES], LANES - 1, 1)
            jp.append(jnp.where(lane == LANES - 1, high_part, pltpu.roll(x, LANES - 1, 1)))
            opposite = flips[f] * moved(across_ref[number], -start)
            jm.append(jnp.where(lane == 0, opposite, pltpu.roll(x, 1, 1)))
            sides = moved(edge_ref[number], -start)
            before = jnp.where(lane1 < plan.full, sides[0:1], befores[f][k : k + 1])
            after = jnp.where(lane1 < plan.full, sides[1:2], afters[f][k : k + 1])
            up, down = turned(x, row, before, after)
            tp.append(up)
            tm.append(down)
            kp.append(state[k + 1, f] if k + 1 < planes else zero)
            km.append(state[k - 1, f] if k > 0 else zero)
        result = advance(coef, q, jp, jm, tp, tm, kp, km)
        for f in range(plan.fields):
            done[k, f] = result[f]
    for copy in stores:
        copy.wait()


def inner(plan, coef, parts, fields, own, sides, rest, part):
    inside = pl.BlockSpec(memory_space=pltpu.VMEM)
    f32 = jnp.float32
    return pl.pallas_call(
        functools.partial(inner_kernel, plan),
        in_specs=[inside] * 12,
        out_specs=[pl.BlockSpec(memory_space=pl.ANY), inside, inside],
        out_shape=[
            jax.ShapeDtypeStruct(fields.shape, f32),
            jax.ShapeDtypeStruct((plan.planes, plan.fields, plan.theta, LANES), f32),
            jax.ShapeDtypeStruct((2, *part.shape[1:]), f32),
        ],
        scratch_shapes=[
            pltpu.VMEM(part.shape, f32),
            pltpu.VMEM((plan.planes, plan.fields, plan.theta, LANES), f32),
            pltpu.SemaphoreType.DMA((plan.planes,)),
        ],
        compiler_params=pltpu.CompilerParams(vmem_limit_bytes=VMEM_LIMIT),
        name="inner",
        cost_estimate=pl.CostEstimate(flops=6000000, bytes_accessed=2500000, transcendentals=0),
    )(coef, *parts, fields, *own, *sides, rest, part)


def finish_kernel(plan, near_ref, far_ref, own_a, own_b, ax_a, ax_b, other_ref, out_ref, ends, sems):
    del other_ref
    planes = plan.planes
    copies = [
        pltpu.make_async_copy(near_ref.at[k], out_ref.at[:, k, :, pl.ds(0, LANES)], sems.at[k])
        for k in range(1, planes - 1)
    ]
    for copy in copies:
        copy.start()
    even_plane = lax.axis_index("ax") % 2 == 0
    nu_dt = viscosity * time_step
    half = 0.5 * time_step
    for tile in range(plan.radial // LANES):
        here = slice(tile * LANES, (tile + 1) * LANES)
        there = slice((tile - 1) * LANES, tile * LANES)
        sent_a = own_a[2, :, here]
        if tile == 0:
            sent_b = own_b[2]
            factor_low = nu_dt + half * jnp.where(even_plane, sent_b, sent_a)
            factor_high = nu_dt - half * jnp.where(even_plane, sent_a, sent_b)
        else:
            factor_low = nu_dt + half * sent_a
            factor_high = nu_dt - half * sent_a
        for f in range(plan.fields):
            b = ax_b[f] if tile == 0 else 0.0
            below, above = slabs_beside(ax_a[f, :, here], b)
            low = near_ref[0, f] if tile == 0 else far_ref[0, f, :, there]
            high = near_ref[planes - 1, f] if tile == 0 else far_ref[1, f, :, there]
            ends[0, f, :, here] = low + factor_low * below
            ends[1, f, :, here] = high + factor_high * above
    for end, k in ((0, 0), (1, planes - 1)):
        copies.append(pltpu.make_async_copy(ends.at[end], out_ref.at[:, k], sems.at[k]))
        copies[-1].start()
    for copy in copies:
        copy.wait()


def finish(plan, near, far, sent, messages, partial):
    anywhere = pl.BlockSpec(memory_space=pl.ANY)
    inside = pl.BlockSpec(memory_space=pltpu.VMEM)
    return pl.pallas_call(
        functools.partial(finish_kernel, plan),
        in_specs=[inside] * 6 + [anywhere],
        out_specs=anywhere,
        out_shape=jax.ShapeDtypeStruct(partial.shape, jnp.float32),
        input_output_aliases={6: 0},
        scratch_shapes=[
            pltpu.VMEM((2, plan.fields, plan.theta, plan.radial), jnp.float32),
            pltpu.SemaphoreType.DMA((plan.planes,)),
        ],
        compiler_params=pltpu.CompilerParams(vmem_limit_bytes=VMEM_LIMIT),
        name="finish",
        cost_estimate=pl.CostEstimate(flops=100000, bytes_accessed=1500000, transcendentals=0),
    )(near, far, *sent, *messages, partial)


def pairs(count, start):
    route = []
    for low in range(start, count, 2):
        high = (low + 1) % count
        route += [(low, high), (high, low)]
    return route


def fast_on_device(fields):
    sectors = lax.axis_size("az")
    slabs = lax.axis_size("ax")
    plan = Plan(fields.shape, sectors)
    coef = jnp.asarray(plan.coefficients())

    def send(x, distance):
        return lax.ppermute(x, "az", [(i, i ^ distance) for i in range(sectors)])

    packed, wide, rest = pack(plan, fields)
    rest_message = lax.ppermute(rest, "ax", pairs(slabs, 1))
    half = sectors // 2
    pieces = [None] * sectors
    pieces[0] = packed
    far = send(packed, half)
    pieces[half] = far
    for p in range(half - 1, 0, -1):
        pieces[p] = send(wide if p == 1 else packed, p)
    part, token = outer(plan, coef, fields)
    onward = gate(far, token)
    for p in range(half - 1, 0, -1):
        pieces[half + p] = send(onward, p)
    pieces[half] = onward
    early = early_spectra(plan, pieces[: half + 1], rest_message)
    column = edges(plan, fields, early[1])
    sides = (pieces[1], lax.ppermute(column, "az", pairs(sectors, 1)))
    *parts, message_a, message_b = filtered(plan, fields, pieces[half + 1 :], early)
    messages = (
        lax.ppermute(message_a, "ax", pairs(slabs, 0)),
        lax.ppermute(message_b, "ax", pairs(slabs, 1)),
    )
    own = (wide, column)
    partial, near, ends = inner(plan, coef, parts, fields, own, sides, rest_message, part)
    return finish(plan, near, ends, (message_a, message_b), messages, partial)


def on_device(fields):
    total_theta = fields.shape[2] * lax.axis_size("az")
    if Plan.fits(fields.shape, lax.axis_size("az"), lax.axis_size("ax"), total_theta):
        return fast_on_device(fields)
    return general_on_device(fields)


def solution(mesh):
    placed = (P(None, "ax", "az", None),)
    return jax.shard_map(
        on_device, mesh=mesh, in_specs=placed, out_specs=P(None, "ax", "az", None), check_vma=False
    )
```

```python
import functools

import jax
import jax.numpy as jnp
import numpy as np
from jax import lax
from jax.experimental import pallas as pl
from jax.experimental.pallas import tpu as pltpu
from jax.sharding import PartitionSpec as P

NEAR = 40


viscosity = 0.2
time_step = 0.1
buoyancy = 1.0

LANES = 128
VMEM_LIMIT = 16 * 1024 * 1024


def swapped(block, axis, distance):
    count = lax.axis_size(axis)
    route = []
    for low in range(count):
        high = low | 1 << distance
        if high != low and high < count:
            route += [(low, high), (high, low)]
    return lax.ppermute(block, axis, route)


def with_halo(block, sides, width, periodic):
    for axis, dim in sides:
        count = lax.axis_size(axis)
        forward = [(i, i + 1) for i in range(count - 1)]
        if periodic:
            forward.append((count - 1, 0))
        backward = [(target, source) for source, target in forward]
        low = lax.ppermute(
            lax.slice_in_dim(block, block.shape[dim] - width, None, axis=dim), axis, forward
        )
        high = lax.ppermute(lax.slice_in_dim(block, 0, width, axis=dim), axis, backward)
        block = jnp.concatenate([low, block, high], axis=dim)
    return block


def mode_tables(theta_index, total_theta, modes):
    column = jnp.arange(modes, dtype=jnp.int32)
    product = theta_index[:, None] * column[None, :] % total_theta
    angle = product.astype(jnp.float32) * (2.0 * jnp.pi / total_theta)
    cosine = jnp.cos(angle)
    sine = jnp.sin(angle)
    weight = jnp.where(column == 0, 1.0, 2.0).astype(jnp.float32) / total_theta
    forward = jnp.concatenate([cosine * weight[None, :], sine * (2.0 / total_theta)], axis=1)
    inverse = jnp.concatenate([cosine, sine], axis=1)
    return (forward, inverse)


def cycle_mask(cycles, modes):
    cycle_index = jnp.arange(cycles, dtype=jnp.int32)
    cutoff = jnp.minimum(355 * (2 * cycle_index + 1) // 226, modes - 1)
    column = jnp.arange(modes, dtype=jnp.int32)
    keep = (column[None, :] <= cutoff[:, None]).astype(jnp.float32)
    return jnp.concatenate([keep, keep], axis=1)


def operators(
    center, radial_plus, radial_minus, theta_plus, theta_minus, axial_plus, axial_minus, total_theta
):
    radius = jnp.arange(center.shape[-1], dtype=jnp.float32) + 0.5
    step_angle = 2.0 * jnp.pi / total_theta
    d_radial = (radial_plus - radial_minus) * 0.5
    d_theta = (theta_plus - theta_minus) / (2.0 * step_angle)
    d_axial = (axial_plus - axial_minus) * 0.5
    laplace = (
        radial_plus - 2.0 * center + radial_minus + (radial_plus - radial_minus) / (2.0 * radius)
    )
    laplace = laplace + (theta_plus - 2.0 * center + theta_minus) / (
        radius * radius * step_angle * step_angle
    )
    laplace = laplace + axial_plus - 2.0 * center + axial_minus
    return (d_radial, d_theta, d_axial, laplace)


def general_on_device(fields):
    count_fields, planes, theta_dev, radial = fields.shape
    sectors = lax.axis_size("az")
    total_theta = theta_dev * sectors
    modes = min(128, total_theta // 2)
    sector = lax.axis_index("az")
    own_index = sector * theta_dev + jnp.arange(theta_dev, dtype=jnp.int32)
    own_forward, own_inverse = mode_tables(own_index, total_theta, modes)
    inner_cycles = fields[:, :, :, :NEAR]
    kept = None
    piece = lax.all_gather(inner_cycles, "az", axis=2, tiled=True)
    piece_index = jnp.arange(piece.shape[2], dtype=jnp.int32)
    piece_forward, unused_inverse = mode_tables(piece_index, total_theta, modes)
    spectra = jnp.einsum("fztj,tc->fzjc", piece, piece_forward, precision=lax.Precision.HIGHEST)
    kept = spectra * cycle_mask(NEAR, modes)[None, None]
    smoothed = jnp.einsum("fzjc,tc->fztj", kept, own_inverse, precision=lax.Precision.HIGHEST)
    state = jnp.concatenate([smoothed, fields[:, :, :, NEAR:]], axis=3)
    flip = jnp.array([-1.0, -1.0, 1.0, 1.0, 1.0], dtype=jnp.float32)[:, None, None]
    top_bit = sectors.bit_length() - 1
    opposite = swapped(state[:, :, :, 0], "az", top_bit - 1)
    opposite = opposite * flip
    theta_padded = with_halo(state, (("az", 2),), 1, True)
    axial_padded = with_halo(state, (("ax", 1),), 1, False)
    radial_plus = jnp.concatenate([state[:, :, :, 1:], jnp.zeros_like(state[:, :, :, :1])], axis=3)
    radial_minus = jnp.concatenate([opposite[:, :, :, None], state[:, :, :, :-1]], axis=3)
    d_radial, d_theta, d_axial, laplace = operators(
        state,
        radial_plus,
        radial_minus,
        theta_padded[:, :, 2:, :],
        theta_padded[:, :, :-2, :],
        axial_padded[:, 2:, :, :],
        axial_padded[:, :-2, :, :],
        total_theta,
    )
    radius = jnp.arange(radial, dtype=jnp.float32) + 0.5
    radial_u = state[0]
    theta_u = state[1]
    axial_u = state[2]
    change = (
        -(radial_u[None] * d_radial + (theta_u / radius)[None] * d_theta + axial_u[None] * d_axial)
        + viscosity * laplace
    )
    inverse_square = 1.0 / (radius * radius)
    first = (
        change[0]
        + theta_u * theta_u / radius
        - viscosity * (radial_u * inverse_square + 2.0 * inverse_square * d_theta[1])
    )
    second = (
        change[1]
        - radial_u * theta_u / radius
        - viscosity * (theta_u * inverse_square - 2.0 * inverse_square * d_theta[0])
    )
    third = change[2] + buoyancy * state[3]
    change = jnp.concatenate([first[None], second[None], third[None], change[3:]], axis=0)
    return state + time_step * change


class Plan:
    def __init__(self, shape, sectors):
        self.fields, self.planes, self.theta, self.radial = shape
        self.sectors = sectors
        self.total = self.theta * sectors
        self.modes = min(128, self.total // 2)
        cycle = np.arange(NEAR)
        self.cut = np.minimum(355 * (2 * cycle + 1) // 226, self.modes - 1)
        self.full = int(np.sum(self.cut < self.modes - 1))
        self.rest = NEAR - self.full
        self.beside = LANES // max(self.full, 1)
        self.groups = -(-self.fields * self.planes // self.beside)
        self.spare = LANES - self.beside * self.full
        self.chunks = -(-self.fields * self.rest // max(self.spare, 1))
        self.early = tuple(range(sectors // 2 + 1))
        self.late = tuple(range(sectors // 2 + 1, sectors))
        self.depth = 256

    def place(self, f, k):
        index = k * self.fields + f
        return index // self.beside, index % self.beside * self.full

    @staticmethod
    def fits(shape, sectors, slabs, total):
        if sectors & (sectors - 1) or total // 2 > 128 or total != LANES or shape[2] != 16:
            return False
        plan = Plan(shape, sectors)
        return (
            plan.full > 0
            and plan.fields == 5
            and plan.planes == plan.theta
            and plan.rest * plan.fields <= LANES
            and plan.groups % 2 == 0
            and plan.spare > 0
            and plan.chunks <= plan.groups
            and slabs % 2 == 0
            and 3 * len(plan.early) * plan.theta <= plan.depth
            and plan.radial % LANES == 0
            and plan.radial > 2 * LANES
        )

    def split(self, table):
        high = table.astype(jnp.bfloat16)
        low = (table - high.astype(np.float32)).astype(jnp.bfloat16)
        return np.concatenate([high, high, low], axis=-1)

    def forward(self, pieces):
        theta = np.arange(self.total)
        mode = np.arange(self.modes)
        angle = (np.outer(mode, theta) % self.total) * (2.0 * np.pi / self.total)
        weight = np.where(mode == 0, 1.0, 2.0)[:, None] / self.total
        table = np.concatenate([np.cos(angle) * weight, np.sin(angle) * 2.0 / self.total], axis=0)
        table = table.astype(np.float32).reshape(2 * self.modes, self.sectors, self.theta)
        blocks = []
        for sector in range(self.sectors):
            chosen = np.concatenate([table[:, sector ^ p] for p in pieces], axis=1)
            chosen = self.split(chosen)
            pad = np.zeros((chosen.shape[0], self.depth - chosen.shape[1]), chosen.dtype)
            blocks.append(np.concatenate([chosen, pad], axis=1))
        return np.stack(blocks)

    def inverse(self):
        mode = np.arange(self.modes)
        blocks = []
        for sector in range(self.sectors):
            own = sector * self.theta + np.arange(self.theta)
            index = np.concatenate([own, own + self.total // 2, own[:1] - 1, own[-1:] + 1])
            angle = (np.outer(index, mode) % self.total) * (2.0 * np.pi / self.total)
            table = np.concatenate([np.cos(angle), np.sin(angle)], axis=1)
            pad = np.zeros((16 - 2, table.shape[1]))
            blocks.append(np.concatenate([table, pad], axis=0))
        return self.split(np.stack(blocks).astype(np.float32))

    def mask(self):
        mode = np.arange(self.modes)
        keep = np.zeros((self.modes, LANES), np.float32)
        for i in range(self.beside):
            keep[:, i * self.full : (i + 1) * self.full] = (
                mode[:, None] <= self.cut[None, : self.full]
            )
        return np.concatenate([keep, keep], axis=0)

    def coefficients(self):
        radius = np.arange(self.radial) + 0.5
        step = 2.0 * np.pi / self.total
        nu_dt = viscosity * time_step
        square = 1.0 / (radius * radius * step * step)
        rows = [
            1.0 - nu_dt * (4.0 + 2.0 * square),
            nu_dt * square,
            nu_dt / (2.0 * radius),
            time_step / (2.0 * step * radius),
            time_step / radius,
            nu_dt / (radius * radius),
            nu_dt / (step * radius * radius),
        ]
        rows.append(np.zeros(self.radial))
        return np.stack(rows).astype(np.float32)


def moved(x, lanes):
    return x if lanes % LANES == 0 else pltpu.roll(x, lanes % LANES, 1)


def pick_columns(plan, x_ref, keep_high, ref, base):
    last = plan.theta - 1
    tiles = plan.radial // LANES
    for f in range(plan.fields):
        for k in range(plan.planes):
            for tile in range(tiles):
                here = slice(tile * LANES, (tile + 1) * LANES)
                low = x_ref[f, k, 0:1, here]
                high = x_ref[f, k, last : last + 1, here]
                ref[base + f * tiles + tile, k : k + 1, :] = jnp.where(keep_high, high, low)


def pack_kernel(plan, x_ref, out_ref, wide_ref, rest_b):
    odd_plane = lax.axis_index("ax") % 2
    rest_b[...] = x_ref[:, odd_plane * (plan.planes - 1), :, LANES:]
    shape = (plan.theta, LANES)
    lane = lax.broadcasted_iota(jnp.int32, shape, 1)
    row = lax.broadcasted_iota(jnp.int32, shape, 0)
    sign = (1 - 2 * (row & 1)).astype(jnp.float32)
    group = jnp.zeros(shape, jnp.float32)
    sums = [jnp.zeros(shape, jnp.float32) for _ in range(plan.fields)]
    for k in range(plan.planes):
        for f in range(plan.fields):
            x = x_ref[f, k, :, :LANES]
            number, first = plan.place(f, k)
            part = moved(x, first)
            if first:
                part = jnp.where((lane >= first) & (lane < first + plan.full), part, group)
            group = part
            if first // plan.full == plan.beside - 1 or (f, k) == (plan.fields - 1, plan.planes - 1):
                out_ref[number] = group
                if number >= plan.chunks:
                    wide_ref[number] = group
            alternating = jnp.sum(x * sign, axis=0, keepdims=True)
            sums[f] = jnp.where(row == k, alternating, sums[f])
    last = sums[0]
    for f in range(plan.fields):
        start = f * plan.rest
        last = jnp.where(lane >= start, moved(sums[f], start - plan.full), last)
    for c in range(plan.chunks):
        start = LANES - plan.spare
        group = jnp.where(lane >= start, moved(last, start - plan.spare * c), out_ref[c])
        out_ref[c] = group
        wide_ref[c] = group
    even_theta = lax.axis_index("az") % 2 == 0
    pick_columns(plan, x_ref, even_theta, wide_ref, plan.groups)


def pack(plan, fields):
    f32 = jnp.float32
    columns = plan.fields * plan.radial // LANES
    plane = jax.ShapeDtypeStruct((plan.fields, plan.theta, plan.radial - LANES), f32)
    inside = pl.BlockSpec(memory_space=pltpu.VMEM)
    return pl.pallas_call(
        functools.partial(pack_kernel, plan),
        in_specs=[inside],
        out_specs=[inside] * 3,
        out_shape=[
            jax.ShapeDtypeStruct((plan.groups, plan.theta, LANES), f32),
            jax.ShapeDtypeStruct((plan.groups + columns, plan.theta, LANES), f32),
            plane,
        ],
        compiler_params=pltpu.CompilerParams(vmem_limit_bytes=VMEM_LIMIT),
        name="pack",
        cost_estimate=pl.CostEstimate(flops=1000000, bytes_accessed=800000, transcendentals=0),
    )(fields)


def edges_kernel(plan, x_ref, after_ref, az_b, rest_a):
    del after_ref
    even_plane = 1 - lax.axis_index("ax") % 2
    rest_a[...] = x_ref[:, even_plane * (plan.planes - 1), :, LANES:]
    even_theta = lax.axis_index("az") % 2 == 0
    pick_columns(plan, x_ref, jnp.logical_not(even_theta), az_b, 0)


def edges(plan, fields, after):
    f32 = jnp.float32
    columns = plan.fields * plan.radial // LANES
    inside = pl.BlockSpec(memory_space=pltpu.VMEM)
    return pl.pallas_call(
        functools.partial(edges_kernel, plan),
        in_specs=[inside] * 2,
        out_specs=[inside] * 2,
        out_shape=[
            jax.ShapeDtypeStruct((columns, plan.theta, LANES), f32),
            jax.ShapeDtypeStruct((plan.fields, plan.theta, plan.radial - LANES), f32),
        ],
        compiler_params=pltpu.CompilerParams(vmem_limit_bytes=VMEM_LIMIT),
        name="edges",
        cost_estimate=pl.CostEstimate(flops=0, bytes_accessed=1000000, transcendentals=0),
    )(fields, after)


def advance(coef, q, jp, jm, tp, tm, kp, km):
    c0, c2, half, angular, over, square, cross = coef
    ur, ut, uz, temp = q[:4]
    radial = half - (0.5 * time_step) * ur
    azimuthal = angular * ut
    axial = (0.5 * time_step) * uz
    nu_dt = viscosity * time_step
    out = []
    d_theta = []
    for f in range(5):
        dt = tp[f] - tm[f]
        if f < 2:
            d_theta.append(dt)
        value = c0 * q[f] + nu_dt * ((jp[f] + jm[f]) + (kp[f] + km[f]))
        value = value + c2 * (tp[f] + tm[f])
        value = value + (jp[f] - jm[f]) * radial
        value = value - dt * azimuthal
        value = value - (kp[f] - km[f]) * axial
        out.append(value)
    swirl = over * ut
    out[0] = out[0] + swirl * ut - square * ur - cross * d_theta[1]
    out[1] = out[1] - swirl * ur - square * ut + cross * d_theta[0]
    out[2] = out[2] + (time_step * buoyancy) * temp
    return out


def turned(x, row, before, after):
    last = x.shape[0] - 1
    up = jnp.where(row == last, after, pltpu.roll(x, last, 0))
    down = jnp.where(row == 0, before, pltpu.roll(x, 1, 0))
    return up, down


def outer_kernel(plan, coef_ref, x_ref, done, token):
    planes = plan.planes
    tiles = plan.radial // LANES
    token[...] = jnp.zeros_like(token)
    shape = (plan.theta, LANES)
    lane = lax.broadcasted_iota(jnp.int32, shape, 1)
    row = lax.broadcasted_iota(jnp.int32, shape, 0)

    def step(group, carry):
        start = pl.multiple_of(group * 4, 4)
        for i in range(4):
            k = start + i
            for tile in range(1, tiles):
                here = pl.ds(tile * LANES, LANES)
                coef = [coef_ref[j : j + 1, here] for j in range(7)]
                q, jp, jm, tp, tm, kp, km = ([] for _ in range(7))
                for f in range(plan.fields):
                    x = x_ref[f, k, :, here]
                    low = x_ref[f, k, :, pl.ds((tile - 1) * LANES, LANES)]
                    q.append(x)
                    high = 0.0
                    if tile + 1 < tiles:
                        high = x_ref[f, k, :, pl.ds((tile + 1) * LANES, LANES)]
                        high = pltpu.roll(high, LANES - 1, 1)
                    jp.append(jnp.where(lane == LANES - 1, high, pltpu.roll(x, LANES - 1, 1)))
                    jm.append(jnp.where(lane == 0, pltpu.roll(low, 1, 1), pltpu.roll(x, 1, 1)))
                    up, down = turned(x, row, 0.0, 0.0)
                    tp.append(up)
                    tm.append(down)
                    if i < 3:
                        above = x_ref[f, k + 1, :, here]
                    else:
                        above = x_ref[f, jnp.minimum(k + 1, planes - 1), :, here]
                        above = jnp.where(k == planes - 1, 0.0, above)
                    if i > 0:
                        below = x_ref[f, k - 1, :, here]
                    else:
                        below = x_ref[f, jnp.maximum(k - 1, 0), :, here]
                        below = jnp.where(k == 0, 0.0, below)
                    kp.append(above)
                    km.append(below)
                result = advance(coef, q, jp, jm, tp, tm, kp, km)
                for f in range(plan.fields):
                    done[k, f, :, pl.ds((tile - 1) * LANES, LANES)] = result[f]
        return carry

    lax.fori_loop(0, planes // 4, step, 0)


def outer(plan, coef, fields):
    inside = pl.BlockSpec(memory_space=pltpu.VMEM)
    f32 = jnp.float32
    return pl.pallas_call(
        functools.partial(outer_kernel, plan),
        in_specs=[inside] * 2,
        out_specs=[inside] * 2,
        out_shape=[
            jax.ShapeDtypeStruct((plan.planes, plan.fields, plan.theta, plan.radial - LANES), f32),
            jax.ShapeDtypeStruct((8, LANES), f32),
        ],
        compiler_params=pltpu.CompilerParams(vmem_limit_bytes=VMEM_LIMIT),
        name="outer",
        cost_estimate=pl.CostEstimate(flops=16000000, bytes_accessed=5000000, transcendentals=0),
    )(coef, fields)


def slabs_beside(a, b):
    slab = lax.axis_index("ax")
    even_plane = slab % 2 == 0
    b = jnp.where((slab > 0) & (slab < lax.axis_size("ax") - 1), b, 0.0)
    return jnp.where(even_plane, b, a), jnp.where(even_plane, a, b)


def seams(plan, coef_ref, x_ref, own_a, own_b, az_a, az_b, ax_a, ax_b, part_ref, done, terms, store):
    nu_dt = viscosity * time_step
    half = 0.5 * time_step
    planes = plan.planes
    tiles = plan.radial // LANES
    base = plan.groups
    even_theta = lax.axis_index("az") % 2 == 0
    last = plan.theta - 1
    row = lax.broadcasted_iota(jnp.int32, (plan.theta, LANES), 0)
    for tile in range(1, tiles):
        here = slice(tile * LANES, (tile + 1) * LANES)
        c2 = coef_ref[1:2, here]
        angular = coef_ref[3:4, here]
        cross = coef_ref[6:7, here]
        number = tiles + tile
        mine_a = own_a[base + number]
        mine_b = own_b[number]
        turn_low = angular * jnp.where(even_theta, mine_b, mine_a)
        turn_high = angular * jnp.where(even_theta, mine_a, mine_b)
        before = []
        after = []
        for f in range(plan.fields):
            a = az_a[base + f * tiles + tile]
            b = az_b[f * tiles + tile]
            before.append(jnp.where(even_theta, b, a))
            after.append(jnp.where(even_theta, a, b))
        for f in range(plan.fields):
            low = (c2 + turn_low) * before[f]
            high = (c2 - turn_high) * after[f]
            if f == 0:
                low = low + cross * before[1]
                high = high - cross * after[1]
            if f == 1:
                low = low - cross * before[0]
                high = high + cross * after[0]
            terms[0, f * tiles + tile] = low
            terms[1, f * tiles + tile] = high
    for k in range(planes):
        for f in range(plan.fields):
            for tile in range(1, tiles):
                here = slice(tile * LANES, (tile + 1) * LANES)
                there = slice((tile - 1) * LANES, tile * LANES)
                value = part_ref[k, f, :, there]
                value = value + jnp.where(row == 0, terms[0, f * tiles + tile, k : k + 1], 0.0)
                value = value + jnp.where(row == last, terms[1, f * tiles + tile, k : k + 1], 0.0)
                if k in (0, planes - 1):
                    below, above = slabs_beside(ax_a[f, :, there], ax_b[f, :, there])
                    if k == 0:
                        value = value + (nu_dt + half * x_ref[2, k, :, here]) * below
                    else:
                        value = value + (nu_dt - half * x_ref[2, k, :, here]) * above
                done[k, f, :, there] = value
        store(k).start()


def gate_kernel(x_ref, token_ref, out_ref):
    del token_ref
    out_ref[...] = x_ref[...]


def gate(x, token):
    inside = pl.BlockSpec(memory_space=pltpu.VMEM)
    return pl.pallas_call(
        gate_kernel,
        in_specs=[inside] * 2,
        out_specs=inside,
        out_shape=jax.ShapeDtypeStruct(x.shape, x.dtype),
        compiler_params=pltpu.CompilerParams(vmem_limit_bytes=VMEM_LIMIT),
        name="gate",
    )(x, token)


def halves(x, depth=None):
    high = x.astype(jnp.bfloat16)
    low = (x - high.astype(jnp.float32)).astype(jnp.bfloat16)
    parts = [high, low, high]
    if depth is not None:
        parts.append(jnp.zeros((depth - 3 * x.shape[0], x.shape[1]), jnp.bfloat16))
    return jnp.concatenate(parts, axis=0)


def two_groups(pieces, g):
    return jnp.concatenate(
        [jnp.concatenate([piece[g + i] for piece in pieces], axis=0) for i in range(2)], axis=1
    )


def alternating_sums(plan, pieces):
    lane = lax.broadcasted_iota(jnp.int32, (plan.theta, LANES), 1)
    total = jnp.zeros((plan.theta, LANES), jnp.float32)
    for c in range(plan.chunks):
        value = pieces[0][c]
        for piece in pieces[1:]:
            value = value + piece[c]
        start = plan.spare * c
        here = (lane >= start) & (lane < start + plan.spare)
        total = jnp.where(here, moved(value, start + plan.spare - LANES), total)
    return total


def early_kernel(plan, forward_ref, after_ref, *refs):
    del after_ref
    pieces = refs[: len(plan.early)]
    spectra_ref, total_ref = refs[len(plan.early) :]
    table = forward_ref[lax.axis_index("az")]
    for g in range(0, plan.groups, 2):
        both = halves(two_groups(pieces, g), plan.depth)
        spectra_ref[g // 2] = jnp.dot(table, both, preferred_element_type=jnp.float32)
    total_ref[...] = alternating_sums(plan, pieces)


def early_spectra(plan, pieces, after):
    inside = pl.BlockSpec(memory_space=pltpu.VMEM)
    f32 = jnp.float32
    return pl.pallas_call(
        functools.partial(early_kernel, plan),
        in_specs=[inside] * (2 + len(pieces)),
        out_specs=[inside] * 2,
        out_shape=[
            jax.ShapeDtypeStruct((plan.groups // 2, 2 * plan.modes, 2 * LANES), f32),
            jax.ShapeDtypeStruct((plan.theta, LANES), f32),
        ],
        compiler_params=pltpu.CompilerParams(vmem_limit_bytes=VMEM_LIMIT),
        name="early",
        cost_estimate=pl.CostEstimate(flops=200000000, bytes_accessed=1500000, transcendentals=0),
    )(jnp.asarray(plan.forward(plan.early)), after, *pieces)


def filter_kernel(plan, x_ref, forward_ref, inverse_ref, mask_ref, early_ref, early_total, *refs):
    count = len(plan.late)
    pieces = refs[:count]
    own_ref, across_ref, edge_ref, sums_ref, message_a, message_b = refs[count:]
    odd_plane = lax.axis_index("ax") % 2
    theta = plan.theta
    sector = lax.axis_index("az")
    forward = forward_ref[sector]
    table = inverse_ref[sector]
    mask = mask_ref[...]
    mask = jnp.concatenate([mask, mask], axis=1)

    for g in range(0, plan.groups, 2):
        both = halves(two_groups(pieces, g), plan.depth)
        spectra = early_ref[g // 2] + jnp.dot(forward, both, preferred_element_type=jnp.float32)
        kept = halves(spectra * mask)
        state = jnp.dot(table, kept, preferred_element_type=jnp.float32)
        for i in range(2):
            lanes = slice(i * LANES, (i + 1) * LANES)
            own_ref[g + i] = state[:theta, lanes]
            across_ref[g + i] = state[theta : 2 * theta, lanes]
            edge_ref[g + i] = state[2 * theta : 2 * theta + 8, lanes]

    total = early_total[...] + alternating_sums(plan, pieces)
    total = total * (1.0 / plan.total)
    lane = lax.broadcasted_iota(jnp.int32, (plan.planes, LANES), 1)
    for f in range(plan.fields):
        value = moved(total, plan.full - f * plan.rest)
        sums_ref[f] = jnp.where((lane >= plan.full) & (lane < NEAR), value, 0.0)

    row = lax.broadcasted_iota(jnp.int32, (theta, LANES), 0)
    sign = (1 - 2 * (row & 1)).astype(jnp.float32)

    def message(ref, k):
        for f in range(plan.fields):
            number, first = plan.place(f, k)
            raw = x_ref[f, k, :, :LANES] - sign * sums_ref[f, k : k + 1]
            ref[f, :theta] = jnp.where(lane < plan.full, moved(own_ref[number], -first), raw)

    def both_messages(a, b):
        message(message_a, a)
        message(message_b, b)
        message_b[:, theta:] = jnp.zeros((plan.fields, 8, LANES), jnp.float32)

    pl.when(odd_plane == 1)(lambda: both_messages(0, plan.planes - 1))
    pl.when(odd_plane == 0)(lambda: both_messages(plan.planes - 1, 0))


def filtered(plan, fields, pieces, early):
    inside = pl.BlockSpec(memory_space=pltpu.VMEM)
    f32 = jnp.float32
    cube = jax.ShapeDtypeStruct((plan.groups, plan.theta, LANES), f32)
    plane = jax.ShapeDtypeStruct((plan.fields, plan.theta, LANES), f32)
    return pl.pallas_call(
        functools.partial(filter_kernel, plan),
        in_specs=[inside] * (6 + len(pieces)),
        out_specs=[inside] * 6,
        out_shape=[
            cube,
            cube,
            jax.ShapeDtypeStruct((plan.groups, 8, LANES), f32),
            jax.ShapeDtypeStruct((plan.fields, plan.planes, LANES), f32),
            plane,
            jax.ShapeDtypeStruct((plan.fields, plan.theta + 8, LANES), f32),
        ],
        compiler_params=pltpu.CompilerParams(vmem_limit_bytes=VMEM_LIMIT),
        name="filter",
        cost_estimate=pl.CostEstimate(flops=200000000, bytes_accessed=1500000, transcendentals=0),
    )(
        fields,
        jnp.asarray(plan.forward(plan.late)),
        jnp.asarray(plan.inverse()),
        jnp.asarray(plan.mask()),
        *early,
        *pieces,
    )


def inner_kernel(
    plan, coef_ref, own_ref, across_ref, edge_ref, sums_ref, x_ref, own_a, own_b, az_a, az_b,
    ax_a, ax_b, part_ref, out_ref, done, far_done, terms, state, outs
):
    planes = plan.planes
    beyond = pl.ds(LANES, plan.radial - LANES)

    def store(k):
        return pltpu.make_async_copy(far_done.at[k], out_ref.at[:, k, :, beyond], outs.at[k])

    seams(
        plan, coef_ref, x_ref, own_a, own_b, az_a, az_b, ax_a, ax_b, part_ref, far_done, terms, store
    )
    theta = plan.theta
    tiles = plan.radial // LANES
    shape = (theta, LANES)
    lane = lax.broadcasted_iota(jnp.int32, shape, 1)
    row = lax.broadcasted_iota(jnp.int32, shape, 0)
    sign = (1 - 2 * (row & 1)).astype(jnp.float32)
    lane1 = lax.broadcasted_iota(jnp.int32, (1, LANES), 1)
    first = slice(0, LANES)
    coef = [coef_ref[i : i + 1, first] for i in range(7)]
    flips = (-1.0, -1.0, 1.0, 1.0, 1.0)
    even_theta = lax.axis_index("az") % 2 == 0

    for k in range(planes):
        for f in range(plan.fields):
            number, start = plan.place(f, k)
            state[k, f] = jnp.where(
                lane < plan.full,
                moved(own_ref[number], -start),
                x_ref[f, k, :, first] - sign * sums_ref[f, k : k + 1],
            )

    befores = []
    afters = []
    for f in range(plan.fields):
        a = az_a[plan.groups + f * tiles]
        b = az_b[f * tiles]
        befores.append(jnp.where(even_theta, b, a) + sums_ref[f])
        afters.append(jnp.where(even_theta, a, b) - sums_ref[f])

    zero = jnp.zeros(shape, jnp.float32)
    for k in range(planes):
        q, jp, jm, tp, tm, kp, km = ([] for _ in range(7))
        for f in range(plan.fields):
            number, start = plan.place(f, k)
            x = state[k, f]
            q.append(x)
            high_part = pltpu.roll(x_ref[f, k, :, LANES : 2 * LANES], LANES - 1, 1)
            jp.append(jnp.where(lane == LANES - 1, high_part, pltpu.roll(x, LANES - 1, 1)))
            opposite = flips[f] * moved(across_ref[number], -start)
            jm.append(jnp.where(lane == 0, opposite, pltpu.roll(x, 1, 1)))
            sides = moved(edge_ref[number], -start)
            before = jnp.where(lane1 < plan.full, sides[0:1], befores[f][k : k + 1])
            after = jnp.where(lane1 < plan.full, sides[1:2], afters[f][k : k + 1])
            up, down = turned(x, row, before, after)
            tp.append(up)
            tm.append(down)
            kp.append(state[k + 1, f] if k + 1 < planes else zero)
            km.append(state[k - 1, f] if k > 0 else zero)
        result = advance(coef, q, jp, jm, tp, tm, kp, km)
        for f in range(plan.fields):
            done[k, f] = result[f]
    for k in range(planes):
        store(k).wait()


def inner(plan, coef, parts, fields, own, sides, rests, part):
    inside = pl.BlockSpec(memory_space=pltpu.VMEM)
    f32 = jnp.float32
    return pl.pallas_call(
        functools.partial(inner_kernel, plan),
        in_specs=[inside] * 13,
        out_specs=[pl.BlockSpec(memory_space=pl.ANY), inside],
        out_shape=[
            jax.ShapeDtypeStruct(fields.shape, f32),
            jax.ShapeDtypeStruct((plan.planes, plan.fields, plan.theta, LANES), f32),
        ],
        scratch_shapes=[
            pltpu.VMEM(part.shape, f32),
            pltpu.VMEM((2, plan.fields * plan.radial // LANES, plan.planes, LANES), f32),
            pltpu.VMEM((plan.planes, plan.fields, plan.theta, LANES), f32),
            pltpu.SemaphoreType.DMA((plan.planes,)),
        ],
        compiler_params=pltpu.CompilerParams(vmem_limit_bytes=VMEM_LIMIT),
        name="inner",
        cost_estimate=pl.CostEstimate(flops=6000000, bytes_accessed=2500000, transcendentals=0),
    )(coef, *parts, fields, *own, *sides, *rests, part)


def finish_kernel(plan, near_ref, own_a, own_b, ax_a, ax_b, other_ref, out_ref, ends, sems):
    del other_ref
    planes = plan.planes
    first = pl.ds(0, LANES)
    copies = [
        pltpu.make_async_copy(near_ref.at[k], out_ref.at[:, k, :, first], sems.at[k])
        for k in range(1, planes - 1)
    ]
    for copy in copies:
        copy.start()
    even_plane = lax.axis_index("ax") % 2 == 0
    nu_dt = viscosity * time_step
    half = 0.5 * time_step
    sent_a = own_a[2]
    sent_b = own_b[2, : plan.theta]
    factor_low = nu_dt + half * jnp.where(even_plane, sent_b, sent_a)
    factor_high = nu_dt - half * jnp.where(even_plane, sent_a, sent_b)
    for f in range(plan.fields):
        below, above = slabs_beside(ax_a[f], ax_b[f, : plan.theta])
        ends[0, f] = near_ref[0, f] + factor_low * below
        ends[1, f] = near_ref[planes - 1, f] + factor_high * above
    for end, k in ((0, 0), (1, planes - 1)):
        copies.append(pltpu.make_async_copy(ends.at[end], out_ref.at[:, k, :, first], sems.at[k]))
        copies[-1].start()
    for copy in copies:
        copy.wait()


def finish(plan, near, sent, messages, partial):
    anywhere = pl.BlockSpec(memory_space=pl.ANY)
    inside = pl.BlockSpec(memory_space=pltpu.VMEM)
    return pl.pallas_call(
        functools.partial(finish_kernel, plan),
        in_specs=[inside] * 5 + [anywhere],
        out_specs=anywhere,
        out_shape=jax.ShapeDtypeStruct(partial.shape, jnp.float32),
        input_output_aliases={5: 0},
        scratch_shapes=[
            pltpu.VMEM((2, plan.fields, plan.theta, LANES), jnp.float32),
            pltpu.SemaphoreType.DMA((plan.planes,)),
        ],
        compiler_params=pltpu.CompilerParams(vmem_limit_bytes=VMEM_LIMIT),
        name="finish",
        cost_estimate=pl.CostEstimate(flops=100000, bytes_accessed=1500000, transcendentals=0),
    )(near, *sent, *messages, partial)


def pairs(count, start):
    route = []
    for low in range(start, count, 2):
        high = (low + 1) % count
        route += [(low, high), (high, low)]
    return route


def fast_on_device(fields):
    sectors = lax.axis_size("az")
    slabs = lax.axis_size("ax")
    plan = Plan(fields.shape, sectors)
    coef = jnp.asarray(plan.coefficients())

    def send(x, distance):
        return lax.ppermute(x, "az", [(i, i ^ distance) for i in range(sectors)])

    packed, wide, rest_b = pack(plan, fields)
    rest_b = lax.ppermute(rest_b, "ax", pairs(slabs, 1))
    half = sectors // 2
    pieces = [None] * sectors
    pieces[0] = packed
    far = send(packed, half)
    pieces[half] = far
    for p in range(half - 1, 0, -1):
        pieces[p] = send(wide if p == 1 else packed, p)
    part, token = outer(plan, coef, fields)
    onward = gate(far, token)
    for p in range(half - 1, 0, -1):
        pieces[half + p] = send(onward, p)
    pieces[half] = onward
    early = early_spectra(plan, pieces[: half + 1], rest_b)
    column, rest_a = edges(plan, fields, early[1])
    rests = (lax.ppermute(rest_a, "ax", pairs(slabs, 0)), rest_b)
    sides = (pieces[1], lax.ppermute(column, "az", pairs(sectors, 1)))
    *parts, message_a, message_b = filtered(plan, fields, pieces[half + 1 :], early)
    messages = (
        lax.ppermute(message_a, "ax", pairs(slabs, 0)),
        lax.ppermute(message_b, "ax", pairs(slabs, 1)),
    )
    partial, near = inner(plan, coef, parts, fields, (wide, column), sides, rests, part)
    return finish(plan, near, (message_a, message_b), messages, partial)


def on_device(fields):
    total_theta = fields.shape[2] * lax.axis_size("az")
    if Plan.fits(fields.shape, lax.axis_size("az"), lax.axis_size("ax"), total_theta):
        return fast_on_device(fields)
    return general_on_device(fields)


def solution(mesh):
    placed = (P(None, "ax", "az", None),)
    return jax.shard_map(
        on_device, mesh=mesh, in_specs=placed, out_specs=P(None, "ax", "az", None), check_vma=False
    )
```

```python
import functools

import jax
import jax.numpy as jnp
import numpy as np
from jax import lax
from jax.experimental import pallas as pl
from jax.experimental.pallas import tpu as pltpu
from jax.sharding import PartitionSpec as P

NEAR = 40


viscosity = 0.2
time_step = 0.1
buoyancy = 1.0

LANES = 128
VMEM_LIMIT = 16 * 1024 * 1024


def swapped(block, axis, distance):
    count = lax.axis_size(axis)
    route = []
    for low in range(count):
        high = low | 1 << distance
        if high != low and high < count:
            route += [(low, high), (high, low)]
    return lax.ppermute(block, axis, route)


def with_halo(block, sides, width, periodic):
    for axis, dim in sides:
        count = lax.axis_size(axis)
        forward = [(i, i + 1) for i in range(count - 1)]
        if periodic:
            forward.append((count - 1, 0))
        backward = [(target, source) for source, target in forward]
        low = lax.ppermute(
            lax.slice_in_dim(block, block.shape[dim] - width, None, axis=dim), axis, forward
        )
        high = lax.ppermute(lax.slice_in_dim(block, 0, width, axis=dim), axis, backward)
        block = jnp.concatenate([low, block, high], axis=dim)
    return block


def mode_tables(theta_index, total_theta, modes):
    column = jnp.arange(modes, dtype=jnp.int32)
    product = theta_index[:, None] * column[None, :] % total_theta
    angle = product.astype(jnp.float32) * (2.0 * jnp.pi / total_theta)
    cosine = jnp.cos(angle)
    sine = jnp.sin(angle)
    weight = jnp.where(column == 0, 1.0, 2.0).astype(jnp.float32) / total_theta
    forward = jnp.concatenate([cosine * weight[None, :], sine * (2.0 / total_theta)], axis=1)
    inverse = jnp.concatenate([cosine, sine], axis=1)
    return (forward, inverse)


def cycle_mask(cycles, modes):
    cycle_index = jnp.arange(cycles, dtype=jnp.int32)
    cutoff = jnp.minimum(355 * (2 * cycle_index + 1) // 226, modes - 1)
    column = jnp.arange(modes, dtype=jnp.int32)
    keep = (column[None, :] <= cutoff[:, None]).astype(jnp.float32)
    return jnp.concatenate([keep, keep], axis=1)


def operators(
    center, radial_plus, radial_minus, theta_plus, theta_minus, axial_plus, axial_minus, total_theta
):
    radius = jnp.arange(center.shape[-1], dtype=jnp.float32) + 0.5
    step_angle = 2.0 * jnp.pi / total_theta
    d_radial = (radial_plus - radial_minus) * 0.5
    d_theta = (theta_plus - theta_minus) / (2.0 * step_angle)
    d_axial = (axial_plus - axial_minus) * 0.5
    laplace = (
        radial_plus - 2.0 * center + radial_minus + (radial_plus - radial_minus) / (2.0 * radius)
    )
    laplace = laplace + (theta_plus - 2.0 * center + theta_minus) / (
        radius * radius * step_angle * step_angle
    )
    laplace = laplace + axial_plus - 2.0 * center + axial_minus
    return (d_radial, d_theta, d_axial, laplace)


def general_on_device(fields):
    count_fields, planes, theta_dev, radial = fields.shape
    sectors = lax.axis_size("az")
    total_theta = theta_dev * sectors
    modes = min(128, total_theta // 2)
    sector = lax.axis_index("az")
    own_index = sector * theta_dev + jnp.arange(theta_dev, dtype=jnp.int32)
    own_forward, own_inverse = mode_tables(own_index, total_theta, modes)
    inner_cycles = fields[:, :, :, :NEAR]
    kept = None
    piece = lax.all_gather(inner_cycles, "az", axis=2, tiled=True)
    piece_index = jnp.arange(piece.shape[2], dtype=jnp.int32)
    piece_forward, unused_inverse = mode_tables(piece_index, total_theta, modes)
    spectra = jnp.einsum("fztj,tc->fzjc", piece, piece_forward, precision=lax.Precision.HIGHEST)
    kept = spectra * cycle_mask(NEAR, modes)[None, None]
    smoothed = jnp.einsum("fzjc,tc->fztj", kept, own_inverse, precision=lax.Precision.HIGHEST)
    state = jnp.concatenate([smoothed, fields[:, :, :, NEAR:]], axis=3)
    flip = jnp.array([-1.0, -1.0, 1.0, 1.0, 1.0], dtype=jnp.float32)[:, None, None]
    top_bit = sectors.bit_length() - 1
    opposite = swapped(state[:, :, :, 0], "az", top_bit - 1)
    opposite = opposite * flip
    theta_padded = with_halo(state, (("az", 2),), 1, True)
    axial_padded = with_halo(state, (("ax", 1),), 1, False)
    radial_plus = jnp.concatenate([state[:, :, :, 1:], jnp.zeros_like(state[:, :, :, :1])], axis=3)
    radial_minus = jnp.concatenate([opposite[:, :, :, None], state[:, :, :, :-1]], axis=3)
    d_radial, d_theta, d_axial, laplace = operators(
        state,
        radial_plus,
        radial_minus,
        theta_padded[:, :, 2:, :],
        theta_padded[:, :, :-2, :],
        axial_padded[:, 2:, :, :],
        axial_padded[:, :-2, :, :],
        total_theta,
    )
    radius = jnp.arange(radial, dtype=jnp.float32) + 0.5
    radial_u = state[0]
    theta_u = state[1]
    axial_u = state[2]
    change = (
        -(radial_u[None] * d_radial + (theta_u / radius)[None] * d_theta + axial_u[None] * d_axial)
        + viscosity * laplace
    )
    inverse_square = 1.0 / (radius * radius)
    first = (
        change[0]
        + theta_u * theta_u / radius
        - viscosity * (radial_u * inverse_square + 2.0 * inverse_square * d_theta[1])
    )
    second = (
        change[1]
        - radial_u * theta_u / radius
        - viscosity * (theta_u * inverse_square - 2.0 * inverse_square * d_theta[0])
    )
    third = change[2] + buoyancy * state[3]
    change = jnp.concatenate([first[None], second[None], third[None], change[3:]], axis=0)
    return state + time_step * change


class Plan:
    def __init__(self, shape, sectors):
        self.fields, self.planes, self.theta, self.radial = shape
        self.sectors = sectors
        self.total = self.theta * sectors
        self.modes = min(128, self.total // 2)
        cycle = np.arange(NEAR)
        self.cut = np.minimum(355 * (2 * cycle + 1) // 226, self.modes - 1)
        self.full = int(np.sum(self.cut < self.modes - 1))
        self.rest = NEAR - self.full
        self.beside = LANES // max(self.full, 1)
        self.groups = -(-self.fields * self.planes // self.beside)
        self.spare = LANES - self.beside * self.full
        self.chunks = -(-self.fields * self.rest // max(self.spare, 1))
        self.early = tuple(range(sectors // 2 + 1))
        self.late = tuple(range(sectors // 2 + 1, sectors))
        self.depth = 256

    def place(self, f, k):
        index = k * self.fields + f
        return index // self.beside, index % self.beside * self.full

    @staticmethod
    def fits(shape, sectors, slabs, total):
        if sectors & (sectors - 1) or total // 2 > 128 or total != LANES or shape[2] != 16:
            return False
        plan = Plan(shape, sectors)
        return (
            plan.full > 0
            and plan.fields == 5
            and plan.planes == plan.theta
            and plan.rest * plan.fields <= LANES
            and plan.groups % 2 == 0
            and plan.spare > 0
            and plan.chunks <= plan.groups
            and slabs % 2 == 0
            and 3 * len(plan.early) * plan.theta <= plan.depth
            and plan.radial % LANES == 0
            and plan.radial > 2 * LANES
        )

    def split(self, table):
        high = table.astype(jnp.bfloat16)
        low = (table - high.astype(np.float32)).astype(jnp.bfloat16)
        return np.concatenate([high, high, low], axis=-1)

    def forward(self, pieces):
        theta = np.arange(self.total)
        mode = np.arange(self.modes)
        angle = (np.outer(mode, theta) % self.total) * (2.0 * np.pi / self.total)
        weight = np.where(mode == 0, 1.0, 2.0)[:, None] / self.total
        table = np.concatenate([np.cos(angle) * weight, np.sin(angle) * 2.0 / self.total], axis=0)
        table = table.astype(np.float32).reshape(2 * self.modes, self.sectors, self.theta)
        blocks = []
        for sector in range(self.sectors):
            chosen = np.concatenate([table[:, sector ^ p] for p in pieces], axis=1)
            chosen = self.split(chosen)
            pad = np.zeros((chosen.shape[0], self.depth - chosen.shape[1]), chosen.dtype)
            blocks.append(np.concatenate([chosen, pad], axis=1))
        return np.stack(blocks)

    def inverse(self):
        mode = np.arange(self.modes)
        blocks = []
        for sector in range(self.sectors):
            own = sector * self.theta + np.arange(self.theta)
            index = np.concatenate([own, own + self.total // 2, own[:1] - 1, own[-1:] + 1])
            angle = (np.outer(index, mode) % self.total) * (2.0 * np.pi / self.total)
            table = np.concatenate([np.cos(angle), np.sin(angle)], axis=1)
            pad = np.zeros((16 - 2, table.shape[1]))
            blocks.append(np.concatenate([table, pad], axis=0))
        return self.split(np.stack(blocks).astype(np.float32))

    def mask(self):
        mode = np.arange(self.modes)
        keep = np.zeros((self.modes, LANES), np.float32)
        for i in range(self.beside):
            keep[:, i * self.full : (i + 1) * self.full] = (
                mode[:, None] <= self.cut[None, : self.full]
            )
        return np.concatenate([keep, keep], axis=0)

    def coefficients(self):
        radius = np.arange(self.radial) + 0.5
        step = 2.0 * np.pi / self.total
        nu_dt = viscosity * time_step
        square = 1.0 / (radius * radius * step * step)
        rows = [
            1.0 - nu_dt * (4.0 + 2.0 * square),
            nu_dt * square,
            nu_dt / (2.0 * radius),
            time_step / (2.0 * step * radius),
            time_step / radius,
            nu_dt / (radius * radius),
            nu_dt / (step * radius * radius),
        ]
        rows.append(np.zeros(self.radial))
        return np.stack(rows).astype(np.float32)


def moved(x, lanes):
    return x if lanes % LANES == 0 else pltpu.roll(x, lanes % LANES, 1)


def pick_columns(plan, x_ref, keep_high, ref, base):
    last = plan.theta - 1
    tiles = plan.radial // LANES
    for f in range(plan.fields):
        for k in range(plan.planes):
            for tile in range(tiles):
                here = slice(tile * LANES, (tile + 1) * LANES)
                low = x_ref[f, k, 0:1, here]
                high = x_ref[f, k, last : last + 1, here]
                ref[base + f * tiles + tile, k : k + 1, :] = jnp.where(keep_high, high, low)


def pack_kernel(plan, x_ref, out_ref, wide_ref, rest_b):
    odd_plane = lax.axis_index("ax") % 2
    rest_b[...] = x_ref[:, odd_plane * (plan.planes - 1), :, LANES:]
    shape = (plan.theta, LANES)
    lane = lax.broadcasted_iota(jnp.int32, shape, 1)
    row = lax.broadcasted_iota(jnp.int32, shape, 0)
    sign = (1 - 2 * (row & 1)).astype(jnp.float32)
    group = jnp.zeros(shape, jnp.float32)
    sums = [jnp.zeros(shape, jnp.float32) for _ in range(plan.fields)]
    for k in range(plan.planes):
        for f in range(plan.fields):
            x = x_ref[f, k, :, :LANES]
            number, first = plan.place(f, k)
            part = moved(x, first)
            if first:
                part = jnp.where((lane >= first) & (lane < first + plan.full), part, group)
            group = part
            if first // plan.full == plan.beside - 1 or (f, k) == (plan.fields - 1, plan.planes - 1):
                out_ref[number] = group
                if number >= plan.chunks:
                    wide_ref[number] = group
            alternating = jnp.sum(x * sign, axis=0, keepdims=True)
            sums[f] = jnp.where(row == k, alternating, sums[f])
    last = sums[0]
    for f in range(plan.fields):
        start = f * plan.rest
        last = jnp.where(lane >= start, moved(sums[f], start - plan.full), last)
    for c in range(plan.chunks):
        start = LANES - plan.spare
        group = jnp.where(lane >= start, moved(last, start - plan.spare * c), out_ref[c])
        out_ref[c] = group
        wide_ref[c] = group
    even_theta = lax.axis_index("az") % 2 == 0
    pick_columns(plan, x_ref, even_theta, wide_ref, plan.groups)


def pack(plan, fields):
    f32 = jnp.float32
    columns = plan.fields * plan.radial // LANES
    plane = jax.ShapeDtypeStruct((plan.fields, plan.theta, plan.radial - LANES), f32)
    inside = pl.BlockSpec(memory_space=pltpu.VMEM)
    return pl.pallas_call(
        functools.partial(pack_kernel, plan),
        in_specs=[inside],
        out_specs=[inside] * 3,
        out_shape=[
            jax.ShapeDtypeStruct((plan.groups, plan.theta, LANES), f32),
            jax.ShapeDtypeStruct((plan.groups + columns, plan.theta, LANES), f32),
            plane,
        ],
        compiler_params=pltpu.CompilerParams(vmem_limit_bytes=VMEM_LIMIT),
        name="pack",
        cost_estimate=pl.CostEstimate(flops=1000000, bytes_accessed=800000, transcendentals=0),
    )(fields)


def edges_kernel(plan, x_ref, after_ref, az_b, rest_a):
    del after_ref
    even_plane = 1 - lax.axis_index("ax") % 2
    rest_a[...] = x_ref[:, even_plane * (plan.planes - 1), :, LANES:]
    even_theta = lax.axis_index("az") % 2 == 0
    pick_columns(plan, x_ref, jnp.logical_not(even_theta), az_b, 0)


def edges(plan, fields, after):
    f32 = jnp.float32
    columns = plan.fields * plan.radial // LANES
    inside = pl.BlockSpec(memory_space=pltpu.VMEM)
    return pl.pallas_call(
        functools.partial(edges_kernel, plan),
        in_specs=[inside] * 2,
        out_specs=[inside] * 2,
        out_shape=[
            jax.ShapeDtypeStruct((columns, plan.theta, LANES), f32),
            jax.ShapeDtypeStruct((plan.fields, plan.theta, plan.radial - LANES), f32),
        ],
        compiler_params=pltpu.CompilerParams(vmem_limit_bytes=VMEM_LIMIT),
        name="edges",
        cost_estimate=pl.CostEstimate(flops=0, bytes_accessed=1000000, transcendentals=0),
    )(fields, after)


def advance(coef, q, jp, jm, tp, tm, kp, km):
    c0, c2, half, angular, over, square, cross = coef
    ur, ut, uz, temp = q[:4]
    radial = half - (0.5 * time_step) * ur
    azimuthal = angular * ut
    axial = (0.5 * time_step) * uz
    nu_dt = viscosity * time_step
    out = []
    d_theta = []
    for f in range(5):
        dt = tp[f] - tm[f]
        if f < 2:
            d_theta.append(dt)
        value = c0 * q[f] + nu_dt * ((jp[f] + jm[f]) + (kp[f] + km[f]))
        value = value + c2 * (tp[f] + tm[f])
        value = value + (jp[f] - jm[f]) * radial
        value = value - dt * azimuthal
        value = value - (kp[f] - km[f]) * axial
        out.append(value)
    swirl = over * ut
    out[0] = out[0] + swirl * ut - square * ur - cross * d_theta[1]
    out[1] = out[1] - swirl * ur - square * ut + cross * d_theta[0]
    out[2] = out[2] + (time_step * buoyancy) * temp
    return out


def turned(x, row, before, after):
    last = x.shape[0] - 1
    up = jnp.where(row == last, after, pltpu.roll(x, last, 0))
    down = jnp.where(row == 0, before, pltpu.roll(x, 1, 0))
    return up, down


def outer_kernel(plan, coef_ref, x_ref, done, token):
    planes = plan.planes
    tiles = plan.radial // LANES
    token[...] = jnp.zeros_like(token)
    shape = (plan.theta, LANES)
    lane = lax.broadcasted_iota(jnp.int32, shape, 1)
    row = lax.broadcasted_iota(jnp.int32, shape, 0)

    def step(group, carry):
        start = pl.multiple_of(group * 4, 4)
        for i in range(4):
            k = start + i
            for tile in range(1, tiles):
                here = pl.ds(tile * LANES, LANES)
                coef = [coef_ref[j : j + 1, here] for j in range(7)]
                q, jp, jm, tp, tm, kp, km = ([] for _ in range(7))
                for f in range(plan.fields):
                    x = x_ref[f, k, :, here]
                    low = x_ref[f, k, :, pl.ds((tile - 1) * LANES, LANES)]
                    q.append(x)
                    high = 0.0
                    if tile + 1 < tiles:
                        high = x_ref[f, k, :, pl.ds((tile + 1) * LANES, LANES)]
                        high = pltpu.roll(high, LANES - 1, 1)
                    jp.append(jnp.where(lane == LANES - 1, high, pltpu.roll(x, LANES - 1, 1)))
                    jm.append(jnp.where(lane == 0, pltpu.roll(low, 1, 1), pltpu.roll(x, 1, 1)))
                    up, down = turned(x, row, 0.0, 0.0)
                    tp.append(up)
                    tm.append(down)
                    if i < 3:
                        above = x_ref[f, k + 1, :, here]
                    else:
                        above = x_ref[f, jnp.minimum(k + 1, planes - 1), :, here]
                        above = jnp.where(k == planes - 1, 0.0, above)
                    if i > 0:
                        below = x_ref[f, k - 1, :, here]
                    else:
                        below = x_ref[f, jnp.maximum(k - 1, 0), :, here]
                        below = jnp.where(k == 0, 0.0, below)
                    kp.append(above)
                    km.append(below)
                result = advance(coef, q, jp, jm, tp, tm, kp, km)
                for f in range(plan.fields):
                    done[k, f, :, pl.ds((tile - 1) * LANES, LANES)] = result[f]
        return carry

    lax.fori_loop(0, planes // 4, step, 0)


def outer(plan, coef, fields):
    inside = pl.BlockSpec(memory_space=pltpu.VMEM)
    f32 = jnp.float32
    return pl.pallas_call(
        functools.partial(outer_kernel, plan),
        in_specs=[inside] * 2,
        out_specs=[inside] * 2,
        out_shape=[
            jax.ShapeDtypeStruct((plan.planes, plan.fields, plan.theta, plan.radial - LANES), f32),
            jax.ShapeDtypeStruct((8, LANES), f32),
        ],
        compiler_params=pltpu.CompilerParams(vmem_limit_bytes=VMEM_LIMIT),
        name="outer",
        cost_estimate=pl.CostEstimate(flops=16000000, bytes_accessed=5000000, transcendentals=0),
    )(coef, fields)


def slabs_beside(a, b):
    slab = lax.axis_index("ax")
    even_plane = slab % 2 == 0
    b = jnp.where((slab > 0) & (slab < lax.axis_size("ax") - 1), b, 0.0)
    return jnp.where(even_plane, b, a), jnp.where(even_plane, a, b)


def seams(plan, coef_ref, x_ref, own_a, own_b, az_a, ax_a, ax_b, part_ref, done, terms):
    nu_dt = viscosity * time_step
    half = 0.5 * time_step
    planes = plan.planes
    tiles = plan.radial // LANES
    base = plan.groups
    even_theta = lax.axis_index("az") % 2 == 0
    last = plan.theta - 1
    row = lax.broadcasted_iota(jnp.int32, (plan.theta, LANES), 0)
    for tile in range(1, tiles):
        here = slice(tile * LANES, (tile + 1) * LANES)
        c2 = coef_ref[1:2, here]
        angular = coef_ref[3:4, here]
        cross = coef_ref[6:7, here]
        number = tiles + tile
        mine_a = own_a[base + number]
        mine_b = own_b[number]
        turn_low = angular * jnp.where(even_theta, mine_b, mine_a)
        turn_high = angular * jnp.where(even_theta, mine_a, mine_b)
        before = []
        after = []
        for f in range(plan.fields):
            a = az_a[base + f * tiles + tile]
            before.append(jnp.where(even_theta, 0.0, a))
            after.append(jnp.where(even_theta, a, 0.0))
        for f in range(plan.fields):
            low = (c2 + turn_low) * before[f]
            high = (c2 - turn_high) * after[f]
            if f == 0:
                low = low + cross * before[1]
                high = high - cross * after[1]
            if f == 1:
                low = low - cross * before[0]
                high = high + cross * after[0]
            terms[0, f * tiles + tile] = low
            terms[1, f * tiles + tile] = high
    for k in range(planes):
        for f in range(plan.fields):
            for tile in range(1, tiles):
                here = slice(tile * LANES, (tile + 1) * LANES)
                there = slice((tile - 1) * LANES, tile * LANES)
                value = part_ref[k, f, :, there]
                value = value + jnp.where(row == 0, terms[0, f * tiles + tile, k : k + 1], 0.0)
                value = value + jnp.where(row == last, terms[1, f * tiles + tile, k : k + 1], 0.0)
                if k in (0, planes - 1):
                    below, above = slabs_beside(ax_a[f, :, there], ax_b[f, :, there])
                    if k == 0:
                        value = value + (nu_dt + half * x_ref[2, k, :, here]) * below
                    else:
                        value = value + (nu_dt - half * x_ref[2, k, :, here]) * above
                done[k, f, :, there] = value


def gate_kernel(x_ref, token_ref, out_ref):
    del token_ref
    out_ref[...] = x_ref[...]


def gate(x, token):
    inside = pl.BlockSpec(memory_space=pltpu.VMEM)
    return pl.pallas_call(
        gate_kernel,
        in_specs=[inside] * 2,
        out_specs=inside,
        out_shape=jax.ShapeDtypeStruct(x.shape, x.dtype),
        compiler_params=pltpu.CompilerParams(vmem_limit_bytes=VMEM_LIMIT),
        name="gate",
    )(x, token)


def halves(x, depth=None):
    high = x.astype(jnp.bfloat16)
    low = (x - high.astype(jnp.float32)).astype(jnp.bfloat16)
    parts = [high, low, high]
    if depth is not None:
        parts.append(jnp.zeros((depth - 3 * x.shape[0], x.shape[1]), jnp.bfloat16))
    return jnp.concatenate(parts, axis=0)


def two_groups(pieces, g):
    return jnp.concatenate(
        [jnp.concatenate([piece[g + i] for piece in pieces], axis=0) for i in range(2)], axis=1
    )


def alternating_sums(plan, pieces):
    lane = lax.broadcasted_iota(jnp.int32, (plan.theta, LANES), 1)
    total = jnp.zeros((plan.theta, LANES), jnp.float32)
    for c in range(plan.chunks):
        value = pieces[0][c]
        for piece in pieces[1:]:
            value = value + piece[c]
        start = plan.spare * c
        here = (lane >= start) & (lane < start + plan.spare)
        total = jnp.where(here, moved(value, start + plan.spare - LANES), total)
    return total


def early_kernel(plan, forward_ref, after_ref, *refs):
    del after_ref
    pieces = refs[: len(plan.early)]
    spectra_ref, total_ref = refs[len(plan.early) :]
    table = forward_ref[lax.axis_index("az")]
    for g in range(0, plan.groups, 2):
        both = halves(two_groups(pieces, g), plan.depth)
        spectra_ref[g // 2] = jnp.dot(table, both, preferred_element_type=jnp.float32)
    total_ref[...] = alternating_sums(plan, pieces)


def early_spectra(plan, pieces, after):
    inside = pl.BlockSpec(memory_space=pltpu.VMEM)
    f32 = jnp.float32
    return pl.pallas_call(
        functools.partial(early_kernel, plan),
        in_specs=[inside] * (2 + len(pieces)),
        out_specs=[inside] * 2,
        out_shape=[
            jax.ShapeDtypeStruct((plan.groups // 2, 2 * plan.modes, 2 * LANES), f32),
            jax.ShapeDtypeStruct((plan.theta, LANES), f32),
        ],
        compiler_params=pltpu.CompilerParams(vmem_limit_bytes=VMEM_LIMIT),
        name="early",
        cost_estimate=pl.CostEstimate(flops=200000000, bytes_accessed=1500000, transcendentals=0),
    )(jnp.asarray(plan.forward(plan.early)), after, *pieces)


def filter_kernel(plan, x_ref, forward_ref, inverse_ref, mask_ref, early_ref, early_total, *refs):
    count = len(plan.late)
    pieces = refs[:count]
    own_ref, across_ref, edge_ref, sums_ref, message_a, message_b = refs[count:]
    odd_plane = lax.axis_index("ax") % 2
    theta = plan.theta
    sector = lax.axis_index("az")
    forward = forward_ref[sector]
    table = inverse_ref[sector]
    mask = mask_ref[...]
    mask = jnp.concatenate([mask, mask], axis=1)

    for g in range(0, plan.groups, 2):
        both = halves(two_groups(pieces, g), plan.depth)
        spectra = early_ref[g // 2] + jnp.dot(forward, both, preferred_element_type=jnp.float32)
        kept = halves(spectra * mask)
        state = jnp.dot(table, kept, preferred_element_type=jnp.float32)
        for i in range(2):
            lanes = slice(i * LANES, (i + 1) * LANES)
            own_ref[g + i] = state[:theta, lanes]
            across_ref[g + i] = state[theta : 2 * theta, lanes]
            edge_ref[g + i] = state[2 * theta : 2 * theta + 8, lanes]

    total = early_total[...] + alternating_sums(plan, pieces)
    total = total * (1.0 / plan.total)
    lane = lax.broadcasted_iota(jnp.int32, (plan.planes, LANES), 1)
    for f in range(plan.fields):
        value = moved(total, plan.full - f * plan.rest)
        sums_ref[f] = jnp.where((lane >= plan.full) & (lane < NEAR), value, 0.0)

    row = lax.broadcasted_iota(jnp.int32, (theta, LANES), 0)
    sign = (1 - 2 * (row & 1)).astype(jnp.float32)

    def message(ref, k):
        for f in range(plan.fields):
            number, first = plan.place(f, k)
            raw = x_ref[f, k, :, :LANES] - sign * sums_ref[f, k : k + 1]
            ref[f, :theta] = jnp.where(lane < plan.full, moved(own_ref[number], -first), raw)

    def both_messages(a, b):
        message(message_a, a)
        message(message_b, b)
        message_b[:, theta:] = jnp.zeros((plan.fields, 8, LANES), jnp.float32)

    pl.when(odd_plane == 1)(lambda: both_messages(0, plan.planes - 1))
    pl.when(odd_plane == 0)(lambda: both_messages(plan.planes - 1, 0))


def filtered(plan, fields, pieces, early):
    inside = pl.BlockSpec(memory_space=pltpu.VMEM)
    f32 = jnp.float32
    cube = jax.ShapeDtypeStruct((plan.groups, plan.theta, LANES), f32)
    plane = jax.ShapeDtypeStruct((plan.fields, plan.theta, LANES), f32)
    return pl.pallas_call(
        functools.partial(filter_kernel, plan),
        in_specs=[inside] * (6 + len(pieces)),
        out_specs=[inside] * 6,
        out_shape=[
            cube,
            cube,
            jax.ShapeDtypeStruct((plan.groups, 8, LANES), f32),
            jax.ShapeDtypeStruct((plan.fields, plan.planes, LANES), f32),
            plane,
            jax.ShapeDtypeStruct((plan.fields, plan.theta + 8, LANES), f32),
        ],
        compiler_params=pltpu.CompilerParams(vmem_limit_bytes=VMEM_LIMIT),
        name="filter",
        cost_estimate=pl.CostEstimate(flops=200000000, bytes_accessed=1500000, transcendentals=0),
    )(
        fields,
        jnp.asarray(plan.forward(plan.late)),
        jnp.asarray(plan.inverse()),
        jnp.asarray(plan.mask()),
        *early,
        *pieces,
    )


def inner_kernel(
    plan, coef_ref, own_ref, across_ref, edge_ref, sums_ref, x_ref, own_a, own_b, az_a,
    ax_a, ax_b, part_ref, done, far_done, swirl_ref, terms, state
):
    planes = plan.planes
    seams(plan, coef_ref, x_ref, own_a, own_b, az_a, ax_a, ax_b, part_ref, far_done, terms)
    theta = plan.theta
    tiles = plan.radial // LANES
    shape = (theta, LANES)
    lane = lax.broadcasted_iota(jnp.int32, shape, 1)
    row = lax.broadcasted_iota(jnp.int32, shape, 0)
    sign = (1 - 2 * (row & 1)).astype(jnp.float32)
    lane1 = lax.broadcasted_iota(jnp.int32, (1, LANES), 1)
    first = slice(0, LANES)
    coef = [coef_ref[i : i + 1, first] for i in range(7)]
    flips = (-1.0, -1.0, 1.0, 1.0, 1.0)
    even_theta = lax.axis_index("az") % 2 == 0

    for k in range(planes):
        for f in range(plan.fields):
            number, start = plan.place(f, k)
            state[k, f] = jnp.where(
                lane < plan.full,
                moved(own_ref[number], -start),
                x_ref[f, k, :, first] - sign * sums_ref[f, k : k + 1],
            )

    befores = []
    afters = []
    for f in range(plan.fields):
        a = az_a[plan.groups + f * tiles]
        befores.append(jnp.where(even_theta, 0.0, a) + sums_ref[f])
        afters.append(jnp.where(even_theta, a, 0.0) - sums_ref[f])

    zero = jnp.zeros(shape, jnp.float32)
    for k in range(planes):
        q, jp, jm, tp, tm, kp, km = ([] for _ in range(7))
        for f in range(plan.fields):
            number, start = plan.place(f, k)
            x = state[k, f]
            q.append(x)
            high_part = pltpu.roll(x_ref[f, k, :, LANES : 2 * LANES], LANES - 1, 1)
            jp.append(jnp.where(lane == LANES - 1, high_part, pltpu.roll(x, LANES - 1, 1)))
            opposite = flips[f] * moved(across_ref[number], -start)
            jm.append(jnp.where(lane == 0, opposite, pltpu.roll(x, 1, 1)))
            sides = moved(edge_ref[number], -start)
            before = jnp.where(lane1 < plan.full, sides[0:1], befores[f][k : k + 1])
            after = jnp.where(lane1 < plan.full, sides[1:2], afters[f][k : k + 1])
            up, down = turned(x, row, before, after)
            tp.append(up)
            tm.append(down)
            kp.append(state[k + 1, f] if k + 1 < planes else zero)
            km.append(state[k - 1, f] if k > 0 else zero)
        result = advance(coef, q, jp, jm, tp, tm, kp, km)
        for f in range(plan.fields):
            done[k, f] = result[f]
    for k in range(planes):
        x = state[k, 1]
        swirl_ref[k : k + 1] = jnp.where(even_theta, x[:1], x[theta - 1 :])


def inner(plan, coef, parts, fields, own, side, rests, part):
    inside = pl.BlockSpec(memory_space=pltpu.VMEM)
    f32 = jnp.float32
    return pl.pallas_call(
        functools.partial(inner_kernel, plan),
        in_specs=[inside] * 12,
        out_specs=[inside, inside, inside],
        out_shape=[
            jax.ShapeDtypeStruct((plan.planes, plan.fields, plan.theta, LANES), f32),
            jax.ShapeDtypeStruct(part.shape, f32),
            jax.ShapeDtypeStruct((plan.planes, LANES), f32),
        ],
        scratch_shapes=[
            pltpu.VMEM((2, plan.fields * plan.radial // LANES, plan.planes, LANES), f32),
            pltpu.VMEM((plan.planes, plan.fields, plan.theta, LANES), f32),
        ],
        compiler_params=pltpu.CompilerParams(vmem_limit_bytes=VMEM_LIMIT),
        name="inner",
        cost_estimate=pl.CostEstimate(flops=6000000, bytes_accessed=2500000, transcendentals=0),
    )(coef, *parts, fields, *own, side, *rests, part)


def column_kernel(
    plan, coef_ref, own_b, az_b, near_ref, far_ref, swirl_ref, out_ref, near, far, terms, outs
):
    planes = plan.planes
    tiles = plan.radial // LANES
    even_theta = lax.axis_index("az") % 2 == 0
    sign = jnp.where(even_theta, 1.0, -1.0)
    beyond = pl.ds(LANES, plan.radial - LANES)
    lane = lax.broadcasted_iota(jnp.int32, (planes, LANES), 1)
    for tile in range(tiles):
        here = slice(tile * LANES, (tile + 1) * LANES)
        c2 = coef_ref[1:2, here]
        cross = sign * coef_ref[6:7, here]
        swirl = swirl_ref[...] if tile == 0 else own_b[tiles + tile]
        turn = c2 + sign * coef_ref[3:4, here] * swirl
        column = [az_b[f * tiles + tile] for f in range(plan.fields)]
        if tile == 0:
            column = [jnp.where(lane < plan.full, 0.0, x) for x in column]
        for f in range(plan.fields):
            value = turn * column[f]
            if f == 0:
                value = value + cross * column[1]
            if f == 1:
                value = value - cross * column[0]
            terms[f * tiles + tile] = value
    row = lax.broadcasted_iota(jnp.int32, (plan.theta, LANES), 0)
    edge = jnp.where(even_theta, 0, plan.theta - 1)
    copies = []
    for k in range(planes):
        for f in range(plan.fields):
            for tile in range(1, tiles):
                there = slice((tile - 1) * LANES, tile * LANES)
                term = terms[f * tiles + tile, k : k + 1]
                far[k, f, :, there] = far_ref[k, f, :, there] + jnp.where(row == edge, term, 0.0)
        copies.append(pltpu.make_async_copy(far.at[k], out_ref.at[:, k, :, beyond], outs.at[k]))
        copies[-1].start()
    for k in range(planes):
        for f in range(plan.fields):
            near[k, f] = near_ref[k, f] + jnp.where(
                row == edge, terms[f * tiles, k : k + 1], 0.0
            )
    for copy in copies:
        copy.wait()


def last_column(plan, coef, own, side, near, far, swirl, fields):
    anywhere = pl.BlockSpec(memory_space=pl.ANY)
    inside = pl.BlockSpec(memory_space=pltpu.VMEM)
    f32 = jnp.float32
    return pl.pallas_call(
        functools.partial(column_kernel, plan),
        in_specs=[inside] * 6,
        out_specs=[anywhere, inside],
        out_shape=[
            jax.ShapeDtypeStruct(fields.shape, f32),
            jax.ShapeDtypeStruct(near.shape, f32),
        ],
        scratch_shapes=[
            pltpu.VMEM((plan.planes, plan.fields, plan.theta, plan.radial - LANES), f32),
            pltpu.VMEM((plan.fields * plan.radial // LANES, plan.planes, LANES), f32),
            pltpu.SemaphoreType.DMA((plan.planes,)),
        ],
        compiler_params=pltpu.CompilerParams(vmem_limit_bytes=VMEM_LIMIT),
        name="last_column",
        cost_estimate=pl.CostEstimate(flops=1000000, bytes_accessed=2500000, transcendentals=0),
    )(coef, own, side, near, far, swirl)


def finish_kernel(plan, near_ref, own_a, own_b, ax_a, ax_b, other_ref, out_ref, ends, sems):
    del other_ref
    planes = plan.planes
    first = pl.ds(0, LANES)
    copies = [
        pltpu.make_async_copy(near_ref.at[k], out_ref.at[:, k, :, first], sems.at[k])
        for k in range(1, planes - 1)
    ]
    for copy in copies:
        copy.start()
    even_plane = lax.axis_index("ax") % 2 == 0
    nu_dt = viscosity * time_step
    half = 0.5 * time_step
    sent_a = own_a[2]
    sent_b = own_b[2, : plan.theta]
    factor_low = nu_dt + half * jnp.where(even_plane, sent_b, sent_a)
    factor_high = nu_dt - half * jnp.where(even_plane, sent_a, sent_b)
    for f in range(plan.fields):
        below, above = slabs_beside(ax_a[f], ax_b[f, : plan.theta])
        ends[0, f] = near_ref[0, f] + factor_low * below
        ends[1, f] = near_ref[planes - 1, f] + factor_high * above
    for end, k in ((0, 0), (1, planes - 1)):
        copies.append(pltpu.make_async_copy(ends.at[end], out_ref.at[:, k, :, first], sems.at[k]))
        copies[-1].start()
    for copy in copies:
        copy.wait()


def finish(plan, near, sent, messages, partial):
    anywhere = pl.BlockSpec(memory_space=pl.ANY)
    inside = pl.BlockSpec(memory_space=pltpu.VMEM)
    return pl.pallas_call(
        functools.partial(finish_kernel, plan),
        in_specs=[inside] * 5 + [anywhere],
        out_specs=anywhere,
        out_shape=jax.ShapeDtypeStruct(partial.shape, jnp.float32),
        input_output_aliases={5: 0},
        scratch_shapes=[
            pltpu.VMEM((2, plan.fields, plan.theta, LANES), jnp.float32),
            pltpu.SemaphoreType.DMA((plan.planes,)),
        ],
        compiler_params=pltpu.CompilerParams(vmem_limit_bytes=VMEM_LIMIT),
        name="finish",
        cost_estimate=pl.CostEstimate(flops=100000, bytes_accessed=1500000, transcendentals=0),
    )(near, *sent, *messages, partial)


def pairs(count, start):
    route = []
    for low in range(start, count, 2):
        high = (low + 1) % count
        route += [(low, high), (high, low)]
    return route


def fast_on_device(fields):
    sectors = lax.axis_size("az")
    slabs = lax.axis_size("ax")
    plan = Plan(fields.shape, sectors)
    coef = jnp.asarray(plan.coefficients())

    def send(x, distance):
        return lax.ppermute(x, "az", [(i, i ^ distance) for i in range(sectors)])

    packed, wide, rest_b = pack(plan, fields)
    rest_b = lax.ppermute(rest_b, "ax", pairs(slabs, 1))
    half = sectors // 2
    pieces = [None] * sectors
    pieces[0] = packed
    far = send(packed, half)
    pieces[half] = far
    for p in range(half - 1, 0, -1):
        pieces[p] = send(wide if p == 1 else packed, p)
    part, token = outer(plan, coef, fields)
    onward = gate(far, token)
    for p in range(half - 1, 0, -1):
        pieces[half + p] = send(onward, p)
    pieces[half] = onward
    early = early_spectra(plan, pieces[: half + 1], rest_b)
    column, rest_a = edges(plan, fields, early[1])
    rests = (lax.ppermute(rest_a, "ax", pairs(slabs, 0)), rest_b)
    sides = (pieces[1], lax.ppermute(column, "az", pairs(sectors, 1)))
    *parts, message_a, message_b = filtered(plan, fields, pieces[half + 1 :], early)
    messages = (
        lax.ppermute(message_a, "ax", pairs(slabs, 0)),
        lax.ppermute(message_b, "ax", pairs(slabs, 1)),
    )
    own = (wide, column)
    near, far, swirl = inner(plan, coef, parts, fields, own, sides[0], rests, part)
    partial, near = last_column(plan, coef, column, sides[1], near, far, swirl, fields)
    return finish(plan, near, (message_a, message_b), messages, partial)


def on_device(fields):
    total_theta = fields.shape[2] * lax.axis_size("az")
    if Plan.fits(fields.shape, lax.axis_size("az"), lax.axis_size("ax"), total_theta):
        return fast_on_device(fields)
    return general_on_device(fields)


def solution(mesh):
    placed = (P(None, "ax", "az", None),)
    return jax.shard_map(
        on_device, mesh=mesh, in_specs=placed, out_specs=P(None, "ax", "az", None), check_vma=False
    )
```

```python
import functools

import jax
import jax.numpy as jnp
import numpy as np
from jax import lax
from jax.experimental import pallas as pl
from jax.experimental.pallas import tpu as pltpu
from jax.sharding import PartitionSpec as P

NEAR = 40


viscosity = 0.2
time_step = 0.1
buoyancy = 1.0

LANES = 128
VMEM_LIMIT = 16 * 1024 * 1024


def swapped(block, axis, distance):
    count = lax.axis_size(axis)
    route = []
    for low in range(count):
        high = low | 1 << distance
        if high != low and high < count:
            route += [(low, high), (high, low)]
    return lax.ppermute(block, axis, route)


def with_halo(block, sides, width, periodic):
    for axis, dim in sides:
        count = lax.axis_size(axis)
        forward = [(i, i + 1) for i in range(count - 1)]
        if periodic:
            forward.append((count - 1, 0))
        backward = [(target, source) for source, target in forward]
        low = lax.ppermute(
            lax.slice_in_dim(block, block.shape[dim] - width, None, axis=dim), axis, forward
        )
        high = lax.ppermute(lax.slice_in_dim(block, 0, width, axis=dim), axis, backward)
        block = jnp.concatenate([low, block, high], axis=dim)
    return block


def mode_tables(theta_index, total_theta, modes):
    column = jnp.arange(modes, dtype=jnp.int32)
    product = theta_index[:, None] * column[None, :] % total_theta
    angle = product.astype(jnp.float32) * (2.0 * jnp.pi / total_theta)
    cosine = jnp.cos(angle)
    sine = jnp.sin(angle)
    weight = jnp.where(column == 0, 1.0, 2.0).astype(jnp.float32) / total_theta
    forward = jnp.concatenate([cosine * weight[None, :], sine * (2.0 / total_theta)], axis=1)
    inverse = jnp.concatenate([cosine, sine], axis=1)
    return (forward, inverse)


def cycle_mask(cycles, modes):
    cycle_index = jnp.arange(cycles, dtype=jnp.int32)
    cutoff = jnp.minimum(355 * (2 * cycle_index + 1) // 226, modes - 1)
    column = jnp.arange(modes, dtype=jnp.int32)
    keep = (column[None, :] <= cutoff[:, None]).astype(jnp.float32)
    return jnp.concatenate([keep, keep], axis=1)


def operators(
    center, radial_plus, radial_minus, theta_plus, theta_minus, axial_plus, axial_minus, total_theta
):
    radius = jnp.arange(center.shape[-1], dtype=jnp.float32) + 0.5
    step_angle = 2.0 * jnp.pi / total_theta
    d_radial = (radial_plus - radial_minus) * 0.5
    d_theta = (theta_plus - theta_minus) / (2.0 * step_angle)
    d_axial = (axial_plus - axial_minus) * 0.5
    laplace = (
        radial_plus - 2.0 * center + radial_minus + (radial_plus - radial_minus) / (2.0 * radius)
    )
    laplace = laplace + (theta_plus - 2.0 * center + theta_minus) / (
        radius * radius * step_angle * step_angle
    )
    laplace = laplace + axial_plus - 2.0 * center + axial_minus
    return (d_radial, d_theta, d_axial, laplace)


def general_on_device(fields):
    count_fields, planes, theta_dev, radial = fields.shape
    sectors = lax.axis_size("az")
    total_theta = theta_dev * sectors
    modes = min(128, total_theta // 2)
    sector = lax.axis_index("az")
    own_index = sector * theta_dev + jnp.arange(theta_dev, dtype=jnp.int32)
    own_forward, own_inverse = mode_tables(own_index, total_theta, modes)
    inner_cycles = fields[:, :, :, :NEAR]
    kept = None
    piece = lax.all_gather(inner_cycles, "az", axis=2, tiled=True)
    piece_index = jnp.arange(piece.shape[2], dtype=jnp.int32)
    piece_forward, unused_inverse = mode_tables(piece_index, total_theta, modes)
    spectra = jnp.einsum("fztj,tc->fzjc", piece, piece_forward, precision=lax.Precision.HIGHEST)
    kept = spectra * cycle_mask(NEAR, modes)[None, None]
    smoothed = jnp.einsum("fzjc,tc->fztj", kept, own_inverse, precision=lax.Precision.HIGHEST)
    state = jnp.concatenate([smoothed, fields[:, :, :, NEAR:]], axis=3)
    flip = jnp.array([-1.0, -1.0, 1.0, 1.0, 1.0], dtype=jnp.float32)[:, None, None]
    top_bit = sectors.bit_length() - 1
    opposite = swapped(state[:, :, :, 0], "az", top_bit - 1)
    opposite = opposite * flip
    theta_padded = with_halo(state, (("az", 2),), 1, True)
    axial_padded = with_halo(state, (("ax", 1),), 1, False)
    radial_plus = jnp.concatenate([state[:, :, :, 1:], jnp.zeros_like(state[:, :, :, :1])], axis=3)
    radial_minus = jnp.concatenate([opposite[:, :, :, None], state[:, :, :, :-1]], axis=3)
    d_radial, d_theta, d_axial, laplace = operators(
        state,
        radial_plus,
        radial_minus,
        theta_padded[:, :, 2:, :],
        theta_padded[:, :, :-2, :],
        axial_padded[:, 2:, :, :],
        axial_padded[:, :-2, :, :],
        total_theta,
    )
    radius = jnp.arange(radial, dtype=jnp.float32) + 0.5
    radial_u = state[0]
    theta_u = state[1]
    axial_u = state[2]
    change = (
        -(radial_u[None] * d_radial + (theta_u / radius)[None] * d_theta + axial_u[None] * d_axial)
        + viscosity * laplace
    )
    inverse_square = 1.0 / (radius * radius)
    first = (
        change[0]
        + theta_u * theta_u / radius
        - viscosity * (radial_u * inverse_square + 2.0 * inverse_square * d_theta[1])
    )
    second = (
        change[1]
        - radial_u * theta_u / radius
        - viscosity * (theta_u * inverse_square - 2.0 * inverse_square * d_theta[0])
    )
    third = change[2] + buoyancy * state[3]
    change = jnp.concatenate([first[None], second[None], third[None], change[3:]], axis=0)
    return state + time_step * change


class Plan:
    def __init__(self, shape, sectors):
        self.fields, self.planes, self.theta, self.radial = shape
        self.sectors = sectors
        self.total = self.theta * sectors
        self.modes = min(128, self.total // 2)
        cycle = np.arange(NEAR)
        self.cut = np.minimum(355 * (2 * cycle + 1) // 226, self.modes - 1)
        self.full = int(np.sum(self.cut < self.modes - 1))
        self.rest = NEAR - self.full
        self.beside = LANES // max(self.full, 1)
        self.groups = -(-self.fields * self.planes // self.beside)
        self.spare = LANES - self.beside * self.full
        self.chunks = -(-self.fields * self.rest // max(self.spare, 1))
        self.early = tuple(range(sectors // 2 + 1))
        self.late = tuple(range(sectors // 2 + 1, sectors))
        self.depth = 256

    def place(self, f, k):
        index = k * self.fields + f
        return index // self.beside, index % self.beside * self.full

    @staticmethod
    def fits(shape, sectors, slabs, total):
        if sectors & (sectors - 1) or total // 2 > 128 or total != LANES or shape[2] != 16:
            return False
        plan = Plan(shape, sectors)
        return (
            plan.full > 0
            and plan.fields == 5
            and plan.planes == plan.theta
            and plan.rest * plan.fields <= LANES
            and plan.groups % 2 == 0
            and plan.spare > 0
            and plan.chunks <= plan.groups
            and slabs % 2 == 0
            and 3 * len(plan.early) * plan.theta <= plan.depth
            and plan.radial % LANES == 0
            and plan.radial > 2 * LANES
        )

    def split(self, table):
        high = table.astype(jnp.bfloat16)
        low = (table - high.astype(np.float32)).astype(jnp.bfloat16)
        return np.concatenate([high, high, low], axis=-1)

    def forward(self, pieces):
        theta = np.arange(self.total)
        mode = np.arange(self.modes)
        angle = (np.outer(mode, theta) % self.total) * (2.0 * np.pi / self.total)
        weight = np.where(mode == 0, 1.0, 2.0)[:, None] / self.total
        table = np.concatenate([np.cos(angle) * weight, np.sin(angle) * 2.0 / self.total], axis=0)
        table = table.astype(np.float32).reshape(2 * self.modes, self.sectors, self.theta)
        blocks = []
        for sector in range(self.sectors):
            chosen = np.concatenate([table[:, sector ^ p] for p in pieces], axis=1)
            chosen = self.split(chosen)
            pad = np.zeros((chosen.shape[0], self.depth - chosen.shape[1]), chosen.dtype)
            blocks.append(np.concatenate([chosen, pad], axis=1))
        return np.stack(blocks)

    def inverse(self):
        mode = np.arange(self.modes)
        blocks = []
        for sector in range(self.sectors):
            own = sector * self.theta + np.arange(self.theta)
            index = np.concatenate([own, own + self.total // 2, own[:1] - 1, own[-1:] + 1])
            angle = (np.outer(index, mode) % self.total) * (2.0 * np.pi / self.total)
            table = np.concatenate([np.cos(angle), np.sin(angle)], axis=1)
            pad = np.zeros((16 - 2, table.shape[1]))
            blocks.append(np.concatenate([table, pad], axis=0))
        return self.split(np.stack(blocks).astype(np.float32))

    def mask(self):
        mode = np.arange(self.modes)
        keep = np.zeros((self.modes, LANES), np.float32)
        for i in range(self.beside):
            keep[:, i * self.full : (i + 1) * self.full] = (
                mode[:, None] <= self.cut[None, : self.full]
            )
        return np.concatenate([keep, keep], axis=0)

    def coefficients(self):
        radius = np.arange(self.radial) + 0.5
        step = 2.0 * np.pi / self.total
        nu_dt = viscosity * time_step
        square = 1.0 / (radius * radius * step * step)
        rows = [
            1.0 - nu_dt * (4.0 + 2.0 * square),
            nu_dt * square,
            nu_dt / (2.0 * radius),
            time_step / (2.0 * step * radius),
            time_step / radius,
            nu_dt / (radius * radius),
            nu_dt / (step * radius * radius),
        ]
        rows.append(np.zeros(self.radial))
        return np.stack(rows).astype(np.float32)


def moved(x, lanes):
    return x if lanes % LANES == 0 else pltpu.roll(x, lanes % LANES, 1)


def pick_columns(plan, x_ref, keep_high, ref, base):
    last = plan.theta - 1
    tiles = plan.radial // LANES
    for f in range(plan.fields):
        for k in range(plan.planes):
            for tile in range(tiles):
                here = slice(tile * LANES, (tile + 1) * LANES)
                low = x_ref[f, k, 0:1, here]
                high = x_ref[f, k, last : last + 1, here]
                ref[base + f * tiles + tile, k : k + 1, :] = jnp.where(keep_high, high, low)


def pack_kernel(plan, x_ref, out_ref, wide_ref, rest_b):
    odd_plane = lax.axis_index("ax") % 2
    rest_b[...] = x_ref[:, odd_plane * (plan.planes - 1), :, LANES:]
    shape = (plan.theta, LANES)
    lane = lax.broadcasted_iota(jnp.int32, shape, 1)
    row = lax.broadcasted_iota(jnp.int32, shape, 0)
    sign = (1 - 2 * (row & 1)).astype(jnp.float32)
    group = jnp.zeros(shape, jnp.float32)
    sums = [jnp.zeros(shape, jnp.float32) for _ in range(plan.fields)]
    for k in range(plan.planes):
        for f in range(plan.fields):
            x = x_ref[f, k, :, :LANES]
            number, first = plan.place(f, k)
            part = moved(x, first)
            if first:
                part = jnp.where((lane >= first) & (lane < first + plan.full), part, group)
            group = part
            if first // plan.full == plan.beside - 1 or (f, k) == (plan.fields - 1, plan.planes - 1):
                out_ref[number] = group
                if number >= plan.chunks:
                    wide_ref[number] = group
            alternating = jnp.sum(x * sign, axis=0, keepdims=True)
            sums[f] = jnp.where(row == k, alternating, sums[f])
    last = sums[0]
    for f in range(plan.fields):
        start = f * plan.rest
        last = jnp.where(lane >= start, moved(sums[f], start - plan.full), last)
    for c in range(plan.chunks):
        start = LANES - plan.spare
        group = jnp.where(lane >= start, moved(last, start - plan.spare * c), out_ref[c])
        out_ref[c] = group
        wide_ref[c] = group
    even_theta = lax.axis_index("az") % 2 == 0
    pick_columns(plan, x_ref, even_theta, wide_ref, plan.groups)


def pack(plan, fields):
    f32 = jnp.float32
    columns = plan.fields * plan.radial // LANES
    plane = jax.ShapeDtypeStruct((plan.fields, plan.theta, plan.radial - LANES), f32)
    inside = pl.BlockSpec(memory_space=pltpu.VMEM)
    return pl.pallas_call(
        functools.partial(pack_kernel, plan),
        in_specs=[inside],
        out_specs=[inside] * 3,
        out_shape=[
            jax.ShapeDtypeStruct((plan.groups, plan.theta, LANES), f32),
            jax.ShapeDtypeStruct((plan.groups + columns, plan.theta, LANES), f32),
            plane,
        ],
        compiler_params=pltpu.CompilerParams(vmem_limit_bytes=VMEM_LIMIT),
        name="pack",
        cost_estimate=pl.CostEstimate(flops=1000000, bytes_accessed=800000, transcendentals=0),
    )(fields)


def advance(coef, q, jp, jm, tp, tm, kp, km):
    c0, c2, half, angular, over, square, cross = coef
    ur, ut, uz, temp = q[:4]
    radial = half - (0.5 * time_step) * ur
    azimuthal = angular * ut
    axial = (0.5 * time_step) * uz
    nu_dt = viscosity * time_step
    out = []
    d_theta = []
    for f in range(5):
        dt = tp[f] - tm[f]
        if f < 2:
            d_theta.append(dt)
        value = c0 * q[f] + nu_dt * ((jp[f] + jm[f]) + (kp[f] + km[f]))
        value = value + c2 * (tp[f] + tm[f])
        value = value + (jp[f] - jm[f]) * radial
        value = value - dt * azimuthal
        value = value - (kp[f] - km[f]) * axial
        out.append(value)
    swirl = over * ut
    out[0] = out[0] + swirl * ut - square * ur - cross * d_theta[1]
    out[1] = out[1] - swirl * ur - square * ut + cross * d_theta[0]
    out[2] = out[2] + (time_step * buoyancy) * temp
    return out


def turned(x, row, before, after):
    last = x.shape[0] - 1
    up = jnp.where(row == last, after, pltpu.roll(x, last, 0))
    down = jnp.where(row == 0, before, pltpu.roll(x, 1, 0))
    return up, down


def outer_kernel(plan, coef_ref, x_ref, done, token):
    planes = plan.planes
    tiles = plan.radial // LANES
    token[...] = jnp.zeros_like(token)
    shape = (plan.theta, LANES)
    lane = lax.broadcasted_iota(jnp.int32, shape, 1)
    row = lax.broadcasted_iota(jnp.int32, shape, 0)

    def step(group, carry):
        start = pl.multiple_of(group * 4, 4)
        for i in range(4):
            k = start + i
            for tile in range(1, tiles):
                here = pl.ds(tile * LANES, LANES)
                coef = [coef_ref[j : j + 1, here] for j in range(7)]
                q, jp, jm, tp, tm, kp, km = ([] for _ in range(7))
                for f in range(plan.fields):
                    x = x_ref[f, k, :, here]
                    low = x_ref[f, k, :, pl.ds((tile - 1) * LANES, LANES)]
                    q.append(x)
                    high = 0.0
                    if tile + 1 < tiles:
                        high = x_ref[f, k, :, pl.ds((tile + 1) * LANES, LANES)]
                        high = pltpu.roll(high, LANES - 1, 1)
                    jp.append(jnp.where(lane == LANES - 1, high, pltpu.roll(x, LANES - 1, 1)))
                    jm.append(jnp.where(lane == 0, pltpu.roll(low, 1, 1), pltpu.roll(x, 1, 1)))
                    up, down = turned(x, row, 0.0, 0.0)
                    tp.append(up)
                    tm.append(down)
                    if i < 3:
                        above = x_ref[f, k + 1, :, here]
                    else:
                        above = x_ref[f, jnp.minimum(k + 1, planes - 1), :, here]
                        above = jnp.where(k == planes - 1, 0.0, above)
                    if i > 0:
                        below = x_ref[f, k - 1, :, here]
                    else:
                        below = x_ref[f, jnp.maximum(k - 1, 0), :, here]
                        below = jnp.where(k == 0, 0.0, below)
                    kp.append(above)
                    km.append(below)
                result = advance(coef, q, jp, jm, tp, tm, kp, km)
                for f in range(plan.fields):
                    done[k, f, :, pl.ds((tile - 1) * LANES, LANES)] = result[f]
        return carry

    lax.fori_loop(0, planes // 4, step, 0)


def outer(plan, coef, fields):
    inside = pl.BlockSpec(memory_space=pltpu.VMEM)
    f32 = jnp.float32
    return pl.pallas_call(
        functools.partial(outer_kernel, plan),
        in_specs=[inside] * 2,
        out_specs=[inside] * 2,
        out_shape=[
            jax.ShapeDtypeStruct((plan.planes, plan.fields, plan.theta, plan.radial - LANES), f32),
            jax.ShapeDtypeStruct((8, LANES), f32),
        ],
        compiler_params=pltpu.CompilerParams(vmem_limit_bytes=VMEM_LIMIT),
        name="outer",
        cost_estimate=pl.CostEstimate(flops=16000000, bytes_accessed=5000000, transcendentals=0),
    )(coef, fields)


def slabs_beside(a, b):
    slab = lax.axis_index("ax")
    even_plane = slab % 2 == 0
    b = jnp.where((slab > 0) & (slab < lax.axis_size("ax") - 1), b, 0.0)
    return jnp.where(even_plane, b, a), jnp.where(even_plane, a, b)


def seams(plan, coef_ref, x_ref, own_a, own_b, az_a, ax_a, ax_b, part_ref, done, terms):
    nu_dt = viscosity * time_step
    half = 0.5 * time_step
    planes = plan.planes
    tiles = plan.radial // LANES
    base = plan.groups
    even_theta = lax.axis_index("az") % 2 == 0
    last = plan.theta - 1
    row = lax.broadcasted_iota(jnp.int32, (plan.theta, LANES), 0)
    for tile in range(1, tiles):
        here = slice(tile * LANES, (tile + 1) * LANES)
        c2 = coef_ref[1:2, here]
        angular = coef_ref[3:4, here]
        cross = coef_ref[6:7, here]
        number = tiles + tile
        mine_a = own_a[base + number]
        mine_b = own_b[number]
        turn_low = angular * jnp.where(even_theta, mine_b, mine_a)
        turn_high = angular * jnp.where(even_theta, mine_a, mine_b)
        before = []
        after = []
        for f in range(plan.fields):
            a = az_a[base + f * tiles + tile]
            before.append(jnp.where(even_theta, 0.0, a))
            after.append(jnp.where(even_theta, a, 0.0))
        for f in range(plan.fields):
            low = (c2 + turn_low) * before[f]
            high = (c2 - turn_high) * after[f]
            if f == 0:
                low = low + cross * before[1]
                high = high - cross * after[1]
            if f == 1:
                low = low - cross * before[0]
                high = high + cross * after[0]
            terms[0, f * tiles + tile] = low
            terms[1, f * tiles + tile] = high
    for k in range(planes):
        for f in range(plan.fields):
            for tile in range(1, tiles):
                here = slice(tile * LANES, (tile + 1) * LANES)
                there = slice((tile - 1) * LANES, tile * LANES)
                value = part_ref[k, f, :, there]
                value = value + jnp.where(row == 0, terms[0, f * tiles + tile, k : k + 1], 0.0)
                value = value + jnp.where(row == last, terms[1, f * tiles + tile, k : k + 1], 0.0)
                if k in (0, planes - 1):
                    below, above = slabs_beside(ax_a[f, :, there], ax_b[f, :, there])
                    if k == 0:
                        value = value + (nu_dt + half * x_ref[2, k, :, here]) * below
                    else:
                        value = value + (nu_dt - half * x_ref[2, k, :, here]) * above
                done[k, f, :, there] = value


def gate_kernel(x_ref, token_ref, out_ref):
    del token_ref
    out_ref[...] = x_ref[...]


def gate(x, token):
    inside = pl.BlockSpec(memory_space=pltpu.VMEM)
    return pl.pallas_call(
        gate_kernel,
        in_specs=[inside] * 2,
        out_specs=inside,
        out_shape=jax.ShapeDtypeStruct(x.shape, x.dtype),
        compiler_params=pltpu.CompilerParams(vmem_limit_bytes=VMEM_LIMIT),
        name="gate",
    )(x, token)


def halves(x, depth=None):
    high = x.astype(jnp.bfloat16)
    low = (x - high.astype(jnp.float32)).astype(jnp.bfloat16)
    parts = [high, low, high]
    if depth is not None:
        parts.append(jnp.zeros((depth - 3 * x.shape[0], x.shape[1]), jnp.bfloat16))
    return jnp.concatenate(parts, axis=0)


def two_groups(pieces, g):
    return jnp.concatenate(
        [jnp.concatenate([piece[g + i] for piece in pieces], axis=0) for i in range(2)], axis=1
    )


def alternating_sums(plan, pieces):
    lane = lax.broadcasted_iota(jnp.int32, (plan.theta, LANES), 1)
    total = jnp.zeros((plan.theta, LANES), jnp.float32)
    for c in range(plan.chunks):
        value = pieces[0][c]
        for piece in pieces[1:]:
            value = value + piece[c]
        start = plan.spare * c
        here = (lane >= start) & (lane < start + plan.spare)
        total = jnp.where(here, moved(value, start + plan.spare - LANES), total)
    return total


def early_kernel(plan, x_ref, forward_ref, after_ref, *refs):
    del after_ref
    pieces = refs[: len(plan.early)]
    spectra_ref, total_ref, az_b, rest_a = refs[len(plan.early) :]
    odd_theta = lax.axis_index("az") % 2 == 1
    pick_columns(plan, x_ref, odd_theta, az_b, 0)
    even_plane = 1 - lax.axis_index("ax") % 2
    rest_a[...] = x_ref[:, even_plane * (plan.planes - 1), :, LANES:]
    table = forward_ref[lax.axis_index("az")]
    for g in range(0, plan.groups, 2):
        both = halves(two_groups(pieces, g), plan.depth)
        spectra_ref[g // 2] = jnp.dot(table, both, preferred_element_type=jnp.float32)
    total_ref[...] = alternating_sums(plan, pieces)


def early_spectra(plan, fields, pieces, after):
    columns = plan.fields * plan.radial // LANES
    inside = pl.BlockSpec(memory_space=pltpu.VMEM)
    f32 = jnp.float32
    return pl.pallas_call(
        functools.partial(early_kernel, plan),
        in_specs=[inside] * (3 + len(pieces)),
        out_specs=[inside] * 4,
        out_shape=[
            jax.ShapeDtypeStruct((plan.groups // 2, 2 * plan.modes, 2 * LANES), f32),
            jax.ShapeDtypeStruct((plan.theta, LANES), f32),
            jax.ShapeDtypeStruct((columns, plan.theta, LANES), f32),
            jax.ShapeDtypeStruct((plan.fields, plan.theta, plan.radial - LANES), f32),
        ],
        compiler_params=pltpu.CompilerParams(vmem_limit_bytes=VMEM_LIMIT),
        name="early",
        cost_estimate=pl.CostEstimate(flops=200000000, bytes_accessed=1500000, transcendentals=0),
    )(fields, jnp.asarray(plan.forward(plan.early)), after, *pieces)


def filter_kernel(plan, x_ref, forward_ref, inverse_ref, mask_ref, early_ref, early_total, *refs):
    count = len(plan.late)
    pieces = refs[:count]
    own_ref, across_ref, edge_ref, sums_ref, message_a, message_b = refs[count:]
    odd_plane = lax.axis_index("ax") % 2
    theta = plan.theta
    sector = lax.axis_index("az")
    forward = forward_ref[sector]
    table = inverse_ref[sector]
    mask = mask_ref[...]
    mask = jnp.concatenate([mask, mask], axis=1)

    for g in range(0, plan.groups, 2):
        both = halves(two_groups(pieces, g), plan.depth)
        spectra = early_ref[g // 2] + jnp.dot(forward, both, preferred_element_type=jnp.float32)
        kept = halves(spectra * mask)
        state = jnp.dot(table, kept, preferred_element_type=jnp.float32)
        for i in range(2):
            lanes = slice(i * LANES, (i + 1) * LANES)
            own_ref[g + i] = state[:theta, lanes]
            across_ref[g + i] = state[theta : 2 * theta, lanes]
            edge_ref[g + i] = state[2 * theta : 2 * theta + 8, lanes]

    total = early_total[...] + alternating_sums(plan, pieces)
    total = total * (1.0 / plan.total)
    lane = lax.broadcasted_iota(jnp.int32, (plan.planes, LANES), 1)
    for f in range(plan.fields):
        value = moved(total, plan.full - f * plan.rest)
        sums_ref[f] = jnp.where((lane >= plan.full) & (lane < NEAR), value, 0.0)

    row = lax.broadcasted_iota(jnp.int32, (theta, LANES), 0)
    sign = (1 - 2 * (row & 1)).astype(jnp.float32)

    def message(ref, k):
        for f in range(plan.fields):
            number, first = plan.place(f, k)
            raw = x_ref[f, k, :, :LANES] - sign * sums_ref[f, k : k + 1]
            ref[f, :theta] = jnp.where(lane < plan.full, moved(own_ref[number], -first), raw)

    def both_messages(a, b):
        message(message_a, a)
        message(message_b, b)
        message_b[:, theta:] = jnp.zeros((plan.fields, 8, LANES), jnp.float32)

    pl.when(odd_plane == 1)(lambda: both_messages(0, plan.planes - 1))
    pl.when(odd_plane == 0)(lambda: both_messages(plan.planes - 1, 0))


def filtered(plan, fields, pieces, early):
    inside = pl.BlockSpec(memory_space=pltpu.VMEM)
    f32 = jnp.float32
    cube = jax.ShapeDtypeStruct((plan.groups, plan.theta, LANES), f32)
    plane = jax.ShapeDtypeStruct((plan.fields, plan.theta, LANES), f32)
    return pl.pallas_call(
        functools.partial(filter_kernel, plan),
        in_specs=[inside] * (6 + len(pieces)),
        out_specs=[inside] * 6,
        out_shape=[
            cube,
            cube,
            jax.ShapeDtypeStruct((plan.groups, 8, LANES), f32),
            jax.ShapeDtypeStruct((plan.fields, plan.planes, LANES), f32),
            plane,
            jax.ShapeDtypeStruct((plan.fields, plan.theta + 8, LANES), f32),
        ],
        compiler_params=pltpu.CompilerParams(vmem_limit_bytes=VMEM_LIMIT),
        name="filter",
        cost_estimate=pl.CostEstimate(flops=200000000, bytes_accessed=1500000, transcendentals=0),
    )(
        fields,
        jnp.asarray(plan.forward(plan.late)),
        jnp.asarray(plan.inverse()),
        jnp.asarray(plan.mask()),
        *early,
        *pieces,
    )


def inner_kernel(
    plan, coef_ref, own_ref, across_ref, edge_ref, sums_ref, x_ref, own_a, own_b, az_a,
    ax_a, ax_b, part_ref, done, far_done, swirl_ref, terms, state
):
    planes = plan.planes
    seams(plan, coef_ref, x_ref, own_a, own_b, az_a, ax_a, ax_b, part_ref, far_done, terms)
    theta = plan.theta
    tiles = plan.radial // LANES
    shape = (theta, LANES)
    lane = lax.broadcasted_iota(jnp.int32, shape, 1)
    row = lax.broadcasted_iota(jnp.int32, shape, 0)
    sign = (1 - 2 * (row & 1)).astype(jnp.float32)
    lane1 = lax.broadcasted_iota(jnp.int32, (1, LANES), 1)
    first = slice(0, LANES)
    coef = [coef_ref[i : i + 1, first] for i in range(7)]
    flips = (-1.0, -1.0, 1.0, 1.0, 1.0)
    even_theta = lax.axis_index("az") % 2 == 0

    for k in range(planes):
        for f in range(plan.fields):
            number, start = plan.place(f, k)
            state[k, f] = jnp.where(
                lane < plan.full,
                moved(own_ref[number], -start),
                x_ref[f, k, :, first] - sign * sums_ref[f, k : k + 1],
            )

    befores = []
    afters = []
    for f in range(plan.fields):
        a = az_a[plan.groups + f * tiles]
        befores.append(jnp.where(even_theta, 0.0, a) + sums_ref[f])
        afters.append(jnp.where(even_theta, a, 0.0) - sums_ref[f])

    zero = jnp.zeros(shape, jnp.float32)
    for k in range(planes):
        q, jp, jm, tp, tm, kp, km = ([] for _ in range(7))
        for f in range(plan.fields):
            number, start = plan.place(f, k)
            x = state[k, f]
            q.append(x)
            high_part = pltpu.roll(x_ref[f, k, :, LANES : 2 * LANES], LANES - 1, 1)
            jp.append(jnp.where(lane == LANES - 1, high_part, pltpu.roll(x, LANES - 1, 1)))
            opposite = flips[f] * moved(across_ref[number], -start)
            jm.append(jnp.where(lane == 0, opposite, pltpu.roll(x, 1, 1)))
            sides = moved(edge_ref[number], -start)
            before = jnp.where(lane1 < plan.full, sides[0:1], befores[f][k : k + 1])
            after = jnp.where(lane1 < plan.full, sides[1:2], afters[f][k : k + 1])
            up, down = turned(x, row, before, after)
            tp.append(up)
            tm.append(down)
            kp.append(state[k + 1, f] if k + 1 < planes else zero)
            km.append(state[k - 1, f] if k > 0 else zero)
        result = advance(coef, q, jp, jm, tp, tm, kp, km)
        for f in range(plan.fields):
            done[k, f] = result[f]
    for k in range(planes):
        x = state[k, 1]
        swirl_ref[k : k + 1] = jnp.where(even_theta, x[:1], x[theta - 1 :])


def inner(plan, coef, parts, fields, own, side, rests, part):
    inside = pl.BlockSpec(memory_space=pltpu.VMEM)
    f32 = jnp.float32
    return pl.pallas_call(
        functools.partial(inner_kernel, plan),
        in_specs=[inside] * 12,
        out_specs=[inside, inside, inside],
        out_shape=[
            jax.ShapeDtypeStruct((plan.planes, plan.fields, plan.theta, LANES), f32),
            jax.ShapeDtypeStruct(part.shape, f32),
            jax.ShapeDtypeStruct((plan.planes, LANES), f32),
        ],
        scratch_shapes=[
            pltpu.VMEM((2, plan.fields * plan.radial // LANES, plan.planes, LANES), f32),
            pltpu.VMEM((plan.planes, plan.fields, plan.theta, LANES), f32),
        ],
        compiler_params=pltpu.CompilerParams(vmem_limit_bytes=VMEM_LIMIT),
        name="inner",
        cost_estimate=pl.CostEstimate(flops=6000000, bytes_accessed=2500000, transcendentals=0),
    )(coef, *parts, fields, *own, side, *rests, part)


def column_kernel(
    plan, coef_ref, own_b, az_b, near_ref, far_ref, swirl_ref, out_ref, near, far, terms, outs
):
    planes = plan.planes
    tiles = plan.radial // LANES
    even_theta = lax.axis_index("az") % 2 == 0
    sign = jnp.where(even_theta, 1.0, -1.0)
    beyond = pl.ds(LANES, plan.radial - LANES)
    lane = lax.broadcasted_iota(jnp.int32, (planes, LANES), 1)
    for tile in range(tiles):
        here = slice(tile * LANES, (tile + 1) * LANES)
        c2 = coef_ref[1:2, here]
        cross = sign * coef_ref[6:7, here]
        swirl = swirl_ref[...] if tile == 0 else own_b[tiles + tile]
        turn = c2 + sign * coef_ref[3:4, here] * swirl
        column = [az_b[f * tiles + tile] for f in range(plan.fields)]
        if tile == 0:
            column = [jnp.where(lane < plan.full, 0.0, x) for x in column]
        for f in range(plan.fields):
            value = turn * column[f]
            if f == 0:
                value = value + cross * column[1]
            if f == 1:
                value = value - cross * column[0]
            terms[f * tiles + tile] = value
    row = lax.broadcasted_iota(jnp.int32, (plan.theta, LANES), 0)
    edge = jnp.where(even_theta, 0, plan.theta - 1)
    copies = []
    for k in range(planes):
        for f in range(plan.fields):
            for tile in range(1, tiles):
                there = slice((tile - 1) * LANES, tile * LANES)
                term = terms[f * tiles + tile, k : k + 1]
                far[k, f, :, there] = far_ref[k, f, :, there] + jnp.where(row == edge, term, 0.0)
        copies.append(pltpu.make_async_copy(far.at[k], out_ref.at[:, k, :, beyond], outs.at[k]))
        copies[-1].start()
    for k in range(planes):
        for f in range(plan.fields):
            near[k, f] = near_ref[k, f] + jnp.where(
                row == edge, terms[f * tiles, k : k + 1], 0.0
            )
    for copy in copies:
        copy.wait()


def last_column(plan, coef, own, side, near, far, swirl, fields):
    anywhere = pl.BlockSpec(memory_space=pl.ANY)
    inside = pl.BlockSpec(memory_space=pltpu.VMEM)
    f32 = jnp.float32
    return pl.pallas_call(
        functools.partial(column_kernel, plan),
        in_specs=[inside] * 6,
        out_specs=[anywhere, inside],
        out_shape=[
            jax.ShapeDtypeStruct(fields.shape, f32),
            jax.ShapeDtypeStruct(near.shape, f32),
        ],
        scratch_shapes=[
            pltpu.VMEM((plan.planes, plan.fields, plan.theta, plan.radial - LANES), f32),
            pltpu.VMEM((plan.fields * plan.radial // LANES, plan.planes, LANES), f32),
            pltpu.SemaphoreType.DMA((plan.planes,)),
        ],
        compiler_params=pltpu.CompilerParams(vmem_limit_bytes=VMEM_LIMIT),
        name="last_column",
        cost_estimate=pl.CostEstimate(flops=1000000, bytes_accessed=2500000, transcendentals=0),
    )(coef, own, side, near, far, swirl)


def finish_kernel(plan, near_ref, own_a, own_b, ax_a, ax_b, other_ref, out_ref, ends, sems):
    del other_ref
    planes = plan.planes
    first = pl.ds(0, LANES)
    copies = [
        pltpu.make_async_copy(near_ref.at[k], out_ref.at[:, k, :, first], sems.at[k])
        for k in range(1, planes - 1)
    ]
    for copy in copies:
        copy.start()
    even_plane = lax.axis_index("ax") % 2 == 0
    nu_dt = viscosity * time_step
    half = 0.5 * time_step
    sent_a = own_a[2]
    sent_b = own_b[2, : plan.theta]
    factor_low = nu_dt + half * jnp.where(even_plane, sent_b, sent_a)
    factor_high = nu_dt - half * jnp.where(even_plane, sent_a, sent_b)
    for f in range(plan.fields):
        below, above = slabs_beside(ax_a[f], ax_b[f, : plan.theta])
        ends[0, f] = near_ref[0, f] + factor_low * below
        ends[1, f] = near_ref[planes - 1, f] + factor_high * above
    for end, k in ((0, 0), (1, planes - 1)):
        copies.append(pltpu.make_async_copy(ends.at[end], out_ref.at[:, k, :, first], sems.at[k]))
        copies[-1].start()
    for copy in copies:
        copy.wait()


def finish(plan, near, sent, messages, partial):
    anywhere = pl.BlockSpec(memory_space=pl.ANY)
    inside = pl.BlockSpec(memory_space=pltpu.VMEM)
    return pl.pallas_call(
        functools.partial(finish_kernel, plan),
        in_specs=[inside] * 5 + [anywhere],
        out_specs=anywhere,
        out_shape=jax.ShapeDtypeStruct(partial.shape, jnp.float32),
        input_output_aliases={5: 0},
        scratch_shapes=[
            pltpu.VMEM((2, plan.fields, plan.theta, LANES), jnp.float32),
            pltpu.SemaphoreType.DMA((plan.planes,)),
        ],
        compiler_params=pltpu.CompilerParams(vmem_limit_bytes=VMEM_LIMIT),
        name="finish",
        cost_estimate=pl.CostEstimate(flops=100000, bytes_accessed=1500000, transcendentals=0),
    )(near, *sent, *messages, partial)


def pairs(count, start):
    route = []
    for low in range(start, count, 2):
        high = (low + 1) % count
        route += [(low, high), (high, low)]
    return route


def fast_on_device(fields):
    sectors = lax.axis_size("az")
    slabs = lax.axis_size("ax")
    plan = Plan(fields.shape, sectors)
    coef = jnp.asarray(plan.coefficients())

    def send(x, distance):
        return lax.ppermute(x, "az", [(i, i ^ distance) for i in range(sectors)])

    packed, wide, rest_b = pack(plan, fields)
    rest_b = lax.ppermute(rest_b, "ax", pairs(slabs, 1))
    half = sectors // 2
    pieces = [None] * sectors
    pieces[0] = packed
    far = send(packed, half)
    pieces[half] = far
    for p in range(half - 1, 0, -1):
        pieces[p] = send(wide if p == 1 else packed, p)
    part, token = outer(plan, coef, fields)
    onward = gate(far, token)
    for p in range(half - 1, 0, -1):
        pieces[half + p] = send(onward, p)
    pieces[half] = onward
    *early, column, rest_a = early_spectra(plan, fields, pieces[: half + 1], rest_b)
    rests = (lax.ppermute(rest_a, "ax", pairs(slabs, 0)), rest_b)
    sides = (pieces[1], lax.ppermute(column, "az", pairs(sectors, 1)))
    *parts, message_a, message_b = filtered(plan, fields, pieces[half + 1 :], early)
    messages = (
        lax.ppermute(message_a, "ax", pairs(slabs, 0)),
        lax.ppermute(message_b, "ax", pairs(slabs, 1)),
    )
    own = (wide, column)
    near, far, swirl = inner(plan, coef, parts, fields, own, sides[0], rests, part)
    partial, near = last_column(plan, coef, column, sides[1], near, far, swirl, fields)
    return finish(plan, near, (message_a, message_b), messages, partial)


def on_device(fields):
    total_theta = fields.shape[2] * lax.axis_size("az")
    if Plan.fits(fields.shape, lax.axis_size("az"), lax.axis_size("ax"), total_theta):
        return fast_on_device(fields)
    return general_on_device(fields)


def solution(mesh):
    placed = (P(None, "ax", "az", None),)
    return jax.shard_map(
        on_device, mesh=mesh, in_specs=placed, out_specs=P(None, "ax", "az", None), check_vma=False
    )
```
